512 devices in a mesh: gx: 32 (over x, y), gy: 16 (over z, core).
Axes of the slice: x: 4, y: 8, z: 8, core: 2. Of those that a mesh axis runs over, the one named last changes fastest.
Arguments:
- latent: bfloat16 [32, 16, 16, 64, 128], P('gx', 'gy'), may hold values from -6 to 6
- occupancy: int32 [32, 16, 16], P('gx', 'gy'), may hold values from 0 to 1, as said below
- carry_x: float32 [32, 16, 16], P('gx', 'gy'), may hold values from 0.003 to 1
- carry_y: float32 [32, 16, 16], P('gx', 'gy'), may hold values from 0.003 to 1
- w_in: bfloat16 [16, 64], replicated, may hold values from -1.5 to 1.5
- w_down: bfloat16 [512, 128], replicated, may hold values from -0.25 to 0.25
- w_mid: bfloat16 [7, 128, 128], replicated, may hold values from -0.1875 to 0.1875
- w_up: bfloat16 [128, 512], replicated, may hold values from -0.5 to 0.5
- w_out: bfloat16 [64, 16], replicated, may hold values from -0.75 to 0.75
Outputs:
- denoised: bfloat16 [32, 16, 16, 64, 128], P('gx', 'gy')
The draws below stay inside these ranges and needn't reach their ends.
Inputs may be any that keep to these rules, and one draw needn't show every extreme that they name: `occupancy`: every tile has at least one and at most 12 occupied blocks; some tile has exactly 12.
All inputs are finite; a program needn't handle non-finite values.
Results may differ from the reference program's by a relative error of at most 0.015.
Values sent between devices are 32-bit elements; how exact they have to be, the bound alone decides.
No kernel may reach another device: no remote copies, remote signals or barrier semaphores. Data moves between devices by JAX's collectives and lax.ppermute only.
A program may use at most 64 MiB of HBM per device.

```python
import jax
import jax.numpy as jnp
from jax import lax

C = 16
FA = 64
FB = 128
STEPS = 2
OCC_MAX = 12
BLOCKS = 16
SUBC = 128
TILE_COLUMNS = 32
TILE_ROWS = 16


def seam_rates(key, sequence_length, share):
    random_key_list = jax.random.split(key, 5)
    drawn_decay_group = jax.random.uniform(random_key_list[0], (C,)) < share
    drawn_decay = jax.random.uniform(random_key_list[1], (TILE_COLUMNS, TILE_ROWS, C), minval=0.3, maxval=1.2) / sequence_length
    sudden_jumps = jax.random.uniform(random_key_list[2], (TILE_COLUMNS, TILE_ROWS, 1)) < 2.0 / sequence_length
    decay_falls = jax.random.uniform(random_key_list[3], (TILE_COLUMNS, TILE_ROWS, C), minval=0.22, maxval=0.69)
    sharp_decay = jax.random.uniform(random_key_list[4], (TILE_COLUMNS, TILE_ROWS, C), minval=2.0, maxval=5.0)
    decay_rates = jnp.where(drawn_decay_group, drawn_decay + jnp.where(sudden_jumps, decay_falls, 0.0), sharp_decay)
    return jnp.exp(-decay_rates).astype(jnp.float32)


def draw_occupancy(key, part):
    key = jax.random.fold_in(key, 11)
    key_count, key_pick, key_perm = jax.random.split(key, 3)
    ntiles = TILE_COLUMNS * TILE_ROWS
    raw = jax.random.randint(key_count, (ntiles,), 0, OCC_MAX)
    counts = 1 + raw * raw // OCC_MAX
    chosen = jax.random.randint(key_pick, (), 0, ntiles)
    counts = jnp.where(jnp.arange(ntiles) == chosen, OCC_MAX, counts)
    ranks = jax.vmap(lambda subkey: jax.random.permutation(subkey, BLOCKS))(jax.random.split(key_perm, ntiles))
    occupied = (ranks < counts[:, None]).astype(jnp.int32)
    return occupied.reshape(TILE_COLUMNS, TILE_ROWS, BLOCKS)


def draw_carry_x(key, part):
    key = jax.random.fold_in(key, 12)
    share = 0.5
    return seam_rates(key, TILE_COLUMNS, share)


def draw_carry_y(key, part):
    key = jax.random.fold_in(key, 13)
    share = 0.5
    return seam_rates(key, TILE_ROWS, share)


def block_scale(stream_key, dims, cuts, smallest, top_value):
    gain, own = 1.0, jax.random.fold_in(stream_key, 6)
    for position, blocks in cuts:
        draws = jnp.exp(jax.random.uniform(jax.random.fold_in(own, position), (blocks,), jnp.float32, smallest / len(cuts), top_value / len(cuts)))
        gain = gain * jnp.repeat(draws, dims[position] // blocks).reshape([-1 if axis == position else 1 for axis in range(len(dims))])
    return gain


def normal_values(rng, shape, scale, most, pieces=(), dtype=jnp.bfloat16):
    values = scale * jax.random.normal(rng, shape, jnp.float32)
    if pieces:
        values = values * block_scale(rng, shape, pieces, -0.22, 0.18)
    return jnp.clip(values, -most, most).astype(dtype)


def setup_inputs(seed: int = 0) -> dict:
    keys = jax.random.split(jax.random.key(seed), 10)
    latent = normal_values(keys[0], (TILE_COLUMNS, TILE_ROWS, BLOCKS, 64, SUBC), 1.0, 6.0, ((0, 32), (1, 16)))
    occupancy = draw_occupancy(jax.random.fold_in(keys[9], 71), 0)
    carry_x = draw_carry_x(jax.random.fold_in(keys[9], 71), 0)
    carry_y = draw_carry_y(jax.random.fold_in(keys[9], 71), 0)
    w_in = normal_values(keys[4], (C, FA), C ** -0.5, 1.5)
    w_down = normal_values(keys[5], (8 * FA, FB), (8 * FA) ** -0.5, 0.25)
    w_mid = normal_values(keys[6], (7, FB, FB), (7 * FB) ** -0.5, 0.1875)
    w_up = normal_values(keys[7], (FB, 8 * FA), FB ** -0.5, 0.5)
    w_out = normal_values(keys[8], (FA, C), FA ** -0.5, 0.75)
    return dict(latent=latent, occupancy=occupancy, carry_x=carry_x, carry_y=carry_y, w_in=w_in, w_down=w_down, w_mid=w_mid, w_up=w_up, w_out=w_out)


def block_net(blocks, w_in, w_down, w_mid, w_up, w_out):
    count = blocks.shape[0]
    chan = w_in.shape[0]
    fa_width = w_in.shape[1]
    fb_width = w_down.shape[1]
    voxels = blocks.reshape(count, 64, 8, chan)
    first = jax.nn.silu(jnp.einsum('nqsc,cf->nqsf', voxels.astype(jnp.float32), w_in.astype(jnp.float32))).astype(jnp.bfloat16)
    first_rows = first.reshape(count * 64, 8 * fa_width)
    pre = jnp.dot(first_rows, w_down, preferred_element_type=jnp.float32)
    pre = pre * lax.rsqrt(lax.optimization_barrier(jnp.mean(pre * pre, axis=-1, keepdims=True)) + 1e-06)
    second = jax.nn.silu(pre).astype(jnp.bfloat16)
    coarse = second.reshape(count, 4, 4, 4, fb_width)
    stencil = [coarse]
    for axis_num in (1, 2, 3):
        widths = [(0, 0)] * 5
        widths[axis_num] = (1, 1)
        padded = jnp.pad(coarse, widths)
        for offset in (-1, 1):
            stencil.append(lax.slice_in_dim(padded, 1 + offset, 5 + offset, axis=axis_num))
    stacked = jnp.concatenate(stencil, axis=-1).reshape(count * 64, 7 * fb_width)
    mixed = jnp.dot(stacked, w_mid.reshape(7 * fb_width, fb_width), preferred_element_type=jnp.float32)
    middle = (second.astype(jnp.float32) + jax.nn.silu(mixed)).astype(jnp.bfloat16)
    upper = jax.nn.silu(jnp.dot(middle, w_up, preferred_element_type=jnp.float32) + first_rows.astype(jnp.float32)).astype(jnp.bfloat16)
    upper = upper.reshape(count, 64, 8, fa_width)
    update = jnp.einsum('nqsf,fc->nqsc', upper.astype(jnp.float32), w_out.astype(jnp.float32))
    return update.reshape(count, 64, 8 * chan)

def strip_x(field, which):
    picked = jnp.take(field, which, axis=-7)
    reduced = lax.optimization_barrier(jnp.mean(picked, axis=-4))
    shape = reduced.shape
    reduced = reduced.reshape(shape[:-1] + (2, shape[-1] // 2))
    return lax.optimization_barrier(jnp.mean(reduced, axis=-2))

def strip_y(field, which):
    picked = jnp.take(field, which, axis=-6)
    reduced = lax.optimization_barrier(jnp.mean(picked, axis=-3))
    shape = reduced.shape
    reduced = reduced.reshape(shape[:-1] + (2, 2, shape[-1] // 4))
    reduced = lax.optimization_barrier(jnp.mean(reduced, axis=-2))
    return reduced.reshape(shape[:-1] + (shape[-1] // 2,))

def spread_x(plane):
    whole = jnp.concatenate([plane, plane], axis=-1)
    return jnp.expand_dims(jnp.expand_dims(whole, -6), -4)

def spread_y(plane):
    shape = plane.shape
    split = plane.reshape(shape[:-1] + (2, 1, shape[-1] // 2))
    split = jnp.broadcast_to(split, shape[:-1] + (2, 2, shape[-1] // 2))
    whole = split.reshape(shape[:-1] + (2 * shape[-1],))
    return jnp.expand_dims(jnp.expand_dims(whole, -5), -3)

def gain_x(decay_rates):
    chan = decay_rates.shape[-1]
    width = 8 * chan
    lanes = jnp.arange(width)
    sub_x = lanes // (4 * chan)
    corner = jnp.arange(4)
    place = (8 * corner[:, None, None] + 2 * corner[None, :, None] + sub_x[None, None, :]).astype(jnp.float32) + 0.5
    logs = jnp.concatenate([jnp.log(decay_rates)] * 8, axis=-1)
    field = jnp.exp(place / 32.0 * logs[..., None, None, :])
    return field.reshape(decay_rates.shape[:-1] + (4, 1, 1, 4, 1, 1, width))

def gain_y(decay_rates):
    chan = decay_rates.shape[-1]
    width = 8 * chan
    lanes = jnp.arange(width)
    sub_y = lanes // (2 * chan) % 2
    corner = jnp.arange(4)
    place = (8 * corner[:, None, None] + 2 * corner[None, :, None] + sub_y[None, None, :]).astype(jnp.float32) + 0.5
    logs = jnp.concatenate([jnp.log(decay_rates)] * 8, axis=-1)
    field = jnp.exp(place / 32.0 * logs[..., None, None, :])
    return field.reshape(decay_rates.shape[:-1] + (1, 4, 1, 1, 4, 1, width))

def reference(latent, occupancy, carry_x, carry_y, w_in, w_down, w_mid, w_up, w_out):
    ncols, nrows, nblocks, cells, width = latent.shape
    depth = nblocks // 16
    chan = width // 8
    shaped = (ncols, nrows, 4, 4, depth, 4, 4, 4, width)
    field_x = gain_x(carry_x)
    field_y = jnp.moveaxis(gain_y(carry_y), 1, 0)
    weights = occupancy.astype(jnp.float32).reshape(ncols * nrows, nblocks)
    current = latent
    for step in range(STEPS):
        tiles = current.reshape(ncols * nrows, nblocks, cells, width)

        def one_tile(item):
            blocks, occupied = item
            update = block_net(blocks, w_in, w_down, w_mid, w_up, w_out)
            return (blocks.astype(jnp.float32) + occupied[:, None, None] * update).astype(jnp.bfloat16)
        pred = lax.map(one_tile, (tiles, weights)).reshape(shaped)

        def column(before, item):
            pred_col, gain_col, column_num = item
            values = pred_col.astype(jnp.float32)
            west = strip_x(values, 0)
            drift = jnp.where(column_num == 0, 0.0, before - west)
            matched = values + gain_col * spread_x(drift)
            return (strip_x(matched, 3), matched)
        start_x = jnp.zeros((nrows, 4, depth, 4, 4, 4 * chan), jnp.float32)
        _, matched = lax.scan(column, start_x, (pred, field_x, jnp.arange(ncols)))
        matched = jnp.moveaxis(matched, 1, 0)

        def rowwise(before, item):
            matched_row, gain_row, row_num = item
            south = strip_y(matched_row, 0)
            drift = jnp.where(row_num == 0, 0.0, before - south)
            result = matched_row + gain_row * spread_y(drift)
            return (strip_y(result, 3), result.astype(jnp.bfloat16))
        start_y = jnp.zeros((ncols, 4, depth, 4, 4, 4 * chan), jnp.float32)
        _, results = lax.scan(rowwise, start_y, (matched, field_y, jnp.arange(nrows)))
        current = jnp.moveaxis(results, 0, 1).reshape(ncols, nrows, nblocks, cells, width)
    return current
```

```python
import functools

import jax
import jax.numpy as jnp
from jax import lax
from jax.experimental import pallas as pl
from jax.experimental.pallas import tpu as pltpu
from jax.sharding import PartitionSpec as P

STEPS = 2
F32 = jnp.float32
BF16 = jnp.bfloat16


def silu(v):
    half = 0.5 * v
    return half + half * jnp.tanh(half)


def iotas(rows):
    sub = lax.broadcasted_iota(jnp.int32, (rows, 128), 0)
    lane = lax.broadcasted_iota(jnp.int32, (rows, 128), 1)
    return sub, lane


def turn_lanes(x, by):
    return pltpu.roll(x, by % 128, x.ndim - 1)


def turn_rows(x, by):
    by = by % x.shape[0]
    return x if by == 0 else pltpu.roll(x, by, 0)


def swap_sy(x, lane):
    return jnp.where((lane // 32) % 2 == 0, turn_lanes(x, -32), turn_lanes(x, 32))


def edge_gain(logs):
    return sum(jnp.exp((p + 0.5) / 32.0 * logs) for p in range(24, 32)) * 0.125


def gain_at(place, logs):
    return jnp.exp(place.astype(F32) / 32.0 * logs + (0.5 / 32.0) * logs)


def widen(narrow, rows, cols):
    r = lax.broadcasted_iota(jnp.int32, (8 * rows, rows), 0) % rows
    k = lax.broadcasted_iota(jnp.int32, (8 * rows, rows), 1)
    tall = jnp.dot((r == k).astype(BF16), narrow, preferred_element_type=F32).astype(BF16)
    k = lax.broadcasted_iota(jnp.int32, (cols, 8 * cols), 0)
    c = lax.broadcasted_iota(jnp.int32, (cols, 8 * cols), 1) % cols
    both = jnp.dot(tall, (k == c).astype(BF16), preferred_element_type=F32)
    r = lax.broadcasted_iota(jnp.int32, (8 * rows, 8 * cols), 0) // rows
    c = lax.broadcasted_iota(jnp.int32, (8 * rows, 8 * cols), 1) // cols
    return jnp.where(r == c, both, 0.0).astype(BF16)


def net(state, aux, weights, scratch, pred_ref, outs):
    w_in, w_down, w_mid, w_up, w_out = weights
    first_ref, second_ref, wide_in_ref, wide_out_ref, line_ref = scratch
    msg_line, msg_x, msg_y, west_ref, south_ref, west_line_ref = outs
    log_x, log_y, col, row, occupied = aux
    wide_in_ref[...] = widen(w_in[...], 16, 64)
    wide_out_ref[...] = widen(w_out[...], 64, 16)
    for qx in range(4):
        rows = pl.ds(256 * qx, 256)
        first = silu(jnp.dot(state[rows, :], wide_in_ref[...], preferred_element_type=F32)).astype(BF16)
        first_ref[rows, :] = first
        pre = jnp.dot(first, w_down[...], preferred_element_type=F32)
        pre = pre * lax.rsqrt(jnp.mean(pre * pre, axis=-1, keepdims=True) + 1e-06)
        second_ref[rows, :] = silu(pre).astype(BF16)

    sub, lane = iotas(16)
    by, bx = sub % 4, sub // 4
    total_x = [[None] * 4 for _ in range(4)]
    south, north = [0.0] * 4, [0.0] * 4
    for qx in range(4):
        base = 256 * qx
        rows = pl.ds(base, 256)
        second = second_ref[rows, :]
        parts = [(0, second)]
        if qx > 0:
            parts.append((1, second_ref[pl.ds(base - 256, 256), :]))
        if qx < 3:
            parts.append((2, second_ref[pl.ds(base + 256, 256), :]))
        gap = jnp.zeros((64, 128), BF16)
        parts.append((3, jnp.concatenate([gap, second[:192]], axis=0)))
        parts.append((4, jnp.concatenate([second[64:], gap], axis=0)))
        gap = jnp.zeros((16, 128), BF16)
        below, above = [], []
        for qy in range(4):
            own = second[64 * qy : 64 * qy + 64]
            below += [gap, own[:48]]
            above += [own[16:], gap]
        parts.append((5, jnp.concatenate(below, axis=0)))
        parts.append((6, jnp.concatenate(above, axis=0)))
        stacked = jnp.concatenate([p for _, p in parts], axis=1)
        mids = jnp.concatenate([w_mid[k] for k, _ in parts], axis=0)
        mixed = jnp.dot(stacked, mids, preferred_element_type=F32)
        middle = (second.astype(F32) + silu(mixed)).astype(BF16)
        upper = jnp.dot(middle, w_up[...], preferred_element_type=F32) + first_ref[rows, :].astype(F32)
        upper = silu(upper).astype(BF16)
        update = jnp.dot(upper, wide_out_ref[...], preferred_element_type=F32)
        update = update.reshape(16, 16, 128) * occupied[None]
        pred = (state[rows, :].astype(F32).reshape(16, 16, 128) + update).astype(BF16)
        pred_ref[rows, :] = pred.reshape(256, 128)
        pred = pred.astype(F32)
        for qy in range(4):
            for qz in range(4):
                value = pred[4 * qy + qz]
                total_x[qy][qz] = value if qx == 0 else total_x[qy][qz] + value
        for qz in range(4):
            s = pred[qz] + pred[4 + qz] + pred[8 + qz] + pred[12 + qz]
            s = (s + swap_sy(s, lane)) * 0.125
            south[qx] = south[qx] + jnp.where(by == qz, turn_rows(s, qz), 0.0)
            north[qx] = north[qx] + jnp.where(by == qz, turn_rows(s, qz - 3), 0.0)

    west, east = [0.0] * 4, [0.0] * 4
    for qy in range(4):
        for qz in range(4):
            s = total_x[qy][qz]
            s = (s + turn_lanes(s, 64)) * 0.125
            west[qy] = west[qy] + jnp.where(bx == qz, turn_rows(s, 4 * qz), 0.0)
            east[qy] = east[qy] + jnp.where(bx == qz, turn_rows(s, 4 * qz + 4), 0.0)
    low_sx, low_sy = lane < 64, (lane // 32) % 2 == 0
    factor_x = jnp.where(col == 0.0, 0.0, edge_gain(log_x))
    factor_y = jnp.where(row == 0.0, 0.0, edge_gain(log_y))
    line_x, line_w = 0.0, 0.0
    for k in range(2):
        w = jnp.where(low_sx, west[k], west[2 + k])
        t = jnp.where(low_sx, east[k], east[2 + k]) - factor_x * w
        west_ref[k] = w
        line_x, line_w = line_x + t, line_w + w
        msg_x[:, pl.ds(16 * k, 16), :] = jnp.broadcast_to(t[None], (msg_x.shape[0], 16, 128))
        s = jnp.where(low_sy, south[k], south[2 + k])
        a = jnp.where(low_sy, north[k], north[2 + k]) - factor_y * s
        south_ref[k] = s
        msg_y[:, pl.ds(16 * k, 16), :] = jnp.broadcast_to(a[None], (msg_y.shape[0], 16, 128))
    part = lane // 32
    lines = []
    for slot, value in enumerate((line_x, line_w)):
        value = value + turn_lanes(value, 64)
        value = (value + turn_lanes(value, 32)) * 0.125
        value = jnp.where(((part == 0) & (by == 0)) | ((part == 3) & (by == 3)), value, 0.0)
        line_ref[slot] = value + turn_rows(value, -3)
        lines.append(line_ref[slot, pl.ds(0, 4, stride=4), :])
    part = iotas(4)[1] // 32
    line = jnp.where(part == 1, factor_x, lines[0])
    msg_line[...] = jnp.broadcast_to(line[None], msg_line.shape)
    west_line_ref[...] = lines[1]


def read_aux(aux_ref):
    logs = jnp.log(aux_ref[0:2, :])
    return logs[0:1], logs[1:2], aux_ref[2:3, :], aux_ref[3:4, :], aux_ref[8:24, :]


def everywhere(x, which):
    part = lax.broadcasted_iota(jnp.int32, x.shape, x.ndim - 1) // 32
    x = jnp.where(part == which, x, 0.0)
    x = x + turn_lanes(x, 32)
    return x + turn_lanes(x, 64)


def middle_kernel(aux_ref, got_line, west_line_ref, msg_v, south_line_ref):
    log_x, log_y, col, row, _ = read_aux(aux_ref)
    factor_y = jnp.where(row == 0.0, 0.0, edge_gain(log_y))
    before = jnp.zeros((4, 128), F32)
    for k in range(got_line.shape[0]):
        value = got_line[k]
        before = jnp.where(col > k, everywhere(value, 1) * before + value, before)
    drift = jnp.where(col == 0.0, 0.0, before - west_line_ref[...])
    south = everywhere(drift, 0)
    line = everywhere(drift, 3) - factor_y * south
    part = iotas(4)[1] // 32
    line = jnp.where(part == 1, factor_y, jnp.where(part == 2, log_x, line))
    msg_v[...] = jnp.broadcast_to(line[None], msg_v.shape)
    south_line_ref[...] = south


def four(line):
    return jnp.concatenate([line] * 4, axis=0)


def seams(aux, pred_ref, got_line, got_x, got_v, got_y, west_ref, south_ref, south_line_ref, put):
    log_x, log_y, col, row, _ = aux
    sub, lane = iotas(16)
    by, bx = sub % 4, sub // 4
    sx, sy = lane // 64, (lane // 32) % 2
    before = [jnp.zeros((16, 128), F32)] * 2
    for k in range(got_x.shape[0]):
        factor = everywhere(got_line[k, 0:1, :], 1)
        go = col > k
        before = [jnp.where(go, factor * before[h] + got_x[k, pl.ds(16 * h, 16), :], before[h]) for h in range(2)]
    drift_x = [jnp.where(col == 0.0, 0.0, before[h] - west_ref[h]) for h in range(2)]
    place = [8 * bx + 2 * (2 * sy + h) + sx for h in range(2)]
    before = [jnp.zeros((16, 128), F32)] * 2
    for k in range(got_y.shape[0]):
        line = got_v[k]
        factor = everywhere(line[0:1], 1)
        logs = everywhere(line[0:1], 2)
        line = four(everywhere(line, 0))
        go = row > k
        before = [
            jnp.where(
                go,
                factor * before[h] + got_y[k, pl.ds(16 * h, 16), :] + gain_at(place[h], logs) * line,
                before[h],
            )
            for h in range(2)
        ]
    south_line = four(south_line_ref[...])
    drift_y = [
        jnp.where(row == 0.0, 0.0, before[h] - south_ref[h] - gain_at(place[h], log_x) * south_line)
        for h in range(2)
    ]
    gain_x = [gain_at(8 * bx + 2 * q + sx, log_x) for q in range(4)]
    gain_y = [gain_at(8 * by + 2 * q + sy, log_y) for q in range(4)]
    spread_x = [[None] * 4 for _ in range(4)]
    spread_y = [[None] * 4 for _ in range(4)]
    for q in range(4):
        d = drift_x[q % 2]
        d = jnp.where(sx == q // 2, d, turn_lanes(d, 64))
        e = drift_y[q % 2]
        e = jnp.where(sy == q // 2, e, swap_sy(e, lane))
        for qz in range(4):
            m = jnp.where(bx == qz, d, 0.0)
            m = m + turn_rows(m, 8)
            spread_x[q][qz] = m + turn_rows(m, 4)
            m = turn_rows(jnp.where(by == qz, e, 0.0), -qz)
            m = m + turn_rows(m, 1)
            spread_y[q][qz] = m + turn_rows(m, 2)
    for qx in range(4):
        for qy in range(4):
            for qz in range(4):
                q = 16 * qx + 4 * qy + qz
                value = pred_ref[pl.ds(16 * q, 16), :].astype(F32)
                value = value + gain_x[qx] * spread_x[qy][qz] + gain_y[qy] * spread_y[qx][qz]
                put(q, value)


def first_kernel(aux_ref, latent, w_in, w_down, w_mid, w_up, w_out, *rest):
    pred_ref, *outs = rest[:7]
    state, *scratch = rest[7:]
    turned = jnp.swapaxes(latent[...].astype(F32), 0, 1)
    state[...] = turned.reshape(1024, 128).astype(BF16)
    net(state, read_aux(aux_ref), (w_in, w_down, w_mid, w_up, w_out), scratch, pred_ref, outs)


def next_kernel(aux_ref, *rest):
    seam_ins, weights, outs, (state, *scratch) = rest[:8], rest[8:13], rest[13:20], rest[20:]
    aux = read_aux(aux_ref)

    def put(q, value):
        state[pl.ds(16 * q, 16), :] = value.astype(BF16)

    seams(aux, *seam_ins, put)
    net(state, aux, weights, scratch, outs[0], outs[1:])


def last_kernel(aux_ref, *rest):
    seam_ins, out, state = rest[:8], rest[8], rest[9]

    def put(q, value):
        state[q] = value

    seams(read_aux(aux_ref), *seam_ins, put)
    out[...] = jnp.swapaxes(state[...], 0, 1).astype(BF16)


def call(kernel, out_shape, scratch, args, name):
    vmem = pl.BlockSpec(memory_space=pltpu.VMEM)
    return pl.pallas_call(
        kernel,
        out_shape=out_shape,
        in_specs=[vmem] * len(args),
        out_specs=jax.tree.map(lambda _: vmem, out_shape),
        scratch_shapes=scratch,
        compiler_params=pltpu.CompilerParams(vmem_limit_bytes=24 * 1024 * 1024),
        name=name,
    )(*args)


def per_device(columns, rows, latent, occupancy, carry_x, carry_y, w_in, w_down, w_mid, w_up, w_out):
    col, row = lax.axis_index("gx"), lax.axis_index("gy")
    aux = jnp.concatenate(
        [
            jnp.tile(carry_x[0, 0], 8)[None],
            jnp.tile(carry_y[0, 0], 8)[None],
            jnp.full((1, 128), col, F32),
            jnp.full((5, 128), row, F32),
            jnp.broadcast_to(occupancy[0, 0].astype(F32)[:, None], (16, 128)),
        ],
        axis=0,
    )
    weights = (w_in, w_down, w_mid, w_up, w_out)
    shape = jax.ShapeDtypeStruct
    net_out = (
        shape((1024, 128), BF16),
        shape((columns, 4, 128), F32),
        shape((columns, 32, 128), F32),
        shape((rows, 32, 128), F32),
        shape((2, 16, 128), F32),
        shape((2, 16, 128), F32),
        shape((4, 128), F32),
    )
    net_scratch = [
        pltpu.VMEM((1024, 128), BF16),
        pltpu.VMEM((1024, 512), BF16),
        pltpu.VMEM((1024, 128), BF16),
        pltpu.VMEM((128, 512), BF16),
        pltpu.VMEM((512, 128), BF16),
        pltpu.VMEM((2, 16, 128), F32),
    ]
    for step in range(STEPS):
        if step == 0:
            outs = call(first_kernel, net_out, net_scratch, (aux, latent[0, 0], *weights), "net_first")
        else:
            outs = call(next_kernel, net_out, net_scratch, (aux, *seam_ins, *weights), "seams_net")
        pred, msg_line, msg_x, msg_y, west, south, west_line = outs
        got_line = lax.all_to_all(msg_line, "gx", 0, 0)
        got_x = lax.all_to_all(msg_x, "gx", 0, 0)
        got_y = lax.all_to_all(msg_y, "gy", 0, 0)
        msg_v, south_line = call(
            middle_kernel,
            (shape((rows, 4, 128), F32), shape((4, 128), F32)),
            [],
            (aux, got_line, west_line),
            "lines",
        )
        got_v = lax.all_to_all(msg_v, "gy", 0, 0)
        seam_ins = (pred, got_line, got_x, got_v, got_y, west, south, south_line)
    out = call(
        last_kernel, shape((16, 64, 128), BF16), [pltpu.VMEM((64, 16, 128), F32)], (aux, *seam_ins), "seams_last"
    )
    return out[None, None]


def solution(mesh):
    in_specs = (
        P("gx", "gy", None, None, None),
        P("gx", "gy", None),
        P("gx", "gy", None),
        P("gx", "gy", None),
        P(),
        P(),
        P(),
        P(),
        P(),
    )
    out_specs = P("gx", "gy", None, None, None)
    return jax.shard_map(
        functools.partial(per_device, mesh.shape["gx"], mesh.shape["gy"]),
        mesh=mesh,
        in_specs=in_specs,
        out_specs=out_specs,
        check_vma=False,
    )
```

```python
import functools

import jax
import jax.numpy as jnp
from jax import lax
from jax.experimental import pallas as pl
from jax.experimental.pallas import tpu as pltpu
from jax.sharding import PartitionSpec as P

STEPS = 2
F32 = jnp.float32
BF16 = jnp.bfloat16


def silu(v):
    half = 0.5 * v
    return half + half * jnp.tanh(half)


def iotas(rows):
    sub = lax.broadcasted_iota(jnp.int32, (rows, 128), 0)
    lane = lax.broadcasted_iota(jnp.int32, (rows, 128), 1)
    return sub, lane


def turn_lanes(x, by):
    return pltpu.roll(x, by % 128, x.ndim - 1)


def turn_rows(x, by):
    by = by % x.shape[0]
    return x if by == 0 else pltpu.roll(x, by, 0)


def swap_sy(x, lane):
    return jnp.where((lane // 32) % 2 == 0, turn_lanes(x, -32), turn_lanes(x, 32))


def edge_gain(logs):
    return sum(jnp.exp((p + 0.5) / 32.0 * logs) for p in range(24, 32)) * 0.125


def gain_at(place, logs):
    return jnp.exp(place.astype(F32) / 32.0 * logs + (0.5 / 32.0) * logs)


def widen(narrow, rows, cols):
    r = lax.broadcasted_iota(jnp.int32, (8 * rows, rows), 0) % rows
    k = lax.broadcasted_iota(jnp.int32, (8 * rows, rows), 1)
    tall = jnp.dot((r == k).astype(BF16), narrow, preferred_element_type=F32).astype(BF16)
    k = lax.broadcasted_iota(jnp.int32, (cols, 8 * cols), 0)
    c = lax.broadcasted_iota(jnp.int32, (cols, 8 * cols), 1) % cols
    both = jnp.dot(tall, (k == c).astype(BF16), preferred_element_type=F32)
    r = lax.broadcasted_iota(jnp.int32, (8 * rows, 8 * cols), 0) // rows
    c = lax.broadcasted_iota(jnp.int32, (8 * rows, 8 * cols), 1) // cols
    return jnp.where(r == c, both, 0.0)


def net(state, aux, weights, first_ref, second_ref, pred_ref, outs):
    wide_in, w_down, w_mid, w_up, wide_out = weights
    msg, west_ref, south_ref, north_ref = outs
    log_x, occupied, col = aux.log_x, aux.occupied, aux.col
    for qx in range(4):
        rows = pl.ds(256 * qx, 256)
        first = silu(jnp.dot(state[rows, :], wide_in[...], preferred_element_type=F32)).astype(BF16)
        first_ref[rows, :] = first
        pre = jnp.dot(first, w_down[...], preferred_element_type=F32)
        pre = pre * lax.rsqrt(jnp.mean(pre * pre, axis=-1, keepdims=True) + 1e-06)
        second_ref[rows, :] = silu(pre).astype(BF16)

    sub, lane = iotas(16)
    by, bx = sub % 4, sub // 4
    total_x = [[None] * 4 for _ in range(4)]
    south, north = [0.0] * 4, [0.0] * 4
    for qx in range(4):
        base = 256 * qx
        rows = pl.ds(base, 256)
        second = second_ref[rows, :]
        parts = [(0, second)]
        if qx > 0:
            parts.append((1, second_ref[pl.ds(base - 256, 256), :]))
        if qx < 3:
            parts.append((2, second_ref[pl.ds(base + 256, 256), :]))
        gap = jnp.zeros((64, 128), BF16)
        parts.append((3, jnp.concatenate([gap, second[:192]], axis=0)))
        parts.append((4, jnp.concatenate([second[64:], gap], axis=0)))
        gap = jnp.zeros((16, 128), BF16)
        below, above = [], []
        for qy in range(4):
            own = second[64 * qy : 64 * qy + 64]
            below += [gap, own[:48]]
            above += [own[16:], gap]
        parts.append((5, jnp.concatenate(below, axis=0)))
        parts.append((6, jnp.concatenate(above, axis=0)))
        stacked = jnp.concatenate([p for _, p in parts], axis=1)
        mids = jnp.concatenate([w_mid[k] for k, _ in parts], axis=0)
        mixed = jnp.dot(stacked, mids, preferred_element_type=F32)
        middle = (second.astype(F32) + silu(mixed)).astype(BF16)
        upper = jnp.dot(middle, w_up[...], preferred_element_type=F32) + first_ref[rows, :].astype(F32)
        upper = silu(upper).astype(BF16)
        update = jnp.dot(upper, wide_out[...], preferred_element_type=F32)
        update = update.reshape(16, 16, 128) * occupied[None]
        pred = (state[rows, :].astype(F32).reshape(16, 16, 128) + update).astype(BF16)
        pred_ref[rows, :] = pred.reshape(256, 128)
        pred = pred.astype(F32)
        for qy in range(4):
            for qz in range(4):
                value = pred[4 * qy + qz]
                total_x[qy][qz] = value if qx == 0 else total_x[qy][qz] + value
        for qz in range(4):
            s = pred[qz] + pred[4 + qz] + pred[8 + qz] + pred[12 + qz]
            s = (s + swap_sy(s, lane)) * 0.125
            south[qx] = south[qx] + jnp.where(by == qz, turn_rows(s, qz), 0.0)
            north[qx] = north[qx] + jnp.where(by == qz, turn_rows(s, qz - 3), 0.0)

    west, east = [0.0] * 4, [0.0] * 4
    for qy in range(4):
        for qz in range(4):
            s = total_x[qy][qz]
            s = (s + turn_lanes(s, 64)) * 0.125
            west[qy] = west[qy] + jnp.where(bx == qz, turn_rows(s, 4 * qz), 0.0)
            east[qy] = east[qy] + jnp.where(bx == qz, turn_rows(s, 4 * qz + 4), 0.0)
    low_sx, low_sy = lane < 64, (lane // 32) % 2 == 0
    factor = jnp.where(col == 0.0, 0.0, edge_gain(log_x))
    for h in range(2):
        w = jnp.where(low_sx, west[h], west[2 + h])
        t = jnp.where(low_sx, east[h], east[2 + h]) - factor * w
        west_ref[h] = w
        south_ref[h] = jnp.where(low_sy, south[h], south[2 + h])
        north_ref[h] = jnp.where(low_sy, north[h], north[2 + h])
        msg[:, pl.ds(16 * h, 16), :] = jnp.broadcast_to(t[None], (msg.shape[0], 16, 128))
    msg[:, 32:40, :] = jnp.broadcast_to(factor[None], (msg.shape[0], 8, 128))


class Aux:
    def __init__(self, ref):
        self.log_x, self.log_y = ref[0:1, :], ref[1:2, :]
        self.col, self.outer, self.inner, self.row = (ref[k : k + 1, :] for k in range(2, 6))
        self.occupied = ref[8:24, :]


def scan(got, place, planes, factor_row):
    zero, one = [jnp.zeros((16, 128), F32)] * 2, jnp.ones((1, 128), F32)
    before, before_f, total, total_f = zero, one, zero, one
    for k in range(got.shape[0]):
        f = got[k, factor_row : factor_row + 1, :]
        t = [got[k, pl.ds(16 * h, 16), :] for h in range(2)]
        go = place > k
        before = [jnp.where(go, f * before[h] + t[h], before[h]) for h in range(2)]
        before_f = jnp.where(go, f * before_f, before_f)
        total = [f * total[h] + t[h] for h in range(2)]
        total_f = f * total_f
    return before, before_f, total, total_f


def group_kernel(aux_ref, got, msg, prefix_ref, prefix_f_ref):
    before, before_f, total, total_f = scan(got, Aux(aux_ref).inner, 2, 32)
    for h in range(2):
        prefix_ref[h] = before[h]
        msg[:, pl.ds(16 * h, 16), :] = jnp.broadcast_to(total[h][None], (msg.shape[0], 16, 128))
    msg[:, 32:40, :] = jnp.broadcast_to(total_f[None], (msg.shape[0], 8, 128))
    prefix_f_ref[...] = jnp.broadcast_to(before_f, (8, 128))


def four(line):
    return jnp.concatenate([line] * 4, axis=0)


def place_y(lane, bx):
    return [8 * bx + 2 * (2 * ((lane // 32) % 2) + h) + lane // 64 for h in range(2)]


def turn_kernel(aux_ref, got, prefix_ref, prefix_f_ref, west_ref, south_ref, north_ref, msg, drift_ref, low_ref, line_ref):
    aux = Aux(aux_ref)
    sub, lane = iotas(16)
    start, _, _, _ = scan(got, aux.outer, 2, 32)
    line = 0.0
    for h in range(2):
        drift = prefix_f_ref[0:1, :] * start[h] + prefix_ref[h] - west_ref[h]
        drift = jnp.where(aux.col == 0.0, 0.0, drift)
        drift_ref[h] = drift
        line = line + drift
    line = line + turn_lanes(line, 64)
    line = (line + turn_lanes(line, 32)) * 0.125
    factor = jnp.where(aux.row == 0.0, 0.0, edge_gain(aux.log_y))
    line_ref[0] = line
    line_ref[1] = turn_rows(line, -3) - factor * line
    south_line = four(line_ref[0, pl.ds(0, 4, stride=4), :])
    term_line = four(line_ref[1, pl.ds(0, 4, stride=4), :])
    places = place_y(lane, sub // 4)
    for h in range(2):
        gain = gain_at(places[h], aux.log_x)
        low_ref[h] = south_ref[h] + gain * south_line
        term = north_ref[h] - factor * south_ref[h] + gain * term_line
        msg[:, pl.ds(16 * h, 16), :] = jnp.broadcast_to(term[None], (msg.shape[0], 16, 128))
    if msg.shape[1] > 32:
        msg[:, 32:40, :] = jnp.broadcast_to(factor[None], (msg.shape[0], 8, 128))


def seams(aux, pred_ref, got, factors, drift_ref, low_ref, put):
    sub, lane = iotas(16)
    by, bx = sub % 4, sub // 4
    sx, sy = lane // 64, (lane // 32) % 2
    before = [jnp.zeros((16, 128), F32)] * 2
    for k in range(got.shape[0]):
        f, go = factors(k), aux.row > k
        before = [jnp.where(go, f * before[h] + got[k, pl.ds(16 * h, 16), :], before[h]) for h in range(2)]
    drift_y = [jnp.where(aux.row == 0.0, 0.0, before[h] - low_ref[h]) for h in range(2)]
    drift_x = [drift_ref[h] for h in range(2)]
    gain_x = [gain_at(8 * bx + 2 * q + sx, aux.log_x) for q in range(4)]
    gain_y = [gain_at(8 * by + 2 * q + sy, aux.log_y) for q in range(4)]
    spread_x = [[None] * 4 for _ in range(4)]
    spread_y = [[None] * 4 for _ in range(4)]
    for q in range(4):
        d = drift_x[q % 2]
        d = jnp.where(sx == q // 2, d, turn_lanes(d, 64))
        e = drift_y[q % 2]
        e = jnp.where(sy == q // 2, e, swap_sy(e, lane))
        for qz in range(4):
            m = jnp.where(bx == qz, d, 0.0)
            m = m + turn_rows(m, 8)
            spread_x[q][qz] = m + turn_rows(m, 4)
            m = turn_rows(jnp.where(by == qz, e, 0.0), -qz)
            m = m + turn_rows(m, 1)
            spread_y[q][qz] = m + turn_rows(m, 2)
    for qx in range(4):
        for qy in range(4):
            for qz in range(4):
                q = 16 * qx + 4 * qy + qz
                value = pred_ref[pl.ds(16 * q, 16), :].astype(F32)
                value = value + gain_x[qx] * spread_x[qy][qz] + gain_y[qy] * spread_y[qx][qz]
                put(q, value)


def first_kernel(inner, latent, occupancy, carry_x, carry_y, w_in, w_down, w_mid, w_up, w_out, *rest):
    pred_ref, msg, west, south, north, aux_ref, wide_in, wide_out = rest[:8]
    latent_v, occupancy_v, carry_x_v, carry_y_v, w_in_v, w_down_v, w_mid_v, w_up_v, w_out_v = rest[8:17]
    state, first_ref, second_ref, sems = rest[17:]
    pairs = [
        (w_in, w_in_v),
        (w_out, w_out_v),
        (occupancy, occupancy_v),
        (carry_x, carry_x_v),
        (carry_y, carry_y_v),
        (latent, latent_v),
        (w_down, w_down_v),
        (w_mid, w_mid_v),
        (w_up, w_up_v),
    ]
    copies = [pltpu.make_async_copy(src, dst, sems.at[k]) for k, (src, dst) in enumerate(pairs)]
    for copy in copies:
        copy.start()
    col, row = lax.axis_index("gx"), lax.axis_index("gy")
    for copy in copies[:5]:
        copy.wait()
    wide_in[...] = widen(w_in_v[...], 16, 64).astype(BF16)
    wide_out[...] = widen(w_out_v[...], 16, 64).T.astype(BF16)
    rates = jnp.concatenate([carry_x_v[...], carry_y_v[...]], axis=0)
    rates = jnp.concatenate([rates] * 8, axis=1)
    aux_ref[0:2, :] = jnp.log(rates)
    for k, place in enumerate((col, col // inner, col % inner, row)):
        aux_ref[2 + k : 3 + k, :] = jnp.full((1, 128), place, jnp.int32).astype(F32)
    r, c = (lax.broadcasted_iota(jnp.int32, (16, 16), k) for k in (0, 1))
    occupied = jnp.where(r == c, occupancy_v[...].astype(F32), 0.0)
    aux_ref[8:24, :] = jnp.broadcast_to(jnp.sum(occupied, axis=1, keepdims=True), (16, 128))
    copies[5].wait()
    turned = jnp.swapaxes(latent_v[...].astype(F32), 0, 1)
    state[...] = turned.reshape(1024, 128).astype(BF16)
    for copy in copies[6:]:
        copy.wait()
    weights = (wide_in, w_down_v, w_mid_v, w_up_v, wide_out)
    net(state, Aux(aux_ref), weights, first_ref, second_ref, pred_ref, (msg, west, south, north))


def next_kernel(aux_ref, pred, got, drift, low, wide_in, w_down, w_mid, w_up, wide_out, *rest):
    outs, (factor_ref, state, first_ref, second_ref) = rest[:5], rest[5:]
    aux = Aux(aux_ref)
    for k in range(got.shape[0]):
        factor_ref[k : k + 1, :] = got[k, 32:33, :]

    def put(q, value):
        state[pl.ds(16 * q, 16), :] = value.astype(BF16)

    seams(aux, pred, got, lambda k: got[k, 32:33, :], drift, low, put)
    net(state, aux, (wide_in, w_down, w_mid, w_up, wide_out), first_ref, second_ref, outs[0], outs[1:])


def last_kernel(aux_ref, pred, got, drift, low, factor_ref, out, state):
    def put(q, value):
        state[q] = value

    seams(Aux(aux_ref), pred, got, lambda k: factor_ref[k : k + 1, :], drift, low, put)
    out[...] = jnp.swapaxes(state[...], 0, 1).astype(BF16)


def call(kernel, out_shape, scratch, args, name, space=pltpu.VMEM, limit=24):
    vmem = pl.BlockSpec(memory_space=pltpu.VMEM)
    return pl.pallas_call(
        kernel,
        out_shape=out_shape,
        in_specs=[pl.BlockSpec(memory_space=space)] * len(args),
        out_specs=jax.tree.map(lambda _: vmem, out_shape),
        scratch_shapes=scratch,
        compiler_params=pltpu.CompilerParams(vmem_limit_bytes=limit * 1024 * 1024),
        name=name,
    )(*args)


def per_device(columns, rows, latent, occupancy, carry_x, carry_y, w_in, w_down, w_mid, w_up, w_out):
    inner = 8 if columns % 8 == 0 else 2
    outer = columns // inner
    near = [[inner * a + b for b in range(inner)] for a in range(outer)]
    far = [[inner * a + b for a in range(outer)] for b in range(inner)]
    shape = jax.ShapeDtypeStruct
    plane = shape((2, 16, 128), F32)
    net_out = (shape((1024, 128), BF16), shape((inner, 40, 128), F32), plane, plane, plane)
    net_scratch = [
        pltpu.VMEM((1024, 128), BF16),
        pltpu.VMEM((1024, 512), BF16),
        pltpu.VMEM((1024, 128), BF16),
    ]
    for step in range(STEPS):
        if step == 0:
            args = (latent[0, 0], occupancy[0], carry_x[0], carry_y[0], w_in, w_down, w_mid, w_up, w_out.T)
            held = [pltpu.VMEM(a.shape, a.dtype) for a in args]
            *outs, aux, wide_in, wide_out = call(
                functools.partial(first_kernel, inner),
                (*net_out, shape((24, 128), F32), shape((128, 512), BF16), shape((512, 128), BF16)),
                held + net_scratch + [pltpu.SemaphoreType.DMA((len(args),))],
                args,
                "net_first",
                pl.ANY,
                60,
            )
        else:
            factors, *outs = call(
                next_kernel,
                (*net_out, shape((rows, 128), F32)),
                net_scratch,
                (aux, *seam_ins, wide_in, w_down, w_mid, w_up, wide_out),
                "seams_net",
            )[::-1]
            outs = outs[::-1]
        pred, msg, west, south, north = outs
        got = lax.all_to_all(msg, "gx", 0, 0, axis_index_groups=near)
        msg, prefix, prefix_f = call(
            group_kernel, (shape((outer, 40, 128), F32), plane, shape((8, 128), F32)), [], (aux, got), "group"
        )
        got = lax.all_to_all(msg, "gx", 0, 0, axis_index_groups=far)
        msg, drift, low = call(
            turn_kernel,
            (shape((rows, 40 if step == 0 else 32, 128), F32), plane, plane),
            [pltpu.VMEM((2, 16, 128), F32)],
            (aux, got, prefix, prefix_f, west, south, north),
            "turn",
        )
        got = lax.all_to_all(msg, "gy", 0, 0)
        seam_ins = (pred, got, drift, low)
    out = call(
        last_kernel,
        shape((16, 64, 128), BF16),
        [pltpu.VMEM((64, 16, 128), F32)],
        (aux, *seam_ins, factors),
        "seams_last",
    )
    return out[None, None]


def solution(mesh):
    in_specs = (
        P("gx", "gy", None, None, None),
        P("gx", "gy", None),
        P("gx", "gy", None),
        P("gx", "gy", None),
        P(),
        P(),
        P(),
        P(),
        P(),
    )
    out_specs = P("gx", "gy", None, None, None)
    return jax.shard_map(
        functools.partial(per_device, mesh.shape["gx"], mesh.shape["gy"]),
        mesh=mesh,
        in_specs=in_specs,
        out_specs=out_specs,
        check_vma=False,
    )
```

```python
import functools

import jax
import jax.numpy as jnp
from jax import lax
from jax.experimental import pallas as pl
from jax.experimental.pallas import tpu as pltpu
from jax.sharding import PartitionSpec as P

STEPS = 2
F32 = jnp.float32
BF16 = jnp.bfloat16


def silu(v):
    half = 0.5 * v
    return half + half * jnp.tanh(half)


def iotas(rows):
    sub = lax.broadcasted_iota(jnp.int32, (rows, 128), 0)
    lane = lax.broadcasted_iota(jnp.int32, (rows, 128), 1)
    return sub, lane


def turn_lanes(x, by):
    return pltpu.roll(x, by % 128, x.ndim - 1)


def turn_rows(x, by):
    by = by % x.shape[0]
    return x if by == 0 else pltpu.roll(x, by, 0)


def swap_sy(x, lane):
    return jnp.where((lane // 32) % 2 == 0, turn_lanes(x, -32), turn_lanes(x, 32))


def edge_gain(logs):
    return sum(jnp.exp((p + 0.5) / 32.0 * logs) for p in range(24, 32)) * 0.125


def gain_at(place, logs):
    return jnp.exp(place.astype(F32) / 32.0 * logs + (0.5 / 32.0) * logs)


def widen(narrow, rows, cols):
    r = lax.broadcasted_iota(jnp.int32, (8 * rows, rows), 0) % rows
    k = lax.broadcasted_iota(jnp.int32, (8 * rows, rows), 1)
    tall = jnp.dot((r == k).astype(BF16), narrow, preferred_element_type=F32).astype(BF16)
    k = lax.broadcasted_iota(jnp.int32, (cols, 8 * cols), 0)
    c = lax.broadcasted_iota(jnp.int32, (cols, 8 * cols), 1) % cols
    both = jnp.dot(tall, (k == c).astype(BF16), preferred_element_type=F32)
    r = lax.broadcasted_iota(jnp.int32, (8 * rows, 8 * cols), 0) // rows
    c = lax.broadcasted_iota(jnp.int32, (8 * rows, 8 * cols), 1) // cols
    return jnp.where(r == c, both, 0.0)


def net(state, aux, weights, first_ref, second_ref, pred_ref, outs):
    wide_in, w_down, w_mid, w_up, wide_out = weights
    msg, west_ref, south_ref, north_ref = outs
    log_x, occupied, col = aux.log_x, aux.occupied, aux.col
    for qx in range(4):
        rows = pl.ds(256 * qx, 256)
        first = silu(jnp.dot(state[rows, :], wide_in[...], preferred_element_type=F32)).astype(BF16)
        first_ref[rows, :] = first
        pre = jnp.dot(first, w_down[...], preferred_element_type=F32)
        pre = pre * lax.rsqrt(jnp.mean(pre * pre, axis=-1, keepdims=True) + 1e-06)
        second_ref[rows, :] = silu(pre).astype(BF16)

    sub, lane = iotas(16)
    by, bx = sub % 4, sub // 4
    total_x = [[None] * 4 for _ in range(4)]
    south, north = [0.0] * 4, [0.0] * 4
    for qx in range(4):
        base = 256 * qx
        rows = pl.ds(base, 256)
        second = second_ref[rows, :]
        parts = [(0, second)]
        if qx > 0:
            parts.append((1, second_ref[pl.ds(base - 256, 256), :]))
        if qx < 3:
            parts.append((2, second_ref[pl.ds(base + 256, 256), :]))
        gap = jnp.zeros((64, 128), BF16)
        parts.append((3, jnp.concatenate([gap, second[:192]], axis=0)))
        parts.append((4, jnp.concatenate([second[64:], gap], axis=0)))
        gap = jnp.zeros((16, 128), BF16)
        below, above = [], []
        for qy in range(4):
            own = second[64 * qy : 64 * qy + 64]
            below += [gap, own[:48]]
            above += [own[16:], gap]
        parts.append((5, jnp.concatenate(below, axis=0)))
        parts.append((6, jnp.concatenate(above, axis=0)))
        stacked = jnp.concatenate([p for _, p in parts], axis=1)
        mids = jnp.concatenate([w_mid[k] for k, _ in parts], axis=0)
        mixed = jnp.dot(stacked, mids, preferred_element_type=F32)
        middle = (second.astype(F32) + silu(mixed)).astype(BF16)
        upper = jnp.dot(middle, w_up[...], preferred_element_type=F32) + first_ref[rows, :].astype(F32)
        upper = silu(upper).astype(BF16)
        update = jnp.dot(upper, wide_out[...], preferred_element_type=F32)
        update = update.reshape(16, 16, 128) * occupied[None]
        pred = (state[rows, :].astype(F32).reshape(16, 16, 128) + update).astype(BF16)
        pred_ref[rows, :] = pred.reshape(256, 128)
        pred = pred.astype(F32)
        for qy in range(4):
            for qz in range(4):
                value = pred[4 * qy + qz]
                total_x[qy][qz] = value if qx == 0 else total_x[qy][qz] + value
        for qz in range(4):
            s = pred[qz] + pred[4 + qz] + pred[8 + qz] + pred[12 + qz]
            s = (s + swap_sy(s, lane)) * 0.125
            south[qx] = south[qx] + jnp.where(by == qz, turn_rows(s, qz), 0.0)
            north[qx] = north[qx] + jnp.where(by == qz, turn_rows(s, qz - 3), 0.0)

    west, east = [0.0] * 4, [0.0] * 4
    for qy in range(4):
        for qz in range(4):
            s = total_x[qy][qz]
            s = (s + turn_lanes(s, 64)) * 0.125
            west[qy] = west[qy] + jnp.where(bx == qz, turn_rows(s, 4 * qz), 0.0)
            east[qy] = east[qy] + jnp.where(bx == qz, turn_rows(s, 4 * qz + 4), 0.0)
    low_sx, low_sy = lane < 64, (lane // 32) % 2 == 0
    factor = jnp.where(col == 0.0, 0.0, edge_gain(log_x))
    terms = []
    for h in range(2):
        w = jnp.where(low_sx, west[h], west[2 + h])
        terms.append(jnp.where(low_sx, east[h], east[2 + h]) - factor * w)
        west_ref[h] = w
        south_ref[h] = jnp.where(low_sy, south[h], south[2 + h])
        north_ref[h] = jnp.where(low_sy, north[h], north[2 + h])
    fill(msg, terms, [jnp.broadcast_to(factor, (8, 128))] if msg.shape[1] > 32 else [])


class Aux:
    def __init__(self, ref):
        self.log_x, self.log_y = ref[0:1, :], ref[1:2, :]
        self.col, self.x, self.y, self.row, self.z, self.core = (ref[k : k + 1, :] for k in range(2, 8))
        self.occupied = ref[8:24, :]


def halves(ref, k):
    return [ref[k, pl.ds(16 * h, 16), :] for h in range(2)]


def fill(msg, planes, rows=()):
    for k, value in enumerate([*planes, *rows]):
        size = 16 if k < 2 else 8
        at = 16 * k if k < 2 else 32 + 8 * (k - 2)
        msg[:, pl.ds(at, size), :] = jnp.broadcast_to(value[None], (msg.shape[0], size, 128))


def line_of(planes, ref):
    sub, lane = iotas(16)
    value = planes[0] + planes[1]
    value = value + turn_lanes(value, 64)
    value = (value + turn_lanes(value, 32)) * 0.125
    by, part = sub % 4, lane // 32
    value = jnp.where(((part == 0) & (by == 0)) | ((part == 3) & (by == 3)), value, 0.0)
    ref[...] = value + turn_rows(value, -3)
    return ref[pl.ds(0, 4, stride=4), :]


def everywhere(x, which):
    part = lax.broadcasted_iota(jnp.int32, x.shape, x.ndim - 1) // 32
    x = jnp.where(part == which, x, 0.0)
    x = x + turn_lanes(x, 32)
    return x + turn_lanes(x, 64)


def four(line):
    return jnp.concatenate([line] * 4, axis=0)


def place_y(sub, lane):
    return [8 * (sub // 4) + 2 * (2 * ((lane // 32) % 2) + h) + lane // 64 for h in range(2)]


def edge_y(aux):
    return jnp.where(aux.row == 0.0, 0.0, edge_gain(aux.log_y))


def group_kernel(aux_ref, got, *rest):
    if got.shape[1] > 32:
        west, south, north, msg, start_ref, start_f_ref, factor_ref, line_ref, line2_ref = rest
        for k in range(got.shape[0]):
            factor_ref[k : k + 1, :] = got[k, 32:33, :]
    else:
        factor_ref, west, south, north, msg, start_ref, start_f_ref, line_ref, line2_ref = rest
    aux = Aux(aux_ref)
    zero, one = [jnp.zeros((16, 128), F32)] * 2, jnp.ones((1, 128), F32)
    before, before_f, total, total_f = zero, one, zero, one
    for k in range(got.shape[0]):
        f, t, go = factor_ref[k : k + 1, :], halves(got, k), aux.y > k
        before = [jnp.where(go, f * before[h] + t[h], before[h]) for h in range(2)]
        before_f = jnp.where(go, f * before_f, before_f)
        total = [f * total[h] + t[h] for h in range(2)]
        total_f = f * total_f
    start = [before[h] - west[h] for h in range(2)]
    factor_y = edge_y(aux)
    term_y = [north[h] - factor_y * south[h] for h in range(2)]
    line_start, line_total = line_of(start, line_ref), line_of(total, line2_ref)
    for h in range(2):
        start_ref[h] = start[h]
    start_f_ref[...] = jnp.broadcast_to(before_f, (8, 128))
    for x in range(msg.shape[0] // 2):
        mine = aux.x == x
        tail = [
            jnp.where(mine, line_start, line_total),
            jnp.where(mine, before_f, total_f),
            factor_y,
            aux.log_x,
            factor_y,
        ]
        tail = jnp.concatenate(tail, axis=0)
        for core in range(2):
            for h in range(2):
                msg[2 * x + core, pl.ds(16 * h, 16), :] = jnp.where(aux.core == core, total[h], term_y[h])
            msg[2 * x + core, 32:40, :] = tail


def turn_kernel(aux_ref, got, start_ref, start_f_ref, south, north, msg, drift_ref, low_ref, pair_ref, pair_f_ref, line_ref):
    aux = Aux(aux_ref)
    first = aux.core == 0.0
    begin = [jnp.zeros((16, 128), F32)] * 2
    begin_line = jnp.zeros((4, 128), F32)
    term, tail = [0.0, 0.0], 0.0
    for x in range(got.shape[0] // 2):
        one, two = halves(got, 2 * x), halves(got, 2 * x + 1)
        tails = got[2 * x, 32:40, :], got[2 * x + 1, 32:40, :]
        own_tail, other_tail = jnp.where(first, *tails), jnp.where(first, *tails[::-1])
        go, mine = aux.x > x, aux.x == x
        own = [jnp.where(first, one[h], two[h]) for h in range(2)]
        begin = [jnp.where(go, own_tail[4:5] * begin[h] + own[h], begin[h]) for h in range(2)]
        begin_line = jnp.where(go, other_tail[4:5] * begin_line + other_tail[0:4], begin_line)
        term = [jnp.where(mine, jnp.where(first, two[h], one[h]), term[h]) for h in range(2)]
        tail = jnp.where(mine, other_tail, tail)
    away = aux.col == 0.0
    drift = [jnp.where(away, 0.0, start_f_ref[0:1, :] * begin[h] + start_ref[h]) for h in range(2)]
    line = line_of(drift, line_ref)
    other_line = jnp.where(away, 0.0, tail[4:5] * begin_line + tail[0:4])
    factor, other_factor = edge_y(aux), tail[5:6]
    south_line = everywhere(line, 0)
    term_line = four(everywhere(line, 3) - factor * south_line)
    other_line = four(everywhere(other_line, 3) - other_factor * everywhere(other_line, 0))
    south_line = four(south_line)
    places = place_y(*iotas(16))
    pairs = []
    for h in range(2):
        gain = gain_at(places[h], aux.log_x)
        drift_ref[h] = drift[h]
        low_ref[h] = south[h] + gain * south_line
        own = north[h] - factor * south[h] + gain * term_line
        other = term[h] + gain_at(places[h], tail[6:7]) * other_line
        pair_ref[h] = jnp.where(first, 0.0, other)
        pairs.append(jnp.where(first, other_factor * own + other, factor * other + own))
    pair_f_ref[...] = jnp.broadcast_to(jnp.where(first, 1.0, other_factor), (8, 128))
    rows = [jnp.broadcast_to(factor * other_factor, (8, 128))] if msg.shape[1] > 32 else []
    fill(msg, pairs, rows)


def seams(aux, pred_ref, got, factors, drift_ref, low_ref, pair_ref, pair_f_ref, put):
    sub, lane = iotas(16)
    by, bx = sub % 4, sub // 4
    sx, sy = lane // 64, (lane // 32) % 2
    before = [jnp.zeros((16, 128), F32)] * 2
    for k in range(got.shape[0]):
        f, t, go = factors(k), halves(got, k), aux.z > k
        before = [jnp.where(go, f * before[h] + t[h], before[h]) for h in range(2)]
    before = [pair_f_ref[0:1, :] * before[h] + pair_ref[h] for h in range(2)]
    drift_y = [jnp.where(aux.row == 0.0, 0.0, before[h] - low_ref[h]) for h in range(2)]
    drift_x = [drift_ref[h] for h in range(2)]
    gain_x = [gain_at(8 * bx + 2 * q + sx, aux.log_x) for q in range(4)]
    gain_y = [gain_at(8 * by + 2 * q + sy, aux.log_y) for q in range(4)]
    spread_x = [[None] * 4 for _ in range(4)]
    spread_y = [[None] * 4 for _ in range(4)]
    for q in range(4):
        d = drift_x[q % 2]
        d = jnp.where(sx == q // 2, d, turn_lanes(d, 64))
        e = drift_y[q % 2]
        e = jnp.where(sy == q // 2, e, swap_sy(e, lane))
        for qz in range(4):
            m = jnp.where(bx == qz, d, 0.0)
            m = m + turn_rows(m, 8)
            spread_x[q][qz] = m + turn_rows(m, 4)
            m = turn_rows(jnp.where(by == qz, e, 0.0), -qz)
            m = m + turn_rows(m, 1)
            spread_y[q][qz] = m + turn_rows(m, 2)
    for qx in range(4):
        for qy in range(4):
            for qz in range(4):
                q = 16 * qx + 4 * qy + qz
                value = pred_ref[pl.ds(16 * q, 16), :].astype(F32)
                value = value + gain_x[qx] * spread_x[qy][qz] + gain_y[qy] * spread_y[qx][qz]
                put(q, value)


def first_kernel(latent, occupancy, carry_x, carry_y, w_in, w_down, w_mid, w_up, w_out, *rest):
    pred_ref, msg, west, south, north, aux_ref, wide_in, wide_out = rest[:8]
    latent_v, occupancy_v, carry_x_v, carry_y_v, w_in_v, w_down_v, w_mid_v, w_up_v, w_out_v = rest[8:17]
    state, first_ref, second_ref, sems = rest[17:]
    pairs = [
        (w_in, w_in_v),
        (w_out, w_out_v),
        (occupancy, occupancy_v),
        (carry_x, carry_x_v),
        (carry_y, carry_y_v),
        (latent, latent_v),
        (w_down, w_down_v),
        (w_mid, w_mid_v),
        (w_up, w_up_v),
    ]
    copies = [pltpu.make_async_copy(src, dst, sems.at[k]) for k, (src, dst) in enumerate(pairs)]
    for copy in copies:
        copy.start()
    x, y, z, core = (lax.axis_index(name) for name in ("x", "y", "z", "core"))
    columns = lax.axis_size("y")
    for copy in copies[:5]:
        copy.wait()
    wide_in[...] = widen(w_in_v[...], 16, 64).astype(BF16)
    wide_out[...] = widen(w_out_v[...], 16, 64).T.astype(BF16)
    rates = jnp.concatenate([carry_x_v[...], carry_y_v[...]], axis=0)
    rates = jnp.concatenate([rates] * 8, axis=1)
    aux_ref[0:2, :] = jnp.log(rates)
    for k, place in enumerate((x * columns + y, x, y, 2 * z + core, z, core)):
        aux_ref[2 + k : 3 + k, :] = jnp.full((1, 128), place, jnp.int32).astype(F32)
    r, c = (lax.broadcasted_iota(jnp.int32, (16, 16), k) for k in (0, 1))
    occupied = jnp.where(r == c, occupancy_v[...].astype(F32), 0.0)
    aux_ref[8:24, :] = jnp.broadcast_to(jnp.sum(occupied, axis=1, keepdims=True), (16, 128))
    copies[5].wait()
    turned = jnp.swapaxes(latent_v[...].astype(F32), 0, 1)
    state[...] = turned.reshape(1024, 128).astype(BF16)
    for copy in copies[6:]:
        copy.wait()
    weights = (wide_in, w_down_v, w_mid_v, w_up_v, wide_out)
    net(state, Aux(aux_ref), weights, first_ref, second_ref, pred_ref, (msg, west, south, north))


def next_kernel(aux_ref, pred, got, drift, low, pair, pair_f, wide_in, w_down, w_mid, w_up, wide_out, *rest):
    outs, (factor_ref, state, first_ref, second_ref) = rest[:5], rest[5:]
    aux = Aux(aux_ref)
    for k in range(got.shape[0]):
        factor_ref[k : k + 1, :] = got[k, 32:33, :]

    def put(q, value):
        state[pl.ds(16 * q, 16), :] = value.astype(BF16)

    seams(aux, pred, got, lambda k: got[k, 32:33, :], drift, low, pair, pair_f, put)
    net(state, aux, (wide_in, w_down, w_mid, w_up, wide_out), first_ref, second_ref, outs[0], outs[1:])


def last_kernel(aux_ref, pred, got, drift, low, pair, pair_f, factor_ref, out, state):
    def put(q, value):
        state[q] = value

    seams(Aux(aux_ref), pred, got, lambda k: factor_ref[k : k + 1, :], drift, low, pair, pair_f, put)
    out[...] = jnp.swapaxes(state[...], 0, 1).astype(BF16)


def call(kernel, out_shape, scratch, args, name, space=pltpu.VMEM, limit=24):
    vmem = pl.BlockSpec(memory_space=pltpu.VMEM)
    return pl.pallas_call(
        kernel,
        out_shape=out_shape,
        in_specs=[pl.BlockSpec(memory_space=space)] * len(args),
        out_specs=jax.tree.map(lambda _: vmem, out_shape),
        scratch_shapes=scratch,
        compiler_params=pltpu.CompilerParams(vmem_limit_bytes=limit * 1024 * 1024),
        name=name,
    )(*args)


def per_device(sizes, latent, occupancy, carry_x, carry_y, w_in, w_down, w_mid, w_up, w_out):
    xs, ys, zs, _ = sizes
    shape = jax.ShapeDtypeStruct
    plane, row = shape((2, 16, 128), F32), shape((8, 128), F32)
    lines = pltpu.VMEM((16, 128), F32)
    net_scratch = [
        pltpu.VMEM((1024, 128), BF16),
        pltpu.VMEM((1024, 512), BF16),
        pltpu.VMEM((1024, 128), BF16),
    ]
    for step in range(STEPS):
        tall = 40 if step == 0 else 32
        net_out = (shape((1024, 128), BF16), shape((ys, tall, 128), F32), plane, plane, plane)
        if step == 0:
            args = (latent[0, 0], occupancy[0], carry_x[0], carry_y[0], w_in, w_down, w_mid, w_up, w_out.T)
            held = [pltpu.VMEM(a.shape, a.dtype) for a in args]
            pred, msg, west, south, north, aux, wide_in, wide_out = call(
                first_kernel,
                (*net_out, shape((24, 128), F32), shape((128, 512), BF16), shape((512, 128), BF16)),
                held + net_scratch + [pltpu.SemaphoreType.DMA((len(args),))],
                args,
                "net_first",
                pl.ANY,
                60,
            )
        else:
            pred, msg, west, south, north, factors_z = call(
                next_kernel,
                (*net_out, shape((zs, 128), F32)),
                net_scratch,
                (aux, *seam_ins, wide_in, w_down, w_mid, w_up, wide_out),
                "seams_net",
            )
        got = lax.all_to_all(msg, "y", 0, 0)
        group_out = (shape((2 * xs, 40, 128), F32), plane, row)
        if step == 0:
            msg, start, start_f, factors_y = call(
                group_kernel,
                (*group_out, shape((ys, 128), F32)),
                [lines, lines],
                (aux, got, west, south, north),
                "group",
            )
        else:
            msg, start, start_f = call(
                group_kernel, group_out, [lines, lines], (aux, got, factors_y, west, south, north), "group"
            )
        got = lax.all_to_all(msg, ("x", "core"), 0, 0)
        msg, *seam_ins = call(
            turn_kernel,
            (shape((zs, tall, 128), F32), plane, plane, plane, row),
            [lines],
            (aux, got, start, start_f, south, north),
            "turn",
        )
        got = lax.all_to_all(msg, "z", 0, 0)
        seam_ins = (pred, got, *seam_ins)
    out = call(
        last_kernel,
        shape((16, 64, 128), BF16),
        [pltpu.VMEM((64, 16, 128), F32)],
        (aux, *seam_ins, factors_z),
        "seams_last",
    )
    return out[None, None]


def solution(mesh):
    columns, rows = mesh.shape["gx"], mesh.shape["gy"]
    inner = 8 if columns % 8 == 0 else 2
    sizes = (columns // inner, inner, rows // 2, 2)
    parts = jax.sharding.Mesh(mesh.devices.reshape(sizes), ("x", "y", "z", "core"))
    gx, gy = ("x", "y"), ("z", "core")
    in_specs = (
        P(gx, gy, None, None, None),
        P(gx, gy, None),
        P(gx, gy, None),
        P(gx, gy, None),
        P(),
        P(),
        P(),
        P(),
        P(),
    )
    return jax.shard_map(
        functools.partial(per_device, sizes),
        mesh=parts,
        in_specs=in_specs,
        out_specs=P(gx, gy, None, None, None),
        check_vma=False,
    )
```

```python
import functools

import jax
import jax.numpy as jnp
from jax import lax
from jax.experimental import pallas as pl
from jax.experimental.pallas import tpu as pltpu
from jax.sharding import PartitionSpec as P

STEPS = 2
F32 = jnp.float32
BF16 = jnp.bfloat16


def silu(v):
    half = 0.5 * v
    return half + half * jnp.tanh(half)


def iotas(rows):
    sub = lax.broadcasted_iota(jnp.int32, (rows, 128), 0)
    lane = lax.broadcasted_iota(jnp.int32, (rows, 128), 1)
    return sub, lane


def turn_lanes(x, by):
    return pltpu.roll(x, by % 128, x.ndim - 1)


def turn_rows(x, by):
    by = by % x.shape[0]
    return x if by == 0 else pltpu.roll(x, by, 0)


def swap_sy(x, lane):
    return jnp.where((lane // 32) % 2 == 0, turn_lanes(x, -32), turn_lanes(x, 32))


def edge_gain(logs):
    return sum(jnp.exp((p + 0.5) / 32.0 * logs) for p in range(24, 32)) * 0.125


def gain_at(place, logs):
    return jnp.exp(place.astype(F32) / 32.0 * logs + (0.5 / 32.0) * logs)


def widen(narrow, rows, cols):
    r = lax.broadcasted_iota(jnp.int32, (8 * rows, rows), 0) % rows
    k = lax.broadcasted_iota(jnp.int32, (8 * rows, rows), 1)
    tall = jnp.dot((r == k).astype(BF16), narrow, preferred_element_type=F32).astype(BF16)
    k = lax.broadcasted_iota(jnp.int32, (cols, 8 * cols), 0)
    c = lax.broadcasted_iota(jnp.int32, (cols, 8 * cols), 1) % cols
    both = jnp.dot(tall, (k == c).astype(BF16), preferred_element_type=F32)
    r = lax.broadcasted_iota(jnp.int32, (8 * rows, 8 * cols), 0) // rows
    c = lax.broadcasted_iota(jnp.int32, (8 * rows, 8 * cols), 1) // cols
    return jnp.where(r == c, both, 0.0)


def net(state, ready, weights, first_ref, second_ref, pred_ref, outs):
    wide_in, w_down, w_mid, w_up, wide_out = weights
    msg, west_ref, south_ref, north_ref = outs
    for qx in range(2):
        rows = pl.ds(512 * qx, 512)
        first = silu(jnp.dot(state[rows, :], wide_in[...], preferred_element_type=F32)).astype(BF16)
        first_ref[rows, :] = first
        pre = jnp.dot(first, w_down[...], preferred_element_type=F32)
        pre = pre * lax.rsqrt(jnp.mean(pre * pre, axis=-1, keepdims=True) + 1e-06)
        second_ref[pl.ds(256 + 512 * qx, 512), :] = silu(pre).astype(BF16)

    sub, lane = iotas(16)
    by, bx = sub % 4, sub // 4
    total_x = [[None] * 4 for _ in range(4)]
    south, north = [0.0] * 4, [0.0] * 4
    aux = ready()
    log_x, occupied, col = aux.log_x, aux.occupied, aux.col
    second_ref[pl.ds(0, 256), :] = jnp.zeros((256, 128), BF16)
    second_ref[pl.ds(1280, 256), :] = jnp.zeros((256, 128), BF16)
    mids = jnp.concatenate([w_mid[k] for k in range(7)], axis=0)
    for group in range(2):
        base = 512 * group
        rows = pl.ds(base, 512)
        second = second_ref[pl.ds(base + 256, 512), :]
        parts = [second, second_ref[pl.ds(base, 512), :], second_ref[pl.ds(base + 512, 512), :]]
        gap = jnp.zeros((64, 128), BF16)
        gap16 = jnp.zeros((16, 128), BF16)
        left, right, below, above = [], [], [], []
        for plane in range(2):
            own = second[256 * plane : 256 * plane + 256]
            left += [gap, own[:192]]
            right += [own[64:], gap]
            for qy in range(4):
                o = own[64 * qy : 64 * qy + 64]
                below += [gap16, o[:48]]
                above += [o[16:], gap16]
        parts += [jnp.concatenate(p, axis=0) for p in (left, right, below, above)]
        stacked = jnp.concatenate(parts, axis=1)
        mixed = jnp.dot(stacked, mids, preferred_element_type=F32)
        middle = (second.astype(F32) + silu(mixed)).astype(BF16)
        upper = jnp.dot(middle, w_up[...], preferred_element_type=F32) + first_ref[rows, :].astype(F32)
        upper = silu(upper).astype(BF16)
        update = jnp.dot(upper, wide_out[...], preferred_element_type=F32)
        update = update.reshape(32, 16, 128) * occupied[None]
        preds = (state[rows, :].astype(F32).reshape(32, 16, 128) + update).astype(BF16)
        pred_ref[rows, :] = preds.reshape(512, 128)
        for plane in range(2):
            qx = 2 * group + plane
            pred = preds[16 * plane : 16 * plane + 16].astype(F32)
            for qy in range(4):
                for qz in range(4):
                    value = pred[4 * qy + qz]
                    total_x[qy][qz] = value if qx == 0 else total_x[qy][qz] + value
            for qz in range(4):
                s = pred[qz] + pred[4 + qz] + pred[8 + qz] + pred[12 + qz]
                s = (s + swap_sy(s, lane)) * 0.125
                south[qx] = south[qx] + jnp.where(by == qz, turn_rows(s, qz), 0.0)
                north[qx] = north[qx] + jnp.where(by == qz, turn_rows(s, qz - 3), 0.0)

    west, east = [0.0] * 4, [0.0] * 4
    for qy in range(4):
        for qz in range(4):
            s = total_x[qy][qz]
            s = (s + turn_lanes(s, 64)) * 0.125
            west[qy] = west[qy] + jnp.where(bx == qz, turn_rows(s, 4 * qz), 0.0)
            east[qy] = east[qy] + jnp.where(bx == qz, turn_rows(s, 4 * qz + 4), 0.0)
    low_sx, low_sy = lane < 64, (lane // 32) % 2 == 0
    factor = jnp.where(col == 0.0, 0.0, edge_gain(log_x))
    terms = []
    for h in range(2):
        w = jnp.where(low_sx, west[h], west[2 + h])
        terms.append(jnp.where(low_sx, east[h], east[2 + h]) - factor * w)
        west_ref[h] = w
        south_ref[h] = jnp.where(low_sy, south[h], south[2 + h])
        north_ref[h] = jnp.where(low_sy, north[h], north[2 + h])
    fill(msg, terms, [jnp.broadcast_to(factor, (8, 128))] if msg.shape[1] > 32 else [])


class Aux:
    def __init__(self, ref):
        self.log_x, self.log_y = ref[0:1, :], ref[1:2, :]
        self.col, self.x, self.y, self.row, self.z, self.core = (ref[k : k + 1, :] for k in range(2, 8))
        self.occupied = ref[8:24, :]


def halves(ref, k):
    return [ref[k, pl.ds(16 * h, 16), :] for h in range(2)]


def fill(msg, planes, rows=()):
    for k, value in enumerate([*planes, *rows]):
        size = 16 if k < 2 else 8
        at = 16 * k if k < 2 else 32 + 8 * (k - 2)
        msg[:, pl.ds(at, size), :] = jnp.broadcast_to(value[None], (msg.shape[0], size, 128))


def line_of(planes, ref):
    sub, lane = iotas(16)
    value = planes[0] + planes[1]
    value = value + turn_lanes(value, 64)
    value = (value + turn_lanes(value, 32)) * 0.125
    by, part = sub % 4, lane // 32
    value = jnp.where(((part == 0) & (by == 0)) | ((part == 3) & (by == 3)), value, 0.0)
    ref[...] = value + turn_rows(value, -3)
    return ref[pl.ds(0, 4, stride=4), :]


def everywhere(x, which):
    part = lax.broadcasted_iota(jnp.int32, x.shape, x.ndim - 1) // 32
    x = jnp.where(part == which, x, 0.0)
    x = x + turn_lanes(x, 32)
    return x + turn_lanes(x, 64)


def four(line):
    return jnp.concatenate([line] * 4, axis=0)


def place_y(sub, lane):
    return [8 * (sub // 4) + 2 * (2 * ((lane // 32) % 2) + h) + lane // 64 for h in range(2)]


def edge_y(aux):
    return jnp.where(aux.row == 0.0, 0.0, edge_gain(aux.log_y))


def group_kernel(aux_ref, got, *rest):
    if got.shape[1] > 32:
        west, south, north, msg, start_ref, start_f_ref, factor_ref, line_ref, line2_ref = rest
        for k in range(got.shape[0]):
            factor_ref[k : k + 1, :] = got[k, 32:33, :]
    else:
        factor_ref, west, south, north, msg, start_ref, start_f_ref, line_ref, line2_ref = rest
    aux = Aux(aux_ref)
    zero, one = [jnp.zeros((16, 128), F32)] * 2, jnp.ones((1, 128), F32)
    before, before_f, total, total_f = zero, one, zero, one
    for k in range(got.shape[0]):
        f, t, go = factor_ref[k : k + 1, :], halves(got, k), aux.y > k
        before = [jnp.where(go, f * before[h] + t[h], before[h]) for h in range(2)]
        before_f = jnp.where(go, f * before_f, before_f)
        total = [f * total[h] + t[h] for h in range(2)]
        total_f = f * total_f
    start = [before[h] - west[h] for h in range(2)]
    factor_y = edge_y(aux)
    term_y = [north[h] - factor_y * south[h] for h in range(2)]
    line_start, line_total = line_of(start, line_ref), line_of(total, line2_ref)
    for h in range(2):
        start_ref[h] = start[h]
    start_f_ref[...] = jnp.broadcast_to(before_f, (8, 128))
    for x in range(msg.shape[0] // 2):
        mine = aux.x == x
        tail = [
            jnp.where(mine, line_start, line_total),
            jnp.where(mine, before_f, total_f),
            factor_y,
            aux.log_x,
            factor_y,
        ]
        tail = jnp.concatenate(tail, axis=0)
        for core in range(2):
            for h in range(2):
                msg[2 * x + core, pl.ds(16 * h, 16), :] = jnp.where(aux.core == core, total[h], term_y[h])
            msg[2 * x + core, 32:40, :] = tail


def turn_kernel(aux_ref, got, start_ref, start_f_ref, south, north, msg, drift_ref, low_ref, pair_ref, pair_f_ref, line_ref):
    aux = Aux(aux_ref)
    first = aux.core == 0.0
    begin = [jnp.zeros((16, 128), F32)] * 2
    begin_line = jnp.zeros((4, 128), F32)
    term, tail = [0.0, 0.0], 0.0
    for x in range(got.shape[0] // 2):
        one, two = halves(got, 2 * x), halves(got, 2 * x + 1)
        tails = got[2 * x, 32:40, :], got[2 * x + 1, 32:40, :]
        own_tail, other_tail = jnp.where(first, *tails), jnp.where(first, *tails[::-1])
        go, mine = aux.x > x, aux.x == x
        own = [jnp.where(first, one[h], two[h]) for h in range(2)]
        begin = [jnp.where(go, own_tail[4:5] * begin[h] + own[h], begin[h]) for h in range(2)]
        begin_line = jnp.where(go, other_tail[4:5] * begin_line + other_tail[0:4], begin_line)
        term = [jnp.where(mine, jnp.where(first, two[h], one[h]), term[h]) for h in range(2)]
        tail = jnp.where(mine, other_tail, tail)
    away = aux.col == 0.0
    drift = [jnp.where(away, 0.0, start_f_ref[0:1, :] * begin[h] + start_ref[h]) for h in range(2)]
    line = line_of(drift, line_ref)
    other_line = jnp.where(away, 0.0, tail[4:5] * begin_line + tail[0:4])
    factor, other_factor = edge_y(aux), tail[5:6]
    south_line = everywhere(line, 0)
    term_line = four(everywhere(line, 3) - factor * south_line)
    other_line = four(everywhere(other_line, 3) - other_factor * everywhere(other_line, 0))
    south_line = four(south_line)
    places = place_y(*iotas(16))
    pairs = []
    for h in range(2):
        gain = gain_at(places[h], aux.log_x)
        drift_ref[h] = drift[h]
        low_ref[h] = south[h] + gain * south_line
        own = north[h] - factor * south[h] + gain * term_line
        other = term[h] + gain_at(places[h], tail[6:7]) * other_line
        pair_ref[h] = jnp.where(first, 0.0, other)
        pairs.append(jnp.where(first, other_factor * own + other, factor * other + own))
    pair_f_ref[...] = jnp.broadcast_to(jnp.where(first, 1.0, other_factor), (8, 128))
    rows = [jnp.broadcast_to(factor * other_factor, (8, 128))] if msg.shape[1] > 32 else []
    fill(msg, pairs, rows)


def seams(aux, pred_ref, got, factors, drift_ref, low_ref, pair_ref, pair_f_ref, put):
    sub, lane = iotas(16)
    by, bx = sub % 4, sub // 4
    sx, sy = lane // 64, (lane // 32) % 2
    before = [jnp.zeros((16, 128), F32)] * 2
    for k in range(got.shape[0]):
        f, t, go = factors(k), halves(got, k), aux.z > k
        before = [jnp.where(go, f * before[h] + t[h], before[h]) for h in range(2)]
    before = [pair_f_ref[0:1, :] * before[h] + pair_ref[h] for h in range(2)]
    drift_y = [jnp.where(aux.row == 0.0, 0.0, before[h] - low_ref[h]) for h in range(2)]
    drift_x = [drift_ref[h] for h in range(2)]
    gain_x = [gain_at(8 * bx + 2 * q + sx, aux.log_x) for q in range(4)]
    gain_y = [gain_at(8 * by + 2 * q + sy, aux.log_y) for q in range(4)]
    spread_x = [[None] * 4 for _ in range(4)]
    spread_y = [[None] * 4 for _ in range(4)]
    for q in range(4):
        d = drift_x[q % 2]
        d = jnp.where(sx == q // 2, d, turn_lanes(d, 64))
        e = drift_y[q % 2]
        e = jnp.where(sy == q // 2, e, swap_sy(e, lane))
        for qz in range(4):
            m = jnp.where(bx == qz, d, 0.0)
            m = m + turn_rows(m, 8)
            spread_x[q][qz] = m + turn_rows(m, 4)
            m = turn_rows(jnp.where(by == qz, e, 0.0), -qz)
            m = m + turn_rows(m, 1)
            spread_y[q][qz] = m + turn_rows(m, 2)
    for qx in range(4):
        for qy in range(4):
            for qz in range(4):
                q = 16 * qx + 4 * qy + qz
                value = pred_ref[pl.ds(16 * q, 16), :].astype(F32)
                value = value + gain_x[qx] * spread_x[qy][qz] + gain_y[qy] * spread_y[qx][qz]
                put(q, value)


def first_kernel(latent, occupancy, carry_x, carry_y, w_in, w_down, w_mid, w_up, w_out, *rest):
    pred_ref, msg, west, south, north, aux_ref, wide_in, wide_out = rest[:8]
    latent_v, occupancy_v, carry_x_v, carry_y_v, w_in_v, w_down_v, w_mid_v, w_up_v, w_out_v = rest[8:17]
    state, first_ref, second_ref, sems = rest[17:]
    pairs = [
        (w_in, w_in_v),
        (latent, latent_v),
        (w_down, w_down_v),
        (w_mid, w_mid_v),
        (w_up, w_up_v),
        (w_out, w_out_v),
        (occupancy, occupancy_v),
        (carry_x, carry_x_v),
        (carry_y, carry_y_v),
    ]
    copies = [pltpu.make_async_copy(src, dst, sems.at[k]) for k, (src, dst) in enumerate(pairs)]
    for copy in copies:
        copy.start()
    x, y, z, core = (lax.axis_index(name) for name in ("x", "y", "z", "core"))
    columns = lax.axis_size("y")
    copies[0].wait()
    wide_in[...] = widen(w_in_v[...], 16, 64).astype(BF16)
    copies[1].wait()
    turned = jnp.swapaxes(latent_v[...].astype(F32), 0, 1)
    state[...] = turned.reshape(1024, 128).astype(BF16)
    copies[2].wait()

    def ready():
        for copy in copies[3:]:
            copy.wait()
        wide_out[...] = widen(w_out_v[...], 16, 64).T.astype(BF16)
        rates = jnp.concatenate([carry_x_v[...], carry_y_v[...]], axis=0)
        rates = jnp.concatenate([rates] * 8, axis=1)
        aux_ref[0:2, :] = jnp.log(rates)
        for k, place in enumerate((x * columns + y, x, y, 2 * z + core, z, core)):
            aux_ref[2 + k : 3 + k, :] = jnp.full((1, 128), place, jnp.int32).astype(F32)
        r, c = (lax.broadcasted_iota(jnp.int32, (16, 16), k) for k in (0, 1))
        occupied = jnp.where(r == c, occupancy_v[...].astype(F32), 0.0)
        aux_ref[8:24, :] = jnp.broadcast_to(jnp.sum(occupied, axis=1, keepdims=True), (16, 128))
        return Aux(aux_ref)

    weights = (wide_in, w_down_v, w_mid_v, w_up_v, wide_out)
    net(state, ready, weights, first_ref, second_ref, pred_ref, (msg, west, south, north))


def next_kernel(aux_ref, pred, got, drift, low, pair, pair_f, wide_in, w_down, w_mid, w_up, wide_out, *rest):
    outs, (factor_ref, state, first_ref, second_ref) = rest[:5], rest[5:]
    aux = Aux(aux_ref)
    for k in range(got.shape[0]):
        factor_ref[k : k + 1, :] = got[k, 32:33, :]

    def put(q, value):
        state[pl.ds(16 * q, 16), :] = value.astype(BF16)

    seams(aux, pred, got, lambda k: got[k, 32:33, :], drift, low, pair, pair_f, put)
    net(state, lambda: aux, (wide_in, w_down, w_mid, w_up, wide_out), first_ref, second_ref, outs[0], outs[1:])


def last_kernel(aux_ref, pred, got, drift, low, pair, pair_f, factor_ref, out, state, turned, sems):
    copies = []

    def put(q, value):
        state[q] = value
        if q % 16 == 15:
            rows = pl.ds(q - 15, 16)
            turned[:, rows, :] = jnp.swapaxes(state[rows], 0, 1).astype(BF16)
            copies.append(pltpu.make_async_copy(turned.at[:, rows, :], out.at[:, rows, :], sems.at[q // 16]))
            copies[-1].start()

    seams(Aux(aux_ref), pred, got, lambda k: factor_ref[k : k + 1, :], drift, low, pair, pair_f, put)
    for copy in copies:
        copy.wait()


def call(kernel, out_shape, scratch, args, name, space=pltpu.VMEM, limit=24, out_space=pltpu.VMEM):
    vmem = pl.BlockSpec(memory_space=out_space)
    return pl.pallas_call(
        kernel,
        out_shape=out_shape,
        in_specs=[pl.BlockSpec(memory_space=space)] * len(args),
        out_specs=jax.tree.map(lambda _: vmem, out_shape),
        scratch_shapes=scratch,
        compiler_params=pltpu.CompilerParams(vmem_limit_bytes=limit * 1024 * 1024),
        name=name,
    )(*args)


def per_device(sizes, latent, occupancy, carry_x, carry_y, w_in, w_down, w_mid, w_up, w_out):
    xs, ys, zs, _ = sizes
    shape = jax.ShapeDtypeStruct
    plane, row = shape((2, 16, 128), F32), shape((8, 128), F32)
    lines = pltpu.VMEM((16, 128), F32)
    net_scratch = [
        pltpu.VMEM((1024, 128), BF16),
        pltpu.VMEM((1024, 512), BF16),
        pltpu.VMEM((1536, 128), BF16),
    ]
    for step in range(STEPS):
        tall = 40 if step == 0 else 32
        net_out = (shape((1024, 128), BF16), shape((ys, tall, 128), F32), plane, plane, plane)
        if step == 0:
            args = (latent[0, 0], occupancy[0], carry_x[0], carry_y[0], w_in, w_down, w_mid, w_up, w_out.T)
            held = [pltpu.VMEM(a.shape, a.dtype) for a in args]
            pred, msg, west, south, north, aux, wide_in, wide_out = call(
                first_kernel,
                (*net_out, shape((24, 128), F32), shape((128, 512), BF16), shape((512, 128), BF16)),
                held + net_scratch + [pltpu.SemaphoreType.DMA((len(args),))],
                args,
                "net_first",
                pl.ANY,
                60,
            )
        else:
            pred, msg, west, south, north, factors_z = call(
                next_kernel,
                (*net_out, shape((zs, 128), F32)),
                net_scratch,
                (aux, *seam_ins, wide_in, w_down, w_mid, w_up, wide_out),
                "seams_net",
            )
        got = lax.all_to_all(msg, "y", 0, 0)
        group_out = (shape((2 * xs, 40, 128), F32), plane, row)
        if step == 0:
            msg, start, start_f, factors_y = call(
                group_kernel,
                (*group_out, shape((ys, 128), F32)),
                [lines, lines],
                (aux, got, west, south, north),
                "group",
            )
        else:
            msg, start, start_f = call(
                group_kernel, group_out, [lines, lines], (aux, got, factors_y, west, south, north), "group"
            )
        got = lax.all_to_all(msg, ("x", "core"), 0, 0)
        msg, *seam_ins = call(
            turn_kernel,
            (shape((zs, tall, 128), F32), plane, plane, plane, row),
            [lines],
            (aux, got, start, start_f, south, north),
            "turn",
        )
        got = lax.all_to_all(msg, "z", 0, 0)
        seam_ins = (pred, got, *seam_ins)
    out = call(
        last_kernel,
        shape((16, 64, 128), BF16),
        [pltpu.VMEM((64, 16, 128), F32), pltpu.VMEM((16, 64, 128), BF16), pltpu.SemaphoreType.DMA((4,))],
        (aux, *seam_ins, factors_z),
        "seams_last",
        out_space=pl.ANY,
    )
    return out[None, None]


def solution(mesh):
    columns, rows = mesh.shape["gx"], mesh.shape["gy"]
    inner = 8 if columns % 8 == 0 else 2
    sizes = (columns // inner, inner, rows // 2, 2)
    parts = jax.sharding.Mesh(mesh.devices.reshape(sizes), ("x", "y", "z", "core"))
    gx, gy = ("x", "y"), ("z", "core")
    in_specs = (
        P(gx, gy, None, None, None),
        P(gx, gy, None),
        P(gx, gy, None),
        P(gx, gy, None),
        P(),
        P(),
        P(),
        P(),
        P(),
    )
    return jax.shard_map(
        functools.partial(per_device, sizes),
        mesh=parts,
        in_specs=in_specs,
        out_specs=P(gx, gy, None, None, None),
        check_vma=False,
    )
```

```python
import functools

import jax
import jax.numpy as jnp
from jax import lax
from jax.experimental import pallas as pl
from jax.experimental.pallas import tpu as pltpu
from jax.sharding import PartitionSpec as P

STEPS = 2
F32 = jnp.float32
BF16 = jnp.bfloat16


def silu(v):
    half = 0.5 * v
    return half + half * jnp.tanh(half)


def iotas(rows):
    sub = lax.broadcasted_iota(jnp.int32, (rows, 128), 0)
    lane = lax.broadcasted_iota(jnp.int32, (rows, 128), 1)
    return sub, lane


def turn_lanes(x, by):
    return pltpu.roll(x, by % 128, x.ndim - 1)


def turn_rows(x, by):
    by = by % x.shape[0]
    return x if by == 0 else pltpu.roll(x, by, 0)


def swap_sy(x, lane):
    return jnp.where((lane // 32) % 2 == 0, turn_lanes(x, -32), turn_lanes(x, 32))


def edge_gain(logs):
    return sum(jnp.exp((p + 0.5) / 32.0 * logs) for p in range(24, 32)) * 0.125


def gain_at(place, logs):
    return jnp.exp(place.astype(F32) / 32.0 * logs + (0.5 / 32.0) * logs)


def widen(narrow):
    row = jnp.concatenate([narrow.astype(F32)] * 8, axis=1)
    both = jnp.concatenate([row] * 8, axis=0)
    r = lax.broadcasted_iota(jnp.int32, both.shape, 0) // 16
    c = lax.broadcasted_iota(jnp.int32, both.shape, 1) // 64
    return jnp.where(r == c, both, 0.0)


def net(state, ready, weights, first_ref, second_ref, pred_ref, outs):
    wide_in, w_down, w_mid, w_up, wide_out = weights
    msg, west_ref, south_ref, north_ref = outs
    for qx in range(2):
        rows = pl.ds(512 * qx, 512)
        first = silu(jnp.dot(state[rows, :], wide_in[...], preferred_element_type=F32)).astype(BF16)
        first_ref[rows, :] = first
        pre = jnp.dot(first, w_down[...], preferred_element_type=F32)
        pre = pre * lax.rsqrt(jnp.mean(pre * pre, axis=-1, keepdims=True) + 1e-06)
        second_ref[pl.ds(256 + 512 * qx, 512), :] = silu(pre).astype(BF16)

    sub, lane = iotas(16)
    by, bx = sub % 4, sub // 4
    total_x = [[None] * 4 for _ in range(4)]
    south, north = [0.0] * 4, [0.0] * 4
    aux = ready()
    log_x, occupied, col = aux.log_x, aux.occupied, aux.col
    second_ref[pl.ds(0, 256), :] = jnp.zeros((256, 128), BF16)
    second_ref[pl.ds(1280, 256), :] = jnp.zeros((256, 128), BF16)
    mids = jnp.concatenate([w_mid[k] for k in range(7)], axis=0)
    for group in range(2):
        base = 512 * group
        rows = pl.ds(base, 512)
        second = second_ref[pl.ds(base + 256, 512), :]
        parts = [second, second_ref[pl.ds(base, 512), :], second_ref[pl.ds(base + 512, 512), :]]
        gap = jnp.zeros((64, 128), BF16)
        gap16 = jnp.zeros((16, 128), BF16)
        left, right, below, above = [], [], [], []
        for plane in range(2):
            own = second[256 * plane : 256 * plane + 256]
            left += [gap, own[:192]]
            right += [own[64:], gap]
            for qy in range(4):
                o = own[64 * qy : 64 * qy + 64]
                below += [gap16, o[:48]]
                above += [o[16:], gap16]
        parts += [jnp.concatenate(p, axis=0) for p in (left, right, below, above)]
        stacked = jnp.concatenate(parts, axis=1)
        mixed = jnp.dot(stacked, mids, preferred_element_type=F32)
        middle = (second.astype(F32) + silu(mixed)).astype(BF16)
        upper = jnp.dot(middle, w_up[...], preferred_element_type=F32) + first_ref[rows, :].astype(F32)
        upper = silu(upper).astype(BF16)
        update = jnp.dot(upper, wide_out[...], preferred_element_type=F32)
        update = update.reshape(32, 16, 128) * occupied[None]
        preds = (state[rows, :].astype(F32).reshape(32, 16, 128) + update).astype(BF16)
        pred_ref[rows, :] = preds.reshape(512, 128)
        for plane in range(2):
            qx = 2 * group + plane
            pred = preds[16 * plane : 16 * plane + 16].astype(F32)
            for qy in range(4):
                for qz in range(4):
                    value = pred[4 * qy + qz]
                    total_x[qy][qz] = value if qx == 0 else total_x[qy][qz] + value
            for qz in range(4):
                s = pred[qz] + pred[4 + qz] + pred[8 + qz] + pred[12 + qz]
                s = (s + swap_sy(s, lane)) * 0.125
                south[qx] = south[qx] + jnp.where(by == qz, turn_rows(s, qz), 0.0)
                north[qx] = north[qx] + jnp.where(by == qz, turn_rows(s, qz - 3), 0.0)

    west, east = [0.0] * 4, [0.0] * 4
    for qy in range(4):
        for qz in range(4):
            s = total_x[qy][qz]
            s = (s + turn_lanes(s, 64)) * 0.125
            west[qy] = west[qy] + jnp.where(bx == qz, turn_rows(s, 4 * qz), 0.0)
            east[qy] = east[qy] + jnp.where(bx == qz, turn_rows(s, 4 * qz + 4), 0.0)
    low_sx, low_sy = lane < 64, (lane // 32) % 2 == 0
    factor = jnp.where(col == 0.0, 0.0, edge_gain(log_x))
    terms = []
    for h in range(2):
        w = jnp.where(low_sx, west[h], west[2 + h])
        terms.append(jnp.where(low_sx, east[h], east[2 + h]) - factor * w)
        west_ref[h] = w
        south_ref[h] = jnp.where(low_sy, south[h], south[2 + h])
        north_ref[h] = jnp.where(low_sy, north[h], north[2 + h])
    fill(msg, terms, [jnp.broadcast_to(factor, (8, 128))] if msg.shape[1] > 32 else [])


class Aux:
    def __init__(self, ref):
        self.log_x, self.log_y = ref[0:1, :], ref[1:2, :]
        self.col, self.x, self.y, self.row, self.z, self.core = (ref[k : k + 1, :] for k in range(2, 8))
        self.occupied = ref[8:24, :]


def halves(ref, k):
    return [ref[k, pl.ds(16 * h, 16), :] for h in range(2)]


def fill(msg, planes, rows=()):
    for k, value in enumerate([*planes, *rows]):
        size = 16 if k < 2 else 8
        at = 16 * k if k < 2 else 32 + 8 * (k - 2)
        msg[:, pl.ds(at, size), :] = jnp.broadcast_to(value[None], (msg.shape[0], size, 128))


def line_of(planes, ref):
    sub, lane = iotas(16)
    value = planes[0] + planes[1]
    value = value + turn_lanes(value, 64)
    value = (value + turn_lanes(value, 32)) * 0.125
    by, part = sub % 4, lane // 32
    value = jnp.where(((part == 0) & (by == 0)) | ((part == 3) & (by == 3)), value, 0.0)
    ref[...] = value + turn_rows(value, -3)
    return ref[pl.ds(0, 4, stride=4), :]


def everywhere(x, which):
    part = lax.broadcasted_iota(jnp.int32, x.shape, x.ndim - 1) // 32
    x = jnp.where(part == which, x, 0.0)
    x = x + turn_lanes(x, 32)
    return x + turn_lanes(x, 64)


def four(line):
    return jnp.concatenate([line] * 4, axis=0)


def place_y(sub, lane):
    return [8 * (sub // 4) + 2 * (2 * ((lane // 32) % 2) + h) + lane // 64 for h in range(2)]


def edge_y(aux):
    return jnp.where(aux.row == 0.0, 0.0, edge_gain(aux.log_y))


def group_kernel(aux_ref, got, *rest):
    if got.shape[1] > 32:
        west, term, msg, start_ref, start_f_ref, factor_ref, line_ref, line2_ref = rest
        for k in range(got.shape[0]):
            factor_ref[k : k + 1, :] = got[k, 32:33, :]
    else:
        factor_ref, west, term, msg, start_ref, start_f_ref, line_ref, line2_ref = rest
    aux = Aux(aux_ref)
    zero, one = [jnp.zeros((16, 128), F32)] * 2, jnp.ones((1, 128), F32)
    before, before_f, total, total_f = zero, one, zero, one
    for k in range(got.shape[0]):
        f, t, go = factor_ref[k : k + 1, :], halves(got, k), aux.y > k
        before = [jnp.where(go, f * before[h] + t[h], before[h]) for h in range(2)]
        before_f = jnp.where(go, f * before_f, before_f)
        total = [f * total[h] + t[h] for h in range(2)]
        total_f = f * total_f
    start = [before[h] - west[h] for h in range(2)]
    factor_y = edge_y(aux)
    term_y = [term[h] for h in range(2)]
    line_start, line_total = line_of(start, line_ref), line_of(total, line2_ref)
    for h in range(2):
        start_ref[h] = start[h]
    start_f_ref[...] = jnp.broadcast_to(before_f, (8, 128))
    for x in range(msg.shape[0] // 2):
        mine = aux.x == x
        tail = [
            jnp.where(mine, line_start, line_total),
            jnp.where(mine, before_f, total_f),
            factor_y,
            aux.log_x,
            factor_y,
        ]
        tail = jnp.concatenate(tail, axis=0)
        for core in range(2):
            for h in range(2):
                msg[2 * x + core, pl.ds(16 * h, 16), :] = jnp.where(aux.core == core, total[h], term_y[h])
            msg[2 * x + core, 32:40, :] = tail


def term_kernel(aux_ref, south, north, term_ref):
    factor = edge_y(Aux(aux_ref))
    for h in range(2):
        term_ref[h] = north[h] - factor * south[h]


def turn_kernel(aux_ref, got, start_ref, start_f_ref, south, north, msg, drift_ref, low_ref, pair_ref, pair_f_ref, line_ref):
    aux = Aux(aux_ref)
    first = aux.core == 0.0
    begin = [jnp.zeros((16, 128), F32)] * 2
    begin_line = jnp.zeros((4, 128), F32)
    term, tail = [0.0, 0.0], 0.0
    for x in range(got.shape[0] // 2):
        one, two = halves(got, 2 * x), halves(got, 2 * x + 1)
        tails = got[2 * x, 32:40, :], got[2 * x + 1, 32:40, :]
        own_tail, other_tail = jnp.where(first, *tails), jnp.where(first, *tails[::-1])
        go, mine = aux.x > x, aux.x == x
        own = [jnp.where(first, one[h], two[h]) for h in range(2)]
        begin = [jnp.where(go, own_tail[4:5] * begin[h] + own[h], begin[h]) for h in range(2)]
        begin_line = jnp.where(go, other_tail[4:5] * begin_line + other_tail[0:4], begin_line)
        term = [jnp.where(mine, jnp.where(first, two[h], one[h]), term[h]) for h in range(2)]
        tail = jnp.where(mine, other_tail, tail)
    away = aux.col == 0.0
    drift = [jnp.where(away, 0.0, start_f_ref[0:1, :] * begin[h] + start_ref[h]) for h in range(2)]
    line = line_of(drift, line_ref)
    other_line = jnp.where(away, 0.0, tail[4:5] * begin_line + tail[0:4])
    factor, other_factor = edge_y(aux), tail[5:6]
    south_line = everywhere(line, 0)
    term_line = four(everywhere(line, 3) - factor * south_line)
    other_line = four(everywhere(other_line, 3) - other_factor * everywhere(other_line, 0))
    south_line = four(south_line)
    places = place_y(*iotas(16))
    pairs = []
    for h in range(2):
        gain = gain_at(places[h], aux.log_x)
        drift_ref[h] = drift[h]
        low_ref[h] = south[h] + gain * south_line
        own = north[h] - factor * south[h] + gain * term_line
        other = term[h] + gain_at(places[h], tail[6:7]) * other_line
        pair_ref[h] = jnp.where(first, 0.0, other)
        pairs.append(jnp.where(first, other_factor * own + other, factor * other + own))
    pair_f_ref[...] = jnp.broadcast_to(jnp.where(first, 1.0, other_factor), (8, 128))
    rows = [jnp.broadcast_to(factor * other_factor, (8, 128))] if msg.shape[1] > 32 else []
    fill(msg, pairs, rows)


def seams(aux, pred_ref, got, factors, drift_ref, low_ref, pair_ref, pair_f_ref, put):
    sub, lane = iotas(16)
    by, bx = sub % 4, sub // 4
    sx, sy = lane // 64, (lane // 32) % 2
    before = [jnp.zeros((16, 128), F32)] * 2
    for k in range(got.shape[0]):
        f, t, go = factors(k), halves(got, k), aux.z > k
        before = [jnp.where(go, f * before[h] + t[h], before[h]) for h in range(2)]
    before = [pair_f_ref[0:1, :] * before[h] + pair_ref[h] for h in range(2)]
    drift_y = [jnp.where(aux.row == 0.0, 0.0, before[h] - low_ref[h]) for h in range(2)]
    drift_x = [drift_ref[h] for h in range(2)]
    gain_x = [gain_at(8 * bx + 2 * q + sx, aux.log_x) for q in range(4)]
    gain_y = [gain_at(8 * by + 2 * q + sy, aux.log_y) for q in range(4)]
    spread_x = [[None] * 4 for _ in range(4)]
    spread_y = [[None] * 4 for _ in range(4)]
    for q in range(4):
        d = drift_x[q % 2]
        d = jnp.where(sx == q // 2, d, turn_lanes(d, 64))
        e = drift_y[q % 2]
        e = jnp.where(sy == q // 2, e, swap_sy(e, lane))
        for qz in range(4):
            m = jnp.where(bx == qz, d, 0.0)
            m = m + turn_rows(m, 8)
            spread_x[q][qz] = m + turn_rows(m, 4)
            m = turn_rows(jnp.where(by == qz, e, 0.0), -qz)
            m = m + turn_rows(m, 1)
            spread_y[q][qz] = m + turn_rows(m, 2)
    for qx in range(4):
        for qy in range(4):
            for qz in range(4):
                q = 16 * qx + 4 * qy + qz
                value = pred_ref[pl.ds(16 * q, 16), :].astype(F32)
                value = value + gain_x[qx] * spread_x[qy][qz] + gain_y[qy] * spread_y[qx][qz]
                put(q, value)


def first_kernel(latent, occupancy, carry_x, carry_y, w_in, w_down, w_mid, w_up, w_out, *rest):
    pred_ref, msg, west, south, north, aux_ref, wide_in, wide_out = rest[:8]
    latent_v, occupancy_v, carry_x_v, carry_y_v, w_in_v, w_down_v, w_mid_v, w_up_v, w_out_v = rest[8:17]
    state, first_ref, second_ref, sems = rest[17:]
    pairs = [
        (latent, latent_v),
        (w_in, w_in_v),
        (w_down, w_down_v),
        (w_mid, w_mid_v),
        (w_up, w_up_v),
        (w_out, w_out_v),
        (occupancy, occupancy_v),
        (carry_x, carry_x_v),
        (carry_y, carry_y_v),
    ]
    copies = [pltpu.make_async_copy(src, dst, sems.at[k]) for k, (src, dst) in enumerate(pairs)]
    for copy in copies:
        copy.start()
    x, y, z, core = (lax.axis_index(name) for name in ("x", "y", "z", "core"))
    columns = lax.axis_size("y")
    copies[0].wait()
    copies[1].wait()
    wide_in[...] = widen(w_in_v[...]).astype(BF16)
    turned = jnp.swapaxes(latent_v[...].astype(F32), 0, 1)
    state[...] = turned.reshape(1024, 128).astype(BF16)
    for copy in copies[2:]:
        copy.wait()

    def ready():
        wide_out[...] = widen(w_out_v[...]).T.astype(BF16)
        rates = jnp.concatenate([carry_x_v[...], carry_y_v[...]], axis=0)
        rates = jnp.concatenate([rates] * 8, axis=1)
        aux_ref[0:2, :] = jnp.log(rates)
        for k, place in enumerate((x * columns + y, x, y, 2 * z + core, z, core)):
            aux_ref[2 + k : 3 + k, :] = jnp.full((1, 128), place, jnp.int32).astype(F32)
        r, c = (lax.broadcasted_iota(jnp.int32, (16, 16), k) for k in (0, 1))
        occupied = jnp.where(r == c, occupancy_v[...].astype(F32), 0.0)
        aux_ref[8:24, :] = jnp.broadcast_to(jnp.sum(occupied, axis=1, keepdims=True), (16, 128))
        return Aux(aux_ref)

    weights = (wide_in, w_down_v, w_mid_v, w_up_v, wide_out)
    net(state, ready, weights, first_ref, second_ref, pred_ref, (msg, west, south, north))


def next_kernel(aux_ref, pred, got, drift, low, pair, pair_f, wide_in, w_down, w_mid, w_up, wide_out, *rest):
    outs, (factor_ref, state, first_ref, second_ref) = rest[:5], rest[5:]
    aux = Aux(aux_ref)
    for k in range(got.shape[0]):
        factor_ref[k : k + 1, :] = got[k, 32:33, :]

    def put(q, value):
        state[pl.ds(16 * q, 16), :] = value.astype(BF16)

    seams(aux, pred, got, lambda k: got[k, 32:33, :], drift, low, pair, pair_f, put)
    net(state, lambda: aux, (wide_in, w_down, w_mid, w_up, wide_out), first_ref, second_ref, outs[0], outs[1:])


def last_kernel(aux_ref, pred, got, drift, low, pair, pair_f, factor_ref, out, state, turned, sems):
    copies = []

    def put(q, value):
        state[q] = value
        if q % 16 == 15:
            rows = pl.ds(q - 15, 16)
            turned[:, rows, :] = jnp.swapaxes(state[rows], 0, 1).astype(BF16)
            copies.append(pltpu.make_async_copy(turned.at[:, rows, :], out.at[:, rows, :], sems.at[q // 16]))
            copies[-1].start()

    seams(Aux(aux_ref), pred, got, lambda k: factor_ref[k : k + 1, :], drift, low, pair, pair_f, put)
    for copy in copies:
        copy.wait()


def call(kernel, out_shape, scratch, args, name, space=pltpu.VMEM, limit=24, out_space=pltpu.VMEM, cost=0):
    vmem = pl.BlockSpec(memory_space=out_space)
    return pl.pallas_call(
        kernel,
        out_shape=out_shape,
        in_specs=[pl.BlockSpec(memory_space=space)] * len(args),
        out_specs=jax.tree.map(lambda _: vmem, out_shape),
        scratch_shapes=scratch,
        compiler_params=pltpu.CompilerParams(vmem_limit_bytes=limit * 1024 * 1024),
        cost_estimate=pl.CostEstimate(flops=cost, bytes_accessed=cost // 500, transcendentals=0) if cost else None,
        name=name,
    )(*args)


def per_device(sizes, latent, occupancy, carry_x, carry_y, w_in, w_down, w_mid, w_up, w_out):
    xs, ys, zs, _ = sizes
    shape = jax.ShapeDtypeStruct
    plane, row = shape((2, 16, 128), F32), shape((8, 128), F32)
    lines = pltpu.VMEM((16, 128), F32)
    net_scratch = [
        pltpu.VMEM((1024, 128), BF16),
        pltpu.VMEM((1024, 512), BF16),
        pltpu.VMEM((1536, 128), BF16),
    ]
    for step in range(STEPS):
        tall = 40 if step == 0 else 32
        net_out = (shape((1024, 128), BF16), shape((ys, tall, 128), F32), plane, plane, plane)
        if step == 0:
            args = (latent[0, 0], occupancy[0], carry_x[0], carry_y[0], w_in, w_down, w_mid, w_up, w_out.T)
            held = [pltpu.VMEM(a.shape, a.dtype) for a in args]
            pred, msg, west, south, north, aux, wide_in, wide_out = call(
                first_kernel,
                (*net_out, shape((24, 128), F32), shape((128, 512), BF16), shape((512, 128), BF16)),
                held + net_scratch + [pltpu.SemaphoreType.DMA((len(args),))],
                args,
                "net_first",
                pl.ANY,
                60,
            )
        else:
            pred, msg, west, south, north, factors_z = call(
                next_kernel,
                (*net_out, shape((zs, 128), F32)),
                net_scratch,
                (aux, *seam_ins, wide_in, w_down, w_mid, w_up, wide_out),
                "seams_net",
            )
        term = call(term_kernel, plane, [], (aux, south, north), "terms", cost=2 * 10**9)
        got = lax.all_to_all(msg, "y", 0, 0)
        group_out = (shape((2 * xs, 40, 128), F32), plane, row)
        if step == 0:
            msg, start, start_f, factors_y = call(
                group_kernel,
                (*group_out, shape((ys, 128), F32)),
                [lines, lines],
                (aux, got, west, term),
                "group",
            )
        else:
            msg, start, start_f = call(
                group_kernel, group_out, [lines, lines], (aux, got, factors_y, west, term), "group"
            )
        got = lax.all_to_all(msg, ("x", "core"), 0, 0)
        msg, *seam_ins = call(
            turn_kernel,
            (shape((zs, tall, 128), F32), plane, plane, plane, row),
            [lines],
            (aux, got, start, start_f, south, north),
            "turn",
        )
        got = lax.all_to_all(msg, "z", 0, 0)
        seam_ins = (pred, got, *seam_ins)
    out = call(
        last_kernel,
        shape((16, 64, 128), BF16),
        [pltpu.VMEM((64, 16, 128), F32), pltpu.VMEM((16, 64, 128), BF16), pltpu.SemaphoreType.DMA((4,))],
        (aux, *seam_ins, factors_z),
        "seams_last",
        out_space=pl.ANY,
    )
    return out[None, None]


def solution(mesh):
    columns, rows = mesh.shape["gx"], mesh.shape["gy"]
    inner = 8 if columns % 8 == 0 else 2
    sizes = (columns // inner, inner, rows // 2, 2)
    parts = jax.sharding.Mesh(mesh.devices.reshape(sizes), ("x", "y", "z", "core"))
    gx, gy = ("x", "y"), ("z", "core")
    in_specs = (
        P(gx, gy, None, None, None),
        P(gx, gy, None),
        P(gx, gy, None),
        P(gx, gy, None),
        P(),
        P(),
        P(),
        P(),
        P(),
    )
    return jax.shard_map(
        functools.partial(per_device, sizes),
        mesh=parts,
        in_specs=in_specs,
        out_specs=P(gx, gy, None, None, None),
        check_vma=False,
    )
```

```python
import functools

import jax
import jax.numpy as jnp
from jax import lax
from jax.experimental import pallas as pl
from jax.experimental.pallas import tpu as pltpu
from jax.sharding import PartitionSpec as P

STEPS = 2
F32 = jnp.float32
BF16 = jnp.bfloat16


def silu_of_half(half):
    return half + half * jnp.tanh(half)


def silu(v):
    return silu_of_half(0.5 * v)


def iotas(rows):
    sub = lax.broadcasted_iota(jnp.int32, (rows, 128), 0)
    lane = lax.broadcasted_iota(jnp.int32, (rows, 128), 1)
    return sub, lane


def turn_lanes(x, by):
    return pltpu.roll(x, by % 128, x.ndim - 1)


def turn_rows(x, by):
    by = by % x.shape[0]
    return x if by == 0 else pltpu.roll(x, by, 0)


def swap_sy(x, lane):
    return jnp.where((lane // 32) % 2 == 0, turn_lanes(x, -32), turn_lanes(x, 32))


def edge_gain(logs):
    return sum(jnp.exp((p + 0.5) / 32.0 * logs) for p in range(24, 32)) * 0.125


def gain_at(place, logs):
    return jnp.exp(place.astype(F32) / 32.0 * logs + (0.5 / 32.0) * logs)


def widen(narrow):
    row = jnp.concatenate([narrow.astype(F32)] * 8, axis=1)
    both = jnp.concatenate([row] * 8, axis=0)
    r = lax.broadcasted_iota(jnp.int32, both.shape, 0) // 16
    c = lax.broadcasted_iota(jnp.int32, both.shape, 1) // 64
    return jnp.where(r == c, both, 0.0)


def net(state, ready, weights, first_ref, second_ref, pred_ref, outs):
    wide_in, w_down, w_mid, w_up, wide_out = weights
    msg, west_ref, south_ref, north_ref = outs
    for qx in range(2):
        rows = pl.ds(512 * qx, 512)
        first = silu_of_half(jnp.dot(state[rows, :], wide_in[...], preferred_element_type=F32)).astype(BF16)
        first_ref[rows, :] = first
        pre = jnp.dot(first, w_down[...], preferred_element_type=F32)
        half = pre * (0.5 * lax.rsqrt(jnp.mean(pre * pre, axis=-1, keepdims=True) + 1e-06))
        second_ref[pl.ds(256 + 512 * qx, 512), :] = silu_of_half(half).astype(BF16)

    sub, lane = iotas(16)
    by, bx = sub % 4, sub // 4
    total_x = [[None] * 4 for _ in range(4)]
    south, north = [0.0] * 4, [0.0] * 4
    aux = ready()
    log_x, occupied, col = aux.log_x, aux.occupied, aux.col
    second_ref[pl.ds(0, 256), :] = jnp.zeros((256, 128), BF16)
    second_ref[pl.ds(1280, 256), :] = jnp.zeros((256, 128), BF16)
    mids = jnp.concatenate([0.5 * w_mid[k] for k in range(7)], axis=0)
    for group in range(2):
        base = 512 * group
        rows = pl.ds(base, 512)
        second = second_ref[pl.ds(base + 256, 512), :]
        parts = [second, second_ref[pl.ds(base, 512), :], second_ref[pl.ds(base + 512, 512), :]]
        gap = jnp.zeros((64, 128), BF16)
        gap16 = jnp.zeros((16, 128), BF16)
        left, right, below, above = [], [], [], []
        for plane in range(2):
            own = second[256 * plane : 256 * plane + 256]
            left += [gap, own[:192]]
            right += [own[64:], gap]
            for qy in range(4):
                o = own[64 * qy : 64 * qy + 64]
                below += [gap16, o[:48]]
                above += [o[16:], gap16]
        parts += [jnp.concatenate(p, axis=0) for p in (left, right, below, above)]
        stacked = jnp.concatenate(parts, axis=1)
        mixed = jnp.dot(stacked, mids, preferred_element_type=F32)
        middle = (second.astype(F32) + silu_of_half(mixed)).astype(BF16)
        upper = jnp.dot(middle, w_up[...], preferred_element_type=F32) + first_ref[rows, :].astype(F32)
        upper = silu(upper).astype(BF16)
        update = jnp.dot(upper, wide_out[...], preferred_element_type=F32)
        update = update.reshape(32, 16, 128) * occupied[None]
        preds = (state[rows, :].astype(F32).reshape(32, 16, 128) + update).astype(BF16)
        pred_ref[rows, :] = preds.reshape(512, 128)
        for plane in range(2):
            qx = 2 * group + plane
            pred = preds[16 * plane : 16 * plane + 16].astype(F32)
            for qy in range(4):
                for qz in range(4):
                    value = pred[4 * qy + qz]
                    total_x[qy][qz] = value if qx == 0 else total_x[qy][qz] + value
            for qz in range(4):
                s = pred[qz] + pred[4 + qz] + pred[8 + qz] + pred[12 + qz]
                s = (s + swap_sy(s, lane)) * 0.125
                south[qx] = south[qx] + jnp.where(by == qz, turn_rows(s, qz), 0.0)
                north[qx] = north[qx] + jnp.where(by == qz, turn_rows(s, qz - 3), 0.0)

    west, east = [0.0] * 4, [0.0] * 4
    for qy in range(4):
        for qz in range(4):
            s = total_x[qy][qz]
            s = (s + turn_lanes(s, 64)) * 0.125
            west[qy] = west[qy] + jnp.where(bx == qz, turn_rows(s, 4 * qz), 0.0)
            east[qy] = east[qy] + jnp.where(bx == qz, turn_rows(s, 4 * qz + 4), 0.0)
    low_sx, low_sy = lane < 64, (lane // 32) % 2 == 0
    factor = jnp.where(col == 0.0, 0.0, edge_gain(log_x))
    terms = []
    for h in range(2):
        w = jnp.where(low_sx, west[h], west[2 + h])
        terms.append(jnp.where(low_sx, east[h], east[2 + h]) - factor * w)
        west_ref[h] = w
        south_ref[h] = jnp.where(low_sy, south[h], south[2 + h])
        north_ref[h] = jnp.where(low_sy, north[h], north[2 + h])
    fill(msg, terms, [jnp.broadcast_to(factor, (8, 128))] if msg.shape[1] > 32 else [])


class Aux:
    def __init__(self, ref):
        self.log_x, self.log_y = ref[0:1, :], ref[1:2, :]
        self.col, self.x, self.y, self.row, self.z, self.core = (ref[k : k + 1, :] for k in range(2, 8))
        self.occupied = ref[8:24, :]


def halves(ref, k):
    return [ref[k, pl.ds(16 * h, 16), :] for h in range(2)]


def fill(msg, planes, rows=()):
    for k, value in enumerate([*planes, *rows]):
        size = 16 if k < 2 else 8
        at = 16 * k if k < 2 else 32 + 8 * (k - 2)
        msg[:, pl.ds(at, size), :] = jnp.broadcast_to(value[None], (msg.shape[0], size, 128))


def line_of(planes):
    sub, lane = iotas(16)
    value = planes[0] + planes[1]
    value = ((value + turn_lanes(value, 32)) + (turn_lanes(value, 64) + turn_lanes(value, 96))) * 0.125
    low, line = lane < 64, value
    for qz in range(4):
        line = jnp.where(low & (sub == qz), turn_rows(value, -3 * qz), line)
        line = jnp.where(~low & (sub == qz), turn_rows(value, -3 * qz - 3), line)
    return line[0:4]


def both_strips(line):
    low = iotas(4)[1] < 64
    other = turn_lanes(line, 64)
    return jnp.where(low, line, other), jnp.where(low, other, line)


def four(line):
    return jnp.concatenate([line] * 4, axis=0)


def place_y(sub, lane):
    return [8 * (sub // 4) + 2 * (2 * ((lane // 32) % 2) + h) + lane // 64 for h in range(2)]


def edge_y(aux):
    return jnp.where(aux.row == 0.0, 0.0, edge_gain(aux.log_y))


def group_kernel(aux_ref, got, *rest):
    if got.shape[1] > 32:
        west, south, north, msg, start_ref, start_f_ref, factor_ref = rest
        for k in range(got.shape[0]):
            factor_ref[k : k + 1, :] = got[k, 32:33, :]
    else:
        factor_ref, west, south, north, msg, start_ref, start_f_ref = rest
    aux = Aux(aux_ref)
    zero, one = [jnp.zeros((16, 128), F32)] * 2, jnp.ones((1, 128), F32)
    before, before_f, total, total_f = zero, one, zero, one
    for k in range(got.shape[0]):
        f, t, go = factor_ref[k : k + 1, :], halves(got, k), aux.y > k
        before = [jnp.where(go, f * before[h] + t[h], before[h]) for h in range(2)]
        before_f = jnp.where(go, f * before_f, before_f)
        total = [f * total[h] + t[h] for h in range(2)]
        total_f = f * total_f
    start = [before[h] - west[h] for h in range(2)]
    factor_y = edge_y(aux)
    term_y = [north[h] - factor_y * south[h] for h in range(2)]
    line_start, line_total = line_of(start), line_of(total)
    for h in range(2):
        start_ref[h] = start[h]
    start_f_ref[...] = jnp.broadcast_to(before_f, (8, 128))
    for x in range(msg.shape[0] // 2):
        mine = aux.x == x
        tail = [
            jnp.where(mine, line_start, line_total),
            jnp.where(mine, before_f, total_f),
            factor_y,
            aux.log_x,
            factor_y,
        ]
        tail = jnp.concatenate(tail, axis=0)
        for core in range(2):
            for h in range(2):
                msg[2 * x + core, pl.ds(16 * h, 16), :] = jnp.where(aux.core == core, total[h], term_y[h])
            msg[2 * x + core, 32:40, :] = tail


def turn_kernel(aux_ref, got, start_ref, start_f_ref, south, north, msg, drift_ref, low_ref, pair_ref, pair_f_ref):
    aux = Aux(aux_ref)
    first = aux.core == 0.0
    begin = [jnp.zeros((16, 128), F32)] * 2
    lines = [jnp.zeros((4, 128), F32)] * 2
    term, mine_tails = [0.0, 0.0], [0.0, 0.0]
    for x in range(got.shape[0] // 2):
        one, two = halves(got, 2 * x), halves(got, 2 * x + 1)
        tails = got[2 * x, 32:40, :], got[2 * x + 1, 32:40, :]
        tails = [jnp.where(first, *tails), jnp.where(first, *tails[::-1])]
        go, mine = aux.x > x, aux.x == x
        own = [jnp.where(first, one[h], two[h]) for h in range(2)]
        begin = [jnp.where(go, tails[0][4:5] * begin[h] + own[h], begin[h]) for h in range(2)]
        lines = [jnp.where(go, t[4:5] * line + t[0:4], line) for t, line in zip(tails, lines)]
        term = [jnp.where(mine, jnp.where(first, two[h], one[h]), term[h]) for h in range(2)]
        mine_tails = [jnp.where(mine, t, kept) for t, kept in zip(tails, mine_tails)]
    away = aux.col == 0.0
    lines = [jnp.where(away, 0.0, t[4:5] * line + t[0:4]) for t, line in zip(mine_tails, lines)]
    factor, other_factor = (t[5:6] for t in mine_tails)
    strips = [both_strips(line) for line in lines]
    south_line = four(strips[0][0])
    term_line = four(strips[0][1] - factor * strips[0][0])
    other_line = four(strips[1][1] - other_factor * strips[1][0])
    places = place_y(*iotas(16))
    pairs = []
    for h in range(2):
        gain = gain_at(places[h], aux.log_x)
        drift_ref[h] = jnp.where(away, 0.0, start_f_ref[0:1, :] * begin[h] + start_ref[h])
        low_ref[h] = south[h] + gain * south_line
        own = north[h] - factor * south[h] + gain * term_line
        other = term[h] + gain_at(places[h], mine_tails[1][6:7]) * other_line
        pair_ref[h] = jnp.where(first, 0.0, other)
        pairs.append(jnp.where(first, other_factor * own + other, factor * other + own))
    pair_f_ref[...] = jnp.broadcast_to(jnp.where(first, 1.0, other_factor), (8, 128))
    rows = [jnp.broadcast_to(factor * other_factor, (8, 128))] if msg.shape[1] > 32 else []
    fill(msg, pairs, rows)


def seams(aux, pred_ref, got, factors, drift_ref, low_ref, pair_ref, pair_f_ref, put):
    sub, lane = iotas(16)
    by, bx = sub % 4, sub // 4
    sx, sy = lane // 64, (lane // 32) % 2
    before = [jnp.zeros((16, 128), F32)] * 2
    for k in range(got.shape[0]):
        f, t, go = factors(k), halves(got, k), aux.z > k
        before = [jnp.where(go, f * before[h] + t[h], before[h]) for h in range(2)]
    before = [pair_f_ref[0:1, :] * before[h] + pair_ref[h] for h in range(2)]
    drift_y = [jnp.where(aux.row == 0.0, 0.0, before[h] - low_ref[h]) for h in range(2)]
    drift_x = [drift_ref[h] for h in range(2)]
    gain_x = [gain_at(8 * bx + 2 * q + sx, aux.log_x) for q in range(4)]
    gain_y = [gain_at(8 * by + 2 * q + sy, aux.log_y) for q in range(4)]
    spread_x = [[None] * 4 for _ in range(4)]
    spread_y = [[None] * 4 for _ in range(4)]
    for q in range(4):
        d = drift_x[q % 2]
        d = jnp.where(sx == q // 2, d, turn_lanes(d, 64))
        e = drift_y[q % 2]
        e = jnp.where(sy == q // 2, e, swap_sy(e, lane))
        for qz in range(4):
            m = d
            for k in range(4):
                m = jnp.where(bx == k, turn_rows(d, 4 * (k - qz)), m)
            spread_x[q][qz] = m
            m = e
            for k in range(4):
                m = jnp.where(by == k, turn_rows(e, k - qz), m)
            spread_y[q][qz] = m
    for qx in range(4):
        for qy in range(4):
            for qz in range(4):
                q = 16 * qx + 4 * qy + qz
                value = pred_ref[pl.ds(16 * q, 16), :].astype(F32)
                value = value + gain_x[qx] * spread_x[qy][qz] + gain_y[qy] * spread_y[qx][qz]
                put(q, value)


def first_kernel(latent, occupancy, carry_x, carry_y, w_in, w_down, w_mid, w_up, w_out, *rest):
    pred_ref, msg, west, south, north, aux_ref, wide_in, wide_out = rest[:8]
    latent_v, occupancy_v, carry_x_v, carry_y_v, w_in_v, w_down_v, w_mid_v, w_up_v, w_out_v = rest[8:17]
    state, first_ref, second_ref, sems = rest[17:]
    pairs = [
        (latent, latent_v),
        (w_in, w_in_v),
        (w_down, w_down_v),
        (w_mid, w_mid_v),
        (w_up, w_up_v),
        (w_out, w_out_v),
        (occupancy, occupancy_v),
        (carry_x, carry_x_v),
        (carry_y, carry_y_v),
    ]
    copies = [pltpu.make_async_copy(src, dst, sems.at[k]) for k, (src, dst) in enumerate(pairs)]
    for copy in copies:
        copy.start()
    x, y, z, core = (lax.axis_index(name) for name in ("x", "y", "z", "core"))
    columns = lax.axis_size("y")
    copies[0].wait()
    copies[1].wait()
    wide_in[...] = (0.5 * widen(w_in_v[...])).astype(BF16)
    turned = jnp.swapaxes(latent_v[...].astype(F32), 0, 1)
    state[...] = turned.reshape(1024, 128).astype(BF16)
    for copy in copies[2:]:
        copy.wait()

    def ready():
        wide_out[...] = widen(w_out_v[...]).T.astype(BF16)
        rates = jnp.concatenate([carry_x_v[...], carry_y_v[...]], axis=0)
        rates = jnp.concatenate([rates] * 8, axis=1)
        aux_ref[0:2, :] = jnp.log(rates)
        for k, place in enumerate((x * columns + y, x, y, 2 * z + core, z, core)):
            aux_ref[2 + k : 3 + k, :] = jnp.full((1, 128), place, jnp.int32).astype(F32)
        r, c = (lax.broadcasted_iota(jnp.int32, (16, 16), k) for k in (0, 1))
        occupied = jnp.where(r == c, occupancy_v[...].astype(F32), 0.0)
        aux_ref[8:24, :] = jnp.broadcast_to(jnp.sum(occupied, axis=1, keepdims=True), (16, 128))
        return Aux(aux_ref)

    weights = (wide_in, w_down_v, w_mid_v, w_up_v, wide_out)
    net(state, ready, weights, first_ref, second_ref, pred_ref, (msg, west, south, north))


def next_kernel(aux_ref, pred, got, drift, low, pair, pair_f, wide_in, w_down, w_mid, w_up, wide_out, *rest):
    outs, (factor_ref, state, first_ref, second_ref) = rest[:5], rest[5:]
    aux = Aux(aux_ref)
    for k in range(got.shape[0]):
        factor_ref[k : k + 1, :] = got[k, 32:33, :]

    def put(q, value):
        state[pl.ds(16 * q, 16), :] = value.astype(BF16)

    seams(aux, pred, got, lambda k: got[k, 32:33, :], drift, low, pair, pair_f, put)
    net(state, lambda: aux, (wide_in, w_down, w_mid, w_up, wide_out), first_ref, second_ref, outs[0], outs[1:])


def last_kernel(aux_ref, pred, got, drift, low, pair, pair_f, factor_ref, out, state, turned, sems):
    copies = []

    def put(q, value):
        state[q] = value
        if q % 16 == 15:
            rows = pl.ds(q - 15, 16)
            turned[:, rows, :] = jnp.swapaxes(state[rows], 0, 1).astype(BF16)
            copies.append(pltpu.make_async_copy(turned.at[:, rows, :], out.at[:, rows, :], sems.at[q // 16]))
            copies[-1].start()

    seams(Aux(aux_ref), pred, got, lambda k: factor_ref[k : k + 1, :], drift, low, pair, pair_f, put)
    for copy in copies:
        copy.wait()


def call(kernel, out_shape, scratch, args, name, space=pltpu.VMEM, limit=24, out_space=pltpu.VMEM):
    vmem = pl.BlockSpec(memory_space=out_space)
    return pl.pallas_call(
        kernel,
        out_shape=out_shape,
        in_specs=[pl.BlockSpec(memory_space=space)] * len(args),
        out_specs=jax.tree.map(lambda _: vmem, out_shape),
        scratch_shapes=scratch,
        compiler_params=pltpu.CompilerParams(vmem_limit_bytes=limit * 1024 * 1024),
        name=name,
    )(*args)


def per_device(sizes, latent, occupancy, carry_x, carry_y, w_in, w_down, w_mid, w_up, w_out):
    xs, ys, zs, _ = sizes
    shape = jax.ShapeDtypeStruct
    plane, row = shape((2, 16, 128), F32), shape((8, 128), F32)
    net_scratch = [
        pltpu.VMEM((1024, 128), BF16),
        pltpu.VMEM((1024, 512), BF16),
        pltpu.VMEM((1536, 128), BF16),
    ]
    for step in range(STEPS):
        tall = 40 if step == 0 else 32
        net_out = (shape((1024, 128), BF16), shape((ys, tall, 128), F32), plane, plane, plane)
        if step == 0:
            args = (latent[0, 0], occupancy[0], carry_x[0], carry_y[0], w_in, w_down, w_mid, w_up, w_out.T)
            held = [pltpu.VMEM(a.shape, a.dtype) for a in args]
            pred, msg, west, south, north, aux, wide_in, wide_out = call(
                first_kernel,
                (*net_out, shape((24, 128), F32), shape((128, 512), BF16), shape((512, 128), BF16)),
                held + net_scratch + [pltpu.SemaphoreType.DMA((len(args),))],
                args,
                "net_first",
                pl.ANY,
                60,
            )
        else:
            pred, msg, west, south, north, factors_z = call(
                next_kernel,
                (*net_out, shape((zs, 128), F32)),
                net_scratch,
                (aux, *seam_ins, wide_in, w_down, w_mid, w_up, wide_out),
                "seams_net",
            )
        got = lax.all_to_all(msg, "y", 0, 0)
        group_out = (shape((2 * xs, 40, 128), F32), plane, row)
        if step == 0:
            msg, start, start_f, factors_y = call(
                group_kernel,
                (*group_out, shape((ys, 128), F32)),
                [],
                (aux, got, west, south, north),
                "group",
            )
        else:
            msg, start, start_f = call(
                group_kernel, group_out, [], (aux, got, factors_y, west, south, north), "group"
            )
        got = lax.all_to_all(msg, ("x", "core"), 0, 0)
        msg, *seam_ins = call(
            turn_kernel,
            (shape((zs, tall, 128), F32), plane, plane, plane, row),
            [],
            (aux, got, start, start_f, south, north),
            "turn",
        )
        got = lax.all_to_all(msg, "z", 0, 0)
        seam_ins = (pred, got, *seam_ins)
    out = call(
        last_kernel,
        shape((16, 64, 128), BF16),
        [pltpu.VMEM((64, 16, 128), F32), pltpu.VMEM((16, 64, 128), BF16), pltpu.SemaphoreType.DMA((4,))],
        (aux, *seam_ins, factors_z),
        "seams_last",
        out_space=pl.ANY,
    )
    return out[None, None]


def solution(mesh):
    columns, rows = mesh.shape["gx"], mesh.shape["gy"]
    inner = 8 if columns % 8 == 0 else 2
    sizes = (columns // inner, inner, rows // 2, 2)
    parts = jax.sharding.Mesh(mesh.devices.reshape(sizes), ("x", "y", "z", "core"))
    gx, gy = ("x", "y"), ("z", "core")
    in_specs = (
        P(gx, gy, None, None, None),
        P(gx, gy, None),
        P(gx, gy, None),
        P(gx, gy, None),
        P(),
        P(),
        P(),
        P(),
        P(),
    )
    return jax.shard_map(
        functools.partial(per_device, sizes),
        mesh=parts,
        in_specs=in_specs,
        out_specs=P(gx, gy, None, None, None),
        check_vma=False,
    )
```

```python
import functools

import jax
import jax.numpy as jnp
from jax import lax
from jax.experimental import pallas as pl
from jax.experimental.pallas import tpu as pltpu
from jax.sharding import PartitionSpec as P

STEPS = 2
F32 = jnp.float32
BF16 = jnp.bfloat16


def silu_of_half(half):
    return half + half * jnp.tanh(half)


def silu(v):
    return silu_of_half(0.5 * v)


def iotas(rows):
    sub = lax.broadcasted_iota(jnp.int32, (rows, 128), 0)
    lane = lax.broadcasted_iota(jnp.int32, (rows, 128), 1)
    return sub, lane


def turn_lanes(x, by):
    return pltpu.roll(x, by % 128, x.ndim - 1)


def turn_rows(x, by):
    by = by % x.shape[0]
    return x if by == 0 else pltpu.roll(x, by, 0)


def swap_sy(x, lane):
    return jnp.where((lane // 32) % 2 == 0, turn_lanes(x, -32), turn_lanes(x, 32))


def edge_gain(logs):
    return sum(jnp.exp((p + 0.5) / 32.0 * logs) for p in range(24, 32)) * 0.125


def gain_at(place, logs):
    return jnp.exp(place.astype(F32) / 32.0 * logs + (0.5 / 32.0) * logs)


def widen(narrow):
    row = jnp.concatenate([narrow.astype(F32)] * 8, axis=1)
    both = jnp.concatenate([row] * 8, axis=0)
    r = lax.broadcasted_iota(jnp.int32, both.shape, 0) // 16
    c = lax.broadcasted_iota(jnp.int32, both.shape, 1) // 64
    return jnp.where(r == c, both, 0.0)


def net(state, ready, weights, first_ref, second_ref, pred_ref, outs):
    wide_in, w_down, w_mid, w_up, wide_out = weights
    msg, west_ref, south_ref, north_ref = outs
    sub, lane = iotas(16)
    by, bx = sub % 4, sub // 4
    total_x = [[None] * 4 for _ in range(4)]
    south, north = [0.0] * 4, [0.0] * 4
    aux = ready()
    log_x, occupied, col = aux.log_x, aux.occupied, aux.col
    second_ref[pl.ds(0, 256), :] = jnp.zeros((256, 128), BF16)
    second_ref[pl.ds(1280, 256), :] = jnp.zeros((256, 128), BF16)
    mids = jnp.concatenate([0.5 * w_mid[k] for k in range(7)], axis=0)
    firsts, middles, uppers = {}, {}, {}

    def lower(k, n):
        rows = pl.ds(n * k, n)
        first = silu_of_half(jnp.dot(state[rows, :], wide_in[...], preferred_element_type=F32)).astype(BF16)
        first_ref[rows, :] = first
        firsts[k] = first

    def down(k, n):
        pre = jnp.dot(firsts.pop(k), w_down[...], preferred_element_type=F32)
        half = pre * (0.5 * lax.rsqrt(jnp.mean(pre * pre, axis=-1, keepdims=True) + 1e-06))
        second_ref[pl.ds(256 + n * k, n), :] = silu_of_half(half).astype(BF16)

    def stencil(k, n):
        base = n * k
        second = second_ref[pl.ds(base + 256, n), :]
        parts = [second, second_ref[pl.ds(base, n), :], second_ref[pl.ds(base + 512, n), :]]
        gap = jnp.zeros((64, 128), BF16)
        gap16 = jnp.zeros((16, 128), BF16)
        left, right, below, above = [], [], [], []
        for plane in range(n // 256):
            own = second[256 * plane : 256 * plane + 256]
            left += [gap, own[:192]]
            right += [own[64:], gap]
            for qy in range(4):
                o = own[64 * qy : 64 * qy + 64]
                below += [gap16, o[:48]]
                above += [o[16:], gap16]
        parts += [jnp.concatenate(p, axis=0) for p in (left, right, below, above)]
        stacked = jnp.concatenate(parts, axis=1)
        mixed = jnp.dot(stacked, mids, preferred_element_type=F32)
        middles[k] = (second.astype(F32) + silu_of_half(mixed)).astype(BF16)

    def up(k, n):
        rows = pl.ds(n * k, n)
        upper = jnp.dot(middles.pop(k), w_up[...], preferred_element_type=F32) + first_ref[rows, :].astype(F32)
        uppers[k] = silu(upper).astype(BF16)

    def out(k, n):
        rows = pl.ds(n * k, n)
        update = jnp.dot(uppers.pop(k), wide_out[...], preferred_element_type=F32)
        update = update.reshape(n // 16, 16, 128) * occupied[None]
        preds = (state[rows, :].astype(F32).reshape(n // 16, 16, 128) + update).astype(BF16)
        pred_ref[rows, :] = preds.reshape(n, 128)
        for plane in range(n // 256):
            qx = n // 256 * k + plane
            pred = preds[16 * plane : 16 * plane + 16].astype(F32)
            for qy in range(4):
                for qz in range(4):
                    value = pred[4 * qy + qz]
                    total_x[qy][qz] = value if qx == 0 else total_x[qy][qz] + value
            for qz in range(4):
                s = pred[qz] + pred[4 + qz] + pred[8 + qz] + pred[12 + qz]
                s = (s + swap_sy(s, lane)) * 0.125
                south[qx] = south[qx] + jnp.where(by == qz, turn_rows(s, qz), 0.0)
                north[qx] = north[qx] + jnp.where(by == qz, turn_rows(s, qz - 3), 0.0)

    for k in range(4):
        lower(k, 256)
        if k > 0:
            down(k - 1, 256)
    down(3, 256)
    for k in range(2):
        stencil(k, 512)
    for k in range(2):
        up(k, 512)
        out(k, 512)

    west, east = [0.0] * 4, [0.0] * 4
    for qy in range(4):
        for qz in range(4):
            s = total_x[qy][qz]
            s = (s + turn_lanes(s, 64)) * 0.125
            west[qy] = west[qy] + jnp.where(bx == qz, turn_rows(s, 4 * qz), 0.0)
            east[qy] = east[qy] + jnp.where(bx == qz, turn_rows(s, 4 * qz + 4), 0.0)
    low_sx, low_sy = lane < 64, (lane // 32) % 2 == 0
    factor = jnp.where(col == 0.0, 0.0, edge_gain(log_x))
    terms = []
    for h in range(2):
        w = jnp.where(low_sx, west[h], west[2 + h])
        terms.append(jnp.where(low_sx, east[h], east[2 + h]) - factor * w)
        west_ref[h] = w
        south_ref[h] = jnp.where(low_sy, south[h], south[2 + h])
        north_ref[h] = jnp.where(low_sy, north[h], north[2 + h])
    fill(msg, terms, [jnp.broadcast_to(factor, (8, 128))] if msg.shape[1] > 32 else [])


class Aux:
    def __init__(self, ref):
        self.log_x, self.log_y = ref[0:1, :], ref[1:2, :]
        self.col, self.x, self.y, self.row, self.z, self.core = (ref[k : k + 1, :] for k in range(2, 8))
        self.occupied = ref[8:24, :]


def halves(ref, k):
    return [ref[k, pl.ds(16 * h, 16), :] for h in range(2)]


def fill(msg, planes, rows=()):
    for k, value in enumerate([*planes, *rows]):
        size = 16 if k < 2 else 8
        at = 16 * k if k < 2 else 32 + 8 * (k - 2)
        msg[:, pl.ds(at, size), :] = jnp.broadcast_to(value[None], (msg.shape[0], size, 128))


def line_of(planes):
    sub, lane = iotas(16)
    value = planes[0] + planes[1]
    value = ((value + turn_lanes(value, 32)) + (turn_lanes(value, 64) + turn_lanes(value, 96))) * 0.125
    low, line = lane < 64, value
    for qz in range(4):
        line = jnp.where(low & (sub == qz), turn_rows(value, -3 * qz), line)
        line = jnp.where(~low & (sub == qz), turn_rows(value, -3 * qz - 3), line)
    return line[0:4]


def both_strips(line):
    low = iotas(4)[1] < 64
    other = turn_lanes(line, 64)
    return jnp.where(low, line, other), jnp.where(low, other, line)


def four(line):
    return jnp.concatenate([line] * 4, axis=0)


def place_y(sub, lane):
    return [8 * (sub // 4) + 2 * (2 * ((lane // 32) % 2) + h) + lane // 64 for h in range(2)]


def edge_y(aux):
    return jnp.where(aux.row == 0.0, 0.0, edge_gain(aux.log_y))


def group_kernel(aux_ref, got, *rest):
    if got.shape[1] > 32:
        west, south, north, msg, start_ref, start_f_ref, factor_ref = rest
        for k in range(got.shape[0]):
            factor_ref[k : k + 1, :] = got[k, 32:33, :]
    else:
        factor_ref, west, south, north, msg, start_ref, start_f_ref = rest
    aux = Aux(aux_ref)
    zero, one = [jnp.zeros((16, 128), F32)] * 2, jnp.ones((1, 128), F32)
    before, before_f, total, total_f = zero, one, zero, one
    for k in range(got.shape[0]):
        f, t, go = factor_ref[k : k + 1, :], halves(got, k), aux.y > k
        before = [jnp.where(go, f * before[h] + t[h], before[h]) for h in range(2)]
        before_f = jnp.where(go, f * before_f, before_f)
        total = [f * total[h] + t[h] for h in range(2)]
        total_f = f * total_f
    start = [before[h] - west[h] for h in range(2)]
    factor_y = edge_y(aux)
    term_y = [north[h] - factor_y * south[h] for h in range(2)]
    line_start, line_total = line_of(start), line_of(total)
    for h in range(2):
        start_ref[h] = start[h]
    start_f_ref[...] = jnp.broadcast_to(before_f, (8, 128))
    for x in range(msg.shape[0] // 2):
        mine = aux.x == x
        tail = [
            jnp.where(mine, line_start, line_total),
            jnp.where(mine, before_f, total_f),
            factor_y,
            aux.log_x,
            factor_y,
        ]
        tail = jnp.concatenate(tail, axis=0)
        for core in range(2):
            for h in range(2):
                msg[2 * x + core, pl.ds(16 * h, 16), :] = jnp.where(aux.core == core, total[h], term_y[h])
            msg[2 * x + core, 32:40, :] = tail


def turn_kernel(aux_ref, got, start_ref, start_f_ref, south, north, msg, drift_ref, low_ref, pair_ref, pair_f_ref):
    aux = Aux(aux_ref)
    first = aux.core == 0.0
    begin = [jnp.zeros((16, 128), F32)] * 2
    lines = [jnp.zeros((4, 128), F32)] * 2
    term, mine_tails = [0.0, 0.0], [0.0, 0.0]
    for x in range(got.shape[0] // 2):
        one, two = halves(got, 2 * x), halves(got, 2 * x + 1)
        tails = got[2 * x, 32:40, :], got[2 * x + 1, 32:40, :]
        tails = [jnp.where(first, *tails), jnp.where(first, *tails[::-1])]
        go, mine = aux.x > x, aux.x == x
        own = [jnp.where(first, one[h], two[h]) for h in range(2)]
        begin = [jnp.where(go, tails[0][4:5] * begin[h] + own[h], begin[h]) for h in range(2)]
        lines = [jnp.where(go, t[4:5] * line + t[0:4], line) for t, line in zip(tails, lines)]
        term = [jnp.where(mine, jnp.where(first, two[h], one[h]), term[h]) for h in range(2)]
        mine_tails = [jnp.where(mine, t, kept) for t, kept in zip(tails, mine_tails)]
    away = aux.col == 0.0
    lines = [jnp.where(away, 0.0, t[4:5] * line + t[0:4]) for t, line in zip(mine_tails, lines)]
    factor, other_factor = (t[5:6] for t in mine_tails)
    strips = [both_strips(line) for line in lines]
    south_line = four(strips[0][0])
    term_line = four(strips[0][1] - factor * strips[0][0])
    other_line = four(strips[1][1] - other_factor * strips[1][0])
    places = place_y(*iotas(16))
    pairs = []
    for h in range(2):
        gain = gain_at(places[h], aux.log_x)
        drift_ref[h] = jnp.where(away, 0.0, start_f_ref[0:1, :] * begin[h] + start_ref[h])
        low_ref[h] = south[h] + gain * south_line
        own = north[h] - factor * south[h] + gain * term_line
        other = term[h] + gain_at(places[h], mine_tails[1][6:7]) * other_line
        pair_ref[h] = jnp.where(first, 0.0, other)
        pairs.append(jnp.where(first, other_factor * own + other, factor * other + own))
    pair_f_ref[...] = jnp.broadcast_to(jnp.where(first, 1.0, other_factor), (8, 128))
    rows = [jnp.broadcast_to(factor * other_factor, (8, 128))] if msg.shape[1] > 32 else []
    fill(msg, pairs, rows)


def seams(aux, pred_ref, got, factors, drift_ref, low_ref, pair_ref, pair_f_ref, put):
    sub, lane = iotas(16)
    by, bx = sub % 4, sub // 4
    sx, sy = lane // 64, (lane // 32) % 2
    before = [jnp.zeros((16, 128), F32)] * 2
    for k in range(got.shape[0]):
        f, t, go = factors(k), halves(got, k), aux.z > k
        before = [jnp.where(go, f * before[h] + t[h], before[h]) for h in range(2)]
    before = [pair_f_ref[0:1, :] * before[h] + pair_ref[h] for h in range(2)]
    drift_y = [jnp.where(aux.row == 0.0, 0.0, before[h] - low_ref[h]) for h in range(2)]
    drift_x = [drift_ref[h] for h in range(2)]
    gain_x = [gain_at(8 * bx + 2 * q + sx, aux.log_x) for q in range(4)]
    gain_y = [gain_at(8 * by + 2 * q + sy, aux.log_y) for q in range(4)]
    spread_x = [[None] * 4 for _ in range(4)]
    spread_y = [[None] * 4 for _ in range(4)]
    for q in range(4):
        d = drift_x[q % 2]
        d = jnp.where(sx == q // 2, d, turn_lanes(d, 64))
        e = drift_y[q % 2]
        e = jnp.where(sy == q // 2, e, swap_sy(e, lane))
        for qz in range(4):
            m = d
            for k in range(4):
                m = jnp.where(bx == k, turn_rows(d, 4 * (k - qz)), m)
            spread_x[q][qz] = m
            m = e
            for k in range(4):
                m = jnp.where(by == k, turn_rows(e, k - qz), m)
            spread_y[q][qz] = m
    for qx in range(4):
        for qy in range(4):
            for qz in range(4):
                q = 16 * qx + 4 * qy + qz
                value = pred_ref[pl.ds(16 * q, 16), :].astype(F32)
                value = value + gain_x[qx] * spread_x[qy][qz] + gain_y[qy] * spread_y[qx][qz]
                put(q, value)


def first_kernel(latent, occupancy, carry_x, carry_y, w_in, w_down, w_mid, w_up, w_out, *rest):
    pred_ref, msg, west, south, north, aux_ref, wide_in, wide_out = rest[:8]
    latent_v, occupancy_v, carry_x_v, carry_y_v, w_in_v, w_down_v, w_mid_v, w_up_v, w_out_v = rest[8:17]
    state, first_ref, second_ref, sems = rest[17:]
    pairs = [
        (latent, latent_v),
        (w_in, w_in_v),
        (w_down, w_down_v),
        (w_mid, w_mid_v),
        (w_up, w_up_v),
        (w_out, w_out_v),
        (occupancy, occupancy_v),
        (carry_x, carry_x_v),
        (carry_y, carry_y_v),
    ]
    copies = [pltpu.make_async_copy(src, dst, sems.at[k]) for k, (src, dst) in enumerate(pairs)]
    for copy in copies:
        copy.start()
    x, y, z, core = (lax.axis_index(name) for name in ("x", "y", "z", "core"))
    columns = lax.axis_size("y")
    copies[0].wait()
    copies[1].wait()
    wide_in[...] = (0.5 * widen(w_in_v[...])).astype(BF16)
    turned = jnp.swapaxes(latent_v[...].astype(F32), 0, 1)
    state[...] = turned.reshape(1024, 128).astype(BF16)
    for copy in copies[2:]:
        copy.wait()

    def ready():
        wide_out[...] = widen(w_out_v[...]).T.astype(BF16)
        rates = jnp.concatenate([carry_x_v[...], carry_y_v[...]], axis=0)
        rates = jnp.concatenate([rates] * 8, axis=1)
        aux_ref[0:2, :] = jnp.log(rates)
        for k, place in enumerate((x * columns + y, x, y, 2 * z + core, z, core)):
            aux_ref[2 + k : 3 + k, :] = jnp.full((1, 128), place, jnp.int32).astype(F32)
        r, c = (lax.broadcasted_iota(jnp.int32, (16, 16), k) for k in (0, 1))
        occupied = jnp.where(r == c, occupancy_v[...].astype(F32), 0.0)
        aux_ref[8:24, :] = jnp.broadcast_to(jnp.sum(occupied, axis=1, keepdims=True), (16, 128))
        return Aux(aux_ref)

    weights = (wide_in, w_down_v, w_mid_v, w_up_v, wide_out)
    net(state, ready, weights, first_ref, second_ref, pred_ref, (msg, west, south, north))


def next_kernel(aux_ref, pred, got, drift, low, pair, pair_f, wide_in, w_down, w_mid, w_up, wide_out, *rest):
    outs, (factor_ref, state, first_ref, second_ref) = rest[:5], rest[5:]
    aux = Aux(aux_ref)
    for k in range(got.shape[0]):
        factor_ref[k : k + 1, :] = got[k, 32:33, :]

    def put(q, value):
        state[pl.ds(16 * q, 16), :] = value.astype(BF16)

    seams(aux, pred, got, lambda k: got[k, 32:33, :], drift, low, pair, pair_f, put)
    net(state, lambda: aux, (wide_in, w_down, w_mid, w_up, wide_out), first_ref, second_ref, outs[0], outs[1:])


def last_kernel(aux_ref, pred, got, drift, low, pair, pair_f, factor_ref, out, state, turned, sems):
    copies = []

    def put(q, value):
        state[q] = value
        if q % 16 == 15:
            rows = pl.ds(q - 15, 16)
            turned[:, rows, :] = jnp.swapaxes(state[rows], 0, 1).astype(BF16)
            copies.append(pltpu.make_async_copy(turned.at[:, rows, :], out.at[:, rows, :], sems.at[q // 16]))
            copies[-1].start()

    seams(Aux(aux_ref), pred, got, lambda k: factor_ref[k : k + 1, :], drift, low, pair, pair_f, put)
    for copy in copies:
        copy.wait()


def call(kernel, out_shape, scratch, args, name, space=pltpu.VMEM, limit=24, out_space=pltpu.VMEM):
    vmem = pl.BlockSpec(memory_space=out_space)
    return pl.pallas_call(
        kernel,
        out_shape=out_shape,
        in_specs=[pl.BlockSpec(memory_space=space)] * len(args),
        out_specs=jax.tree.map(lambda _: vmem, out_shape),
        scratch_shapes=scratch,
        compiler_params=pltpu.CompilerParams(vmem_limit_bytes=limit * 1024 * 1024),
        name=name,
    )(*args)


def per_device(sizes, latent, occupancy, carry_x, carry_y, w_in, w_down, w_mid, w_up, w_out):
    xs, ys, zs, _ = sizes
    shape = jax.ShapeDtypeStruct
    plane, row = shape((2, 16, 128), F32), shape((8, 128), F32)
    net_scratch = [
        pltpu.VMEM((1024, 128), BF16),
        pltpu.VMEM((1024, 512), BF16),
        pltpu.VMEM((1536, 128), BF16),
    ]
    for step in range(STEPS):
        tall = 40 if step == 0 else 32
        net_out = (shape((1024, 128), BF16), shape((ys, tall, 128), F32), plane, plane, plane)
        if step == 0:
            args = (latent[0, 0], occupancy[0], carry_x[0], carry_y[0], w_in, w_down, w_mid, w_up, w_out.T)
            held = [pltpu.VMEM(a.shape, a.dtype) for a in args]
            pred, msg, west, south, north, aux, wide_in, wide_out = call(
                first_kernel,
                (*net_out, shape((24, 128), F32), shape((128, 512), BF16), shape((512, 128), BF16)),
                held + net_scratch + [pltpu.SemaphoreType.DMA((len(args),))],
                args,
                "net_first",
                pl.ANY,
                60,
            )
        else:
            pred, msg, west, south, north, factors_z = call(
                next_kernel,
                (*net_out, shape((zs, 128), F32)),
                net_scratch,
                (aux, *seam_ins, wide_in, w_down, w_mid, w_up, wide_out),
                "seams_net",
            )
        got = lax.all_to_all(msg, "y", 0, 0)
        group_out = (shape((2 * xs, 40, 128), F32), plane, row)
        if step == 0:
            msg, start, start_f, factors_y = call(
                group_kernel,
                (*group_out, shape((ys, 128), F32)),
                [],
                (aux, got, west, south, north),
                "group",
            )
        else:
            msg, start, start_f = call(
                group_kernel, group_out, [], (aux, got, factors_y, west, south, north), "group"
            )
        got = lax.all_to_all(msg, ("x", "core"), 0, 0)
        msg, *seam_ins = call(
            turn_kernel,
            (shape((zs, tall, 128), F32), plane, plane, plane, row),
            [],
            (aux, got, start, start_f, south, north),
            "turn",
        )
        got = lax.all_to_all(msg, "z", 0, 0)
        seam_ins = (pred, got, *seam_ins)
    out = call(
        last_kernel,
        shape((16, 64, 128), BF16),
        [pltpu.VMEM((64, 16, 128), F32), pltpu.VMEM((16, 64, 128), BF16), pltpu.SemaphoreType.DMA((4,))],
        (aux, *seam_ins, factors_z),
        "seams_last",
        out_space=pl.ANY,
    )
    return out[None, None]


def solution(mesh):
    columns, rows = mesh.shape["gx"], mesh.shape["gy"]
    inner = 8 if columns % 8 == 0 else 2
    sizes = (columns // inner, inner, rows // 2, 2)
    parts = jax.sharding.Mesh(mesh.devices.reshape(sizes), ("x", "y", "z", "core"))
    gx, gy = ("x", "y"), ("z", "core")
    in_specs = (
        P(gx, gy, None, None, None),
        P(gx, gy, None),
        P(gx, gy, None),
        P(gx, gy, None),
        P(),
        P(),
        P(),
        P(),
        P(),
    )
    return jax.shard_map(
        functools.partial(per_device, sizes),
        mesh=parts,
        in_specs=in_specs,
        out_specs=P(gx, gy, None, None, None),
        check_vma=False,
    )
```

```python
import functools

import jax
import jax.numpy as jnp
from jax import lax
from jax.experimental import pallas as pl
from jax.experimental.pallas import tpu as pltpu
from jax.sharding import PartitionSpec as P

STEPS = 2
F32 = jnp.float32
BF16 = jnp.bfloat16


def silu_of_half(half):
    return half + half * jnp.tanh(half)


def silu(v):
    return silu_of_half(0.5 * v)


def iotas(rows):
    sub = lax.broadcasted_iota(jnp.int32, (rows, 128), 0)
    lane = lax.broadcasted_iota(jnp.int32, (rows, 128), 1)
    return sub, lane


def turn_lanes(x, by):
    return pltpu.roll(x, by % 128, x.ndim - 1)


def turn_rows(x, by):
    by = by % x.shape[0]
    return x if by == 0 else pltpu.roll(x, by, 0)


def swap_sy(x, lane):
    return jnp.where((lane // 32) % 2 == 0, turn_lanes(x, -32), turn_lanes(x, 32))


def edge_gain(logs):
    return sum(jnp.exp((p + 0.5) / 32.0 * logs) for p in range(24, 32)) * 0.125


def gain_at(place, logs):
    return jnp.exp(place.astype(F32) / 32.0 * logs + (0.5 / 32.0) * logs)


def widen(narrow):
    row = jnp.concatenate([narrow.astype(F32)] * 8, axis=1)
    both = jnp.concatenate([row] * 8, axis=0)
    r = lax.broadcasted_iota(jnp.int32, both.shape, 0) // 16
    c = lax.broadcasted_iota(jnp.int32, both.shape, 1) // 64
    return jnp.where(r == c, both, 0.0)


def net(state, ready, weights, first_ref, second_ref, pred_ref, outs):
    wide_in, w_down, w_mid, w_up, wide_out = weights
    msg, west_ref, south_ref, north_ref = outs
    sub, lane = iotas(16)
    by, bx = sub % 4, sub // 4
    total_x = [[None] * 4 for _ in range(4)]
    south, north = [0.0] * 4, [0.0] * 4
    aux = ready()
    log_x, occupied, col = aux.log_x, aux.occupied, aux.col
    second_ref[pl.ds(0, 256), :] = jnp.zeros((256, 128), BF16)
    second_ref[pl.ds(1280, 256), :] = jnp.zeros((256, 128), BF16)
    mids = jnp.concatenate([0.5 * w_mid[k] for k in range(7)], axis=0)
    firsts, middles, uppers = {}, {}, {}

    def lower(k, n):
        rows = pl.ds(n * k, n)
        first = silu_of_half(jnp.dot(state[rows, :], wide_in[...], preferred_element_type=F32)).astype(BF16)
        first_ref[rows, :] = first
        firsts[k] = first

    def down(k, n):
        pre = jnp.dot(firsts.pop(k), w_down[...], preferred_element_type=F32)
        half = pre * (0.5 * lax.rsqrt(jnp.mean(pre * pre, axis=-1, keepdims=True) + 1e-06))
        second_ref[pl.ds(256 + n * k, n), :] = silu_of_half(half).astype(BF16)

    def stencil(k, n):
        base = n * k
        second = second_ref[pl.ds(base + 256, n), :]
        parts = [second, second_ref[pl.ds(base, n), :], second_ref[pl.ds(base + 512, n), :]]
        gap = jnp.zeros((64, 128), BF16)
        gap16 = jnp.zeros((16, 128), BF16)
        left, right, below, above = [], [], [], []
        for plane in range(n // 256):
            own = second[256 * plane : 256 * plane + 256]
            left += [gap, own[:192]]
            right += [own[64:], gap]
            for qy in range(4):
                o = own[64 * qy : 64 * qy + 64]
                below += [gap16, o[:48]]
                above += [o[16:], gap16]
        parts += [jnp.concatenate(p, axis=0) for p in (left, right, below, above)]
        stacked = jnp.concatenate(parts, axis=1)
        mixed = jnp.dot(stacked, mids, preferred_element_type=F32)
        middles[k] = (second.astype(F32) + silu_of_half(mixed)).astype(BF16)

    def up(k, n):
        rows = pl.ds(n * k, n)
        upper = jnp.dot(middles.pop(k), w_up[...], preferred_element_type=F32) + first_ref[rows, :].astype(F32)
        uppers[k] = silu(upper).astype(BF16)

    def out(k, n):
        rows = pl.ds(n * k, n)
        update = jnp.dot(uppers.pop(k), wide_out[...], preferred_element_type=F32)
        update = update.reshape(n // 16, 16, 128) * occupied[None]
        preds = (state[rows, :].astype(F32).reshape(n // 16, 16, 128) + update).astype(BF16)
        pred_ref[rows, :] = preds.reshape(n, 128)
        for plane in range(n // 256):
            qx = n // 256 * k + plane
            pred = preds[16 * plane : 16 * plane + 16].astype(F32)
            for qy in range(4):
                for qz in range(4):
                    value = pred[4 * qy + qz]
                    total_x[qy][qz] = value if qx == 0 else total_x[qy][qz] + value
            for qz in range(4):
                s = pred[qz] + pred[4 + qz] + pred[8 + qz] + pred[12 + qz]
                s = (s + swap_sy(s, lane)) * 0.125
                south[qx] = south[qx] + jnp.where(by == qz, turn_rows(s, qz), 0.0)
                north[qx] = north[qx] + jnp.where(by == qz, turn_rows(s, qz - 3), 0.0)

    for k in range(4):
        lower(k, 256)
        if k > 0:
            down(k - 1, 256)
    down(3, 256)
    for k in range(2):
        stencil(k, 512)
    for k in range(2):
        up(k, 512)
        out(k, 512)

    west, east = [0.0] * 4, [0.0] * 4
    for qy in range(4):
        for qz in range(4):
            s = total_x[qy][qz]
            s = (s + turn_lanes(s, 64)) * 0.125
            west[qy] = west[qy] + jnp.where(bx == qz, turn_rows(s, 4 * qz), 0.0)
            east[qy] = east[qy] + jnp.where(bx == qz, turn_rows(s, 4 * qz + 4), 0.0)
    low_sx, low_sy = lane < 64, (lane // 32) % 2 == 0
    factor = jnp.where(col == 0.0, 0.0, edge_gain(log_x))
    terms = []
    for h in range(2):
        w = jnp.where(low_sx, west[h], west[2 + h])
        terms.append(jnp.where(low_sx, east[h], east[2 + h]) - factor * w)
        west_ref[h] = w
        south_ref[h] = jnp.where(low_sy, south[h], south[2 + h])
        north_ref[h] = jnp.where(low_sy, north[h], north[2 + h])
    fill(msg, terms, [jnp.broadcast_to(factor, (8, 128))] if msg.shape[1] > 32 else [])


class Aux:
    def __init__(self, ref):
        self.log_x, self.log_y = ref[0:1, :], ref[1:2, :]
        self.col, self.x, self.y, self.row, self.z, self.core = (ref[k : k + 1, :] for k in range(2, 8))
        self.occupied = ref[8:24, :]


def halves(ref, k):
    return [ref[k, pl.ds(16 * h, 16), :] for h in range(2)]


def fill(msg, planes, rows=()):
    for k, value in enumerate([*planes, *rows]):
        size = 16 if k < 2 else 8
        at = 16 * k if k < 2 else 32 + 8 * (k - 2)
        msg[:, pl.ds(at, size), :] = jnp.broadcast_to(value[None], (msg.shape[0], size, 128))


def line_of(planes):
    sub, lane = iotas(16)
    value = planes[0] + planes[1]
    value = ((value + turn_lanes(value, 32)) + (turn_lanes(value, 64) + turn_lanes(value, 96))) * 0.125
    low, line = lane < 64, value
    for qz in range(4):
        line = jnp.where(low & (sub == qz), turn_rows(value, -3 * qz), line)
        line = jnp.where(~low & (sub == qz), turn_rows(value, -3 * qz - 3), line)
    return line[0:4]


def both_strips(line):
    low = iotas(4)[1] < 64
    other = turn_lanes(line, 64)
    return jnp.where(low, line, other), jnp.where(low, other, line)


def four(line):
    return jnp.concatenate([line] * 4, axis=0)


def place_y(sub, lane):
    return [8 * (sub // 4) + 2 * (2 * ((lane // 32) % 2) + h) + lane // 64 for h in range(2)]


def edge_y(aux):
    return jnp.where(aux.row == 0.0, 0.0, edge_gain(aux.log_y))


def group_kernel(aux_ref, got, *rest):
    if got.shape[1] > 32:
        west, south, north, msg, start_ref, start_f_ref, factor_ref = rest
        for k in range(got.shape[0]):
            factor_ref[k : k + 1, :] = got[k, 32:33, :]
    else:
        factor_ref, west, south, north, msg, start_ref, start_f_ref = rest
    aux = Aux(aux_ref)
    zero, one = [jnp.zeros((16, 128), F32)] * 2, jnp.ones((1, 128), F32)
    before, before_f, total, total_f = zero, one, zero, one
    for k in range(got.shape[0]):
        f, t, go = factor_ref[k : k + 1, :], halves(got, k), aux.y > k
        before = [jnp.where(go, f * before[h] + t[h], before[h]) for h in range(2)]
        before_f = jnp.where(go, f * before_f, before_f)
        total = [f * total[h] + t[h] for h in range(2)]
        total_f = f * total_f
    start = [before[h] - west[h] for h in range(2)]
    factor_y = edge_y(aux)
    term_y = [north[h] - factor_y * south[h] for h in range(2)]
    line_start, line_total = line_of(start), line_of(total)
    for h in range(2):
        start_ref[h] = start[h]
    start_f_ref[...] = jnp.broadcast_to(before_f, (8, 128))
    for x in range(msg.shape[0] // 2):
        mine = aux.x == x
        tail = [
            jnp.where(mine, line_start, line_total),
            jnp.where(mine, before_f, total_f),
            factor_y,
            aux.log_x,
            factor_y,
        ]
        tail = jnp.concatenate(tail, axis=0)
        for core in range(2):
            for h in range(2):
                msg[2 * x + core, pl.ds(16 * h, 16), :] = jnp.where(aux.core == core, total[h], term_y[h])
            msg[2 * x + core, 32:40, :] = tail


def turn_kernel(aux_ref, got, start_ref, start_f_ref, south, north, msg, drift_ref, low_ref, pair_ref, pair_f_ref):
    aux = Aux(aux_ref)
    first = aux.core == 0.0
    begin = [jnp.zeros((16, 128), F32)] * 2
    lines = [jnp.zeros((4, 128), F32)] * 2
    term, mine_tails = [0.0, 0.0], [0.0, 0.0]
    for x in range(got.shape[0] // 2):
        one, two = halves(got, 2 * x), halves(got, 2 * x + 1)
        tails = got[2 * x, 32:40, :], got[2 * x + 1, 32:40, :]
        tails = [jnp.where(first, *tails), jnp.where(first, *tails[::-1])]
        go, mine = aux.x > x, aux.x == x
        own = [jnp.where(first, one[h], two[h]) for h in range(2)]
        begin = [jnp.where(go, tails[0][4:5] * begin[h] + own[h], begin[h]) for h in range(2)]
        lines = [jnp.where(go, t[4:5] * line + t[0:4], line) for t, line in zip(tails, lines)]
        term = [jnp.where(mine, jnp.where(first, two[h], one[h]), term[h]) for h in range(2)]
        mine_tails = [jnp.where(mine, t, kept) for t, kept in zip(tails, mine_tails)]
    away = aux.col == 0.0
    lines = [jnp.where(away, 0.0, t[4:5] * line + t[0:4]) for t, line in zip(mine_tails, lines)]
    factor, other_factor = (t[5:6] for t in mine_tails)
    strips = [both_strips(line) for line in lines]
    south_line = four(strips[0][0])
    term_line = four(strips[0][1] - factor * strips[0][0])
    other_line = four(strips[1][1] - other_factor * strips[1][0])
    places = place_y(*iotas(16))
    pairs = []
    for h in range(2):
        gain = gain_at(places[h], aux.log_x)
        drift_ref[h] = jnp.where(away, 0.0, start_f_ref[0:1, :] * begin[h] + start_ref[h])
        low_ref[h] = south[h] + gain * south_line
        own = north[h] - factor * south[h] + gain * term_line
        other = term[h] + gain_at(places[h], mine_tails[1][6:7]) * other_line
        pair_ref[h] = jnp.where(first, 0.0, other)
        pairs.append(jnp.where(first, other_factor * own + other, factor * other + own))
    pair_f_ref[...] = jnp.broadcast_to(jnp.where(first, 1.0, other_factor), (8, 128))
    rows = [jnp.broadcast_to(factor * other_factor, (8, 128))] if msg.shape[1] > 32 else []
    fill(msg, pairs, rows)


def seams(aux, pred_ref, got, factors, drift_ref, low_ref, pair_ref, pair_f_ref, put):
    sub, lane = iotas(16)
    by, bx = sub % 4, sub // 4
    sx, sy = lane // 64, (lane // 32) % 2
    before = [jnp.zeros((16, 128), F32)] * 2
    for k in range(got.shape[0]):
        f, t, go = factors(k), halves(got, k), aux.z > k
        before = [jnp.where(go, f * before[h] + t[h], before[h]) for h in range(2)]
    before = [pair_f_ref[0:1, :] * before[h] + pair_ref[h] for h in range(2)]
    drift_y = [jnp.where(aux.row == 0.0, 0.0, before[h] - low_ref[h]) for h in range(2)]
    drift_x = [drift_ref[h] for h in range(2)]
    gain_x = [gain_at(8 * bx + 2 * q + sx, aux.log_x) for q in range(4)]
    gain_y = [gain_at(8 * by + 2 * q + sy, aux.log_y) for q in range(4)]
    spread_x = [[None] * 4 for _ in range(4)]
    spread_y = [[None] * 4 for _ in range(4)]
    for q in range(4):
        d = drift_x[q % 2]
        d = jnp.where(sx == q // 2, d, turn_lanes(d, 64))
        e = drift_y[q % 2]
        e = jnp.where(sy == q // 2, e, swap_sy(e, lane))
        for qz in range(4):
            m = d
            for k in range(4):
                m = jnp.where(bx == k, turn_rows(d, 4 * (k - qz)), m)
            spread_x[q][qz] = m
            m = e
            for k in range(4):
                m = jnp.where(by == k, turn_rows(e, k - qz), m)
            spread_y[q][qz] = m
    for qx in range(4):
        for qy in range(4):
            for qz in range(4):
                q = 16 * qx + 4 * qy + qz
                value = pred_ref[pl.ds(16 * q, 16), :].astype(F32)
                value = value + gain_x[qx] * spread_x[qy][qz] + gain_y[qy] * spread_y[qx][qz]
                put(q, value)


def first_kernel(latent, occupancy, carry_x, carry_y, w_in, w_down, w_mid, w_up, w_out, *rest):
    pred_ref, msg, west, south, north, aux_ref, wide_in, wide_out = rest[:8]
    latent_v, occupancy_v, carry_x_v, carry_y_v, w_in_v, w_down_v, w_mid_v, w_up_v, w_out_v = rest[8:17]
    state, first_ref, second_ref, sems = rest[17:]
    pairs = [
        (latent, latent_v),
        (w_in, w_in_v),
        (w_down, w_down_v),
        (w_mid, w_mid_v),
        (w_up, w_up_v),
        (w_out, w_out_v),
        (occupancy, occupancy_v),
        (carry_x, carry_x_v),
        (carry_y, carry_y_v),
    ]
    copies = [pltpu.make_async_copy(src, dst, sems.at[k]) for k, (src, dst) in enumerate(pairs)]
    for copy in copies:
        copy.start()
    x, y, z, core = (lax.axis_index(name) for name in ("x", "y", "z", "core"))
    columns = lax.axis_size("y")
    copies[0].wait()
    copies[1].wait()
    wide_in[...] = (0.5 * widen(w_in_v[...])).astype(BF16)
    turned = jnp.swapaxes(latent_v[...].astype(F32), 0, 1)
    state[...] = turned.reshape(1024, 128).astype(BF16)
    for copy in copies[2:]:
        copy.wait()

    def ready():
        wide_out[...] = widen(w_out_v[...]).T.astype(BF16)
        rates = jnp.concatenate([carry_x_v[...], carry_y_v[...]], axis=0)
        rates = jnp.concatenate([rates] * 8, axis=1)
        aux_ref[0:2, :] = jnp.log(rates)
        for k, place in enumerate((x * columns + y, x, y, 2 * z + core, z, core)):
            aux_ref[2 + k : 3 + k, :] = jnp.full((1, 128), place, jnp.int32).astype(F32)
        r, c = (lax.broadcasted_iota(jnp.int32, (16, 16), k) for k in (0, 1))
        occupied = jnp.where(r == c, occupancy_v[...].astype(F32), 0.0)
        aux_ref[8:24, :] = jnp.broadcast_to(jnp.sum(occupied, axis=1, keepdims=True), (16, 128))
        return Aux(aux_ref)

    weights = (wide_in, w_down_v, w_mid_v, w_up_v, wide_out)
    net(state, ready, weights, first_ref, second_ref, pred_ref, (msg, west, south, north))


def next_kernel(aux_ref, pred, got, drift, low, pair, pair_f, wide_in, w_down, w_mid, w_up, wide_out, *rest):
    outs, (factor_ref, state, first_ref, second_ref) = rest[:5], rest[5:]
    aux = Aux(aux_ref)
    for k in range(got.shape[0]):
        factor_ref[k : k + 1, :] = got[k, 32:33, :]

    def put(q, value):
        state[pl.ds(16 * q, 16), :] = value.astype(BF16)

    seams(aux, pred, got, lambda k: got[k, 32:33, :], drift, low, pair, pair_f, put)
    net(state, lambda: aux, (wide_in, w_down, w_mid, w_up, wide_out), first_ref, second_ref, outs[0], outs[1:])


def last_kernel(aux_ref, pred, got, drift, low, pair, pair_f, factor_ref, out, state, turned, sems):
    copies = []

    def put(q, value):
        state[q] = value
        if q % 16 == 15:
            rows = pl.ds(q - 15, 16)
            turned[:, rows, :] = jnp.swapaxes(state[rows], 0, 1).astype(BF16)
            copies.append(pltpu.make_async_copy(turned.at[:, rows, :], out.at[:, rows, :], sems.at[q // 16]))
            copies[-1].start()

    seams(Aux(aux_ref), pred, got, lambda k: factor_ref[k : k + 1, :], drift, low, pair, pair_f, put)
    for copy in copies:
        copy.wait()


def call(kernel, out_shape, scratch, args, name, space=pltpu.VMEM, limit=24, out_space=pltpu.VMEM):
    vmem = pl.BlockSpec(memory_space=out_space)
    return pl.pallas_call(
        kernel,
        out_shape=out_shape,
        in_specs=[pl.BlockSpec(memory_space=space)] * len(args),
        out_specs=jax.tree.map(lambda _: vmem, out_shape),
        scratch_shapes=scratch,
        compiler_params=pltpu.CompilerParams(vmem_limit_bytes=limit * 1024 * 1024),
        name=name,
    )(*args)


def per_device(sizes, latent, occupancy, carry_x, carry_y, w_in, w_down, w_mid, w_up, w_out):
    xs, ys, zs, _ = sizes
    shape = jax.ShapeDtypeStruct
    plane, row = shape((2, 16, 128), F32), shape((8, 128), F32)
    net_scratch = [
        pltpu.VMEM((1024, 128), BF16),
        pltpu.VMEM((1024, 512), BF16),
        pltpu.VMEM((1536, 128), BF16),
    ]
    for step in range(STEPS):
        tall = 40 if step == 0 else 32
        net_out = (shape((1024, 128), BF16), shape((ys, tall, 128), F32), plane, plane, plane)
        if step == 0:
            args = (latent[0, 0], occupancy[0], carry_x[0], carry_y[0], w_in, w_down, w_mid, w_up, w_out.T)
            held = [pltpu.VMEM(a.shape, a.dtype) for a in args]
            args = [pltpu.with_memory_space_constraint(a, pltpu.HBM) for a in args]
            pred, msg, west, south, north, aux, wide_in, wide_out = call(
                first_kernel,
                (*net_out, shape((24, 128), F32), shape((128, 512), BF16), shape((512, 128), BF16)),
                held + net_scratch + [pltpu.SemaphoreType.DMA((len(args),))],
                args,
                "net_first",
                pl.ANY,
            )
        else:
            pred, msg, west, south, north, factors_z = call(
                next_kernel,
                (*net_out, shape((zs, 128), F32)),
                net_scratch,
                (aux, *seam_ins, wide_in, w_down, w_mid, w_up, wide_out),
                "seams_net",
            )
        got = lax.all_to_all(msg, "y", 0, 0)
        group_out = (shape((2 * xs, 40, 128), F32), plane, row)
        if step == 0:
            msg, start, start_f, factors_y = call(
                group_kernel,
                (*group_out, shape((ys, 128), F32)),
                [],
                (aux, got, west, south, north),
                "group",
            )
        else:
            msg, start, start_f = call(
                group_kernel, group_out, [], (aux, got, factors_y, west, south, north), "group"
            )
        got = lax.all_to_all(msg, ("x", "core"), 0, 0)
        msg, *seam_ins = call(
            turn_kernel,
            (shape((zs, tall, 128), F32), plane, plane, plane, row),
            [],
            (aux, got, start, start_f, south, north),
            "turn",
        )
        got = lax.all_to_all(msg, "z", 0, 0)
        seam_ins = (pred, got, *seam_ins)
    out = call(
        last_kernel,
        shape((16, 64, 128), BF16),
        [pltpu.VMEM((64, 16, 128), F32), pltpu.VMEM((16, 64, 128), BF16), pltpu.SemaphoreType.DMA((4,))],
        (aux, *seam_ins, factors_z),
        "seams_last",
        out_space=pl.ANY,
    )
    return out[None, None]


def solution(mesh):
    columns, rows = mesh.shape["gx"], mesh.shape["gy"]
    inner = 8 if columns % 8 == 0 else 2
    sizes = (columns // inner, inner, rows // 2, 2)
    parts = jax.sharding.Mesh(mesh.devices.reshape(sizes), ("x", "y", "z", "core"))
    gx, gy = ("x", "y"), ("z", "core")
    in_specs = (
        P(gx, gy, None, None, None),
        P(gx, gy, None),
        P(gx, gy, None),
        P(gx, gy, None),
        P(),
        P(),
        P(),
        P(),
        P(),
    )
    return jax.shard_map(
        functools.partial(per_device, sizes),
        mesh=parts,
        in_specs=in_specs,
        out_specs=P(gx, gy, None, None, None),
        check_vma=False,
    )
```

```python
import functools

import jax
import jax.numpy as jnp
from jax import lax
from jax.experimental import pallas as pl
from jax.experimental.pallas import tpu as pltpu
from jax.sharding import PartitionSpec as P

STEPS = 2
F32 = jnp.float32
BF16 = jnp.bfloat16


def silu_of_half(half):
    return half + half * jnp.tanh(half)


def silu(v):
    return silu_of_half(0.5 * v)


def iotas(rows):
    sub = lax.broadcasted_iota(jnp.int32, (rows, 128), 0)
    lane = lax.broadcasted_iota(jnp.int32, (rows, 128), 1)
    return sub, lane


def turn_lanes(x, by):
    return pltpu.roll(x, by % 128, x.ndim - 1)


def turn_rows(x, by):
    by = by % x.shape[0]
    return x if by == 0 else pltpu.roll(x, by, 0)


def swap_sy(x, lane):
    return jnp.where((lane // 32) % 2 == 0, turn_lanes(x, -32), turn_lanes(x, 32))


def edge_gain(logs):
    return sum(jnp.exp((p + 0.5) / 32.0 * logs) for p in range(24, 32)) * 0.125


def gain_at(place, logs):
    return jnp.exp(place.astype(F32) / 32.0 * logs + (0.5 / 32.0) * logs)


def widen(narrow):
    row = jnp.concatenate([narrow.astype(F32)] * 8, axis=1)
    both = jnp.concatenate([row] * 8, axis=0)
    r = lax.broadcasted_iota(jnp.int32, both.shape, 0) // 16
    c = lax.broadcasted_iota(jnp.int32, both.shape, 1) // 64
    return jnp.where(r == c, both, 0.0)


def net(state, ready, weights, first_ref, second_ref, pred_ref, outs):
    wide_in, w_down, w_mid, w_up, wide_out = weights
    msg, west_ref, south_ref, north_ref = outs
    sub, lane = iotas(16)
    by, bx = sub % 4, sub // 4
    total_x = [[None] * 4 for _ in range(4)]
    south, north = [0.0] * 4, [0.0] * 4
    aux = ready()
    log_x, occupied, col = aux.log_x, aux.occupied, aux.col
    second_ref[pl.ds(0, 256), :] = jnp.zeros((256, 128), BF16)
    second_ref[pl.ds(1280, 256), :] = jnp.zeros((256, 128), BF16)
    mids = jnp.concatenate([0.5 * w_mid[k] for k in range(7)], axis=0)
    firsts, middles, uppers = {}, {}, {}

    def lower(k, n):
        rows = pl.ds(n * k, n)
        first = silu_of_half(jnp.dot(state[rows, :], wide_in[...], preferred_element_type=F32)).astype(BF16)
        first_ref[rows, :] = 0.5 * first
        firsts[k] = first

    def down(k, n):
        pre = jnp.dot(firsts.pop(k), w_down[...], preferred_element_type=F32)
        half = pre * (0.5 * lax.rsqrt(jnp.mean(pre * pre, axis=-1, keepdims=True) + 1e-06))
        second_ref[pl.ds(256 + n * k, n), :] = silu_of_half(half).astype(BF16)

    def stencil(k, n):
        base = n * k
        second = second_ref[pl.ds(base + 256, n), :]
        parts = [second, second_ref[pl.ds(base, n), :], second_ref[pl.ds(base + 512, n), :]]
        gap = jnp.zeros((64, 128), BF16)
        gap16 = jnp.zeros((16, 128), BF16)
        left, right, below, above = [], [], [], []
        for plane in range(n // 256):
            own = second[256 * plane : 256 * plane + 256]
            left += [gap, own[:192]]
            right += [own[64:], gap]
            for qy in range(4):
                o = own[64 * qy : 64 * qy + 64]
                below += [gap16, o[:48]]
                above += [o[16:], gap16]
        parts += [jnp.concatenate(p, axis=0) for p in (left, right, below, above)]
        stacked = jnp.concatenate(parts, axis=1)
        mixed = jnp.dot(stacked, mids, preferred_element_type=F32)
        middles[k] = (second.astype(F32) + silu_of_half(mixed)).astype(BF16)

    def up(k, n):
        rows = pl.ds(n * k, n)
        upper = jnp.dot(middles.pop(k), 0.5 * w_up[...], preferred_element_type=F32) + first_ref[rows, :].astype(F32)
        uppers[k] = silu_of_half(upper).astype(BF16)

    def out(k, n):
        rows = pl.ds(n * k, n)
        update = jnp.dot(uppers.pop(k), wide_out[...], preferred_element_type=F32)
        update = update.reshape(n // 16, 16, 128) * occupied[None]
        preds = (state[rows, :].astype(F32).reshape(n // 16, 16, 128) + update).astype(BF16)
        pred_ref[rows, :] = preds.reshape(n, 128)
        for plane in range(n // 256):
            qx = n // 256 * k + plane
            pred = preds[16 * plane : 16 * plane + 16].astype(F32)
            for qy in range(4):
                for qz in range(4):
                    value = pred[4 * qy + qz]
                    total_x[qy][qz] = value if qx == 0 else total_x[qy][qz] + value
            for qz in range(4):
                s = pred[qz] + pred[4 + qz] + pred[8 + qz] + pred[12 + qz]
                s = (s + swap_sy(s, lane)) * 0.125
                south[qx] = south[qx] + jnp.where(by == qz, turn_rows(s, qz), 0.0)
                north[qx] = north[qx] + jnp.where(by == qz, turn_rows(s, qz - 3), 0.0)

    lower(0, 256)
    lower(1, 256)
    for k in range(2, 4):
        lower(k, 256)
        down(k - 2, 256)
    down(2, 256)
    down(3, 256)
    for k in range(2):
        stencil(k, 512)
    for k in range(2):
        up(k, 512)
        out(k, 512)

    west, east = [0.0] * 4, [0.0] * 4
    for qy in range(4):
        for qz in range(4):
            s = total_x[qy][qz]
            s = (s + turn_lanes(s, 64)) * 0.125
            west[qy] = west[qy] + jnp.where(bx == qz, turn_rows(s, 4 * qz), 0.0)
            east[qy] = east[qy] + jnp.where(bx == qz, turn_rows(s, 4 * qz + 4), 0.0)
    low_sx, low_sy = lane < 64, (lane // 32) % 2 == 0
    factor = jnp.where(col == 0.0, 0.0, edge_gain(log_x))
    terms = []
    for h in range(2):
        w = jnp.where(low_sx, west[h], west[2 + h])
        terms.append(jnp.where(low_sx, east[h], east[2 + h]) - factor * w)
        west_ref[h] = w
        south_ref[h] = jnp.where(low_sy, south[h], south[2 + h])
        north_ref[h] = jnp.where(low_sy, north[h], north[2 + h])
    fill(msg, terms, [jnp.broadcast_to(factor, (8, 128))] if msg.shape[1] > 32 else [])


class Aux:
    def __init__(self, ref):
        self.log_x, self.log_y = ref[0:1, :], ref[1:2, :]
        self.col, self.x, self.y, self.row, self.z, self.core = (ref[k : k + 1, :] for k in range(2, 8))
        self.occupied = ref[8:24, :]


def halves(ref, k):
    return [ref[k, pl.ds(16 * h, 16), :] for h in range(2)]


def fill(msg, planes, rows=()):
    for k, value in enumerate([*planes, *rows]):
        size = 16 if k < 2 else 8
        at = 16 * k if k < 2 else 32 + 8 * (k - 2)
        msg[:, pl.ds(at, size), :] = jnp.broadcast_to(value[None], (msg.shape[0], size, 128))


def line_of(planes):
    sub, lane = iotas(16)
    value = planes[0] + planes[1]
    value = ((value + turn_lanes(value, 32)) + (turn_lanes(value, 64) + turn_lanes(value, 96))) * 0.125
    low, line = lane < 64, value
    for qz in range(4):
        line = jnp.where(low & (sub == qz), turn_rows(value, -3 * qz), line)
        line = jnp.where(~low & (sub == qz), turn_rows(value, -3 * qz - 3), line)
    return line[0:4]


def both_strips(line):
    low = iotas(4)[1] < 64
    other = turn_lanes(line, 64)
    return jnp.where(low, line, other), jnp.where(low, other, line)


def four(line):
    return jnp.concatenate([line] * 4, axis=0)


def place_y(sub, lane):
    return [8 * (sub // 4) + 2 * (2 * ((lane // 32) % 2) + h) + lane // 64 for h in range(2)]


def edge_y(aux):
    return jnp.where(aux.row == 0.0, 0.0, edge_gain(aux.log_y))


def group_kernel(aux_ref, got, *rest):
    if got.shape[1] > 32:
        west, south, north, msg, start_ref, start_f_ref, factor_ref = rest
        for k in range(got.shape[0]):
            factor_ref[k : k + 1, :] = got[k, 32:33, :]
    else:
        factor_ref, west, south, north, msg, start_ref, start_f_ref = rest
    aux = Aux(aux_ref)
    zero, one = [jnp.zeros((16, 128), F32)] * 2, jnp.ones((1, 128), F32)
    before, before_f, total, total_f = zero, one, zero, one
    for k in range(got.shape[0]):
        f, t, go = factor_ref[k : k + 1, :], halves(got, k), aux.y > k
        before = [jnp.where(go, f * before[h] + t[h], before[h]) for h in range(2)]
        before_f = jnp.where(go, f * before_f, before_f)
        total = [f * total[h] + t[h] for h in range(2)]
        total_f = f * total_f
    start = [before[h] - west[h] for h in range(2)]
    factor_y = edge_y(aux)
    term_y = [north[h] - factor_y * south[h] for h in range(2)]
    line_start, line_total = line_of(start), line_of(total)
    for h in range(2):
        start_ref[h] = start[h]
    start_f_ref[...] = jnp.broadcast_to(before_f, (8, 128))
    for x in range(msg.shape[0] // 2):
        mine = aux.x == x
        tail = [
            jnp.where(mine, line_start, line_total),
            jnp.where(mine, before_f, total_f),
            factor_y,
            aux.log_x,
            factor_y,
        ]
        tail = jnp.concatenate(tail, axis=0)
        for core in range(2):
            for h in range(2):
                msg[2 * x + core, pl.ds(16 * h, 16), :] = jnp.where(aux.core == core, total[h], term_y[h])
            msg[2 * x + core, 32:40, :] = tail


def turn_kernel(aux_ref, got, start_ref, start_f_ref, south, north, msg, drift_ref, low_ref, pair_ref, pair_f_ref):
    aux = Aux(aux_ref)
    first = aux.core == 0.0
    begin = [jnp.zeros((16, 128), F32)] * 2
    lines = [jnp.zeros((4, 128), F32)] * 2
    term, mine_tails = [0.0, 0.0], [0.0, 0.0]
    for x in range(got.shape[0] // 2):
        one, two = halves(got, 2 * x), halves(got, 2 * x + 1)
        tails = got[2 * x, 32:40, :], got[2 * x + 1, 32:40, :]
        tails = [jnp.where(first, *tails), jnp.where(first, *tails[::-1])]
        go, mine = aux.x > x, aux.x == x
        own = [jnp.where(first, one[h], two[h]) for h in range(2)]
        begin = [jnp.where(go, tails[0][4:5] * begin[h] + own[h], begin[h]) for h in range(2)]
        lines = [jnp.where(go, t[4:5] * line + t[0:4], line) for t, line in zip(tails, lines)]
        term = [jnp.where(mine, jnp.where(first, two[h], one[h]), term[h]) for h in range(2)]
        mine_tails = [jnp.where(mine, t, kept) for t, kept in zip(tails, mine_tails)]
    away = aux.col == 0.0
    lines = [jnp.where(away, 0.0, t[4:5] * line + t[0:4]) for t, line in zip(mine_tails, lines)]
    factor, other_factor = (t[5:6] for t in mine_tails)
    strips = [both_strips(line) for line in lines]
    south_line = four(strips[0][0])
    term_line = four(strips[0][1] - factor * strips[0][0])
    other_line = four(strips[1][1] - other_factor * strips[1][0])
    places = place_y(*iotas(16))
    pairs = []
    for h in range(2):
        gain = gain_at(places[h], aux.log_x)
        drift_ref[h] = jnp.where(away, 0.0, start_f_ref[0:1, :] * begin[h] + start_ref[h])
        low_ref[h] = south[h] + gain * south_line
        own = north[h] - factor * south[h] + gain * term_line
        other = term[h] + gain_at(places[h], mine_tails[1][6:7]) * other_line
        pair_ref[h] = jnp.where(first, 0.0, other)
        pairs.append(jnp.where(first, other_factor * own + other, factor * other + own))
    pair_f_ref[...] = jnp.broadcast_to(jnp.where(first, 1.0, other_factor), (8, 128))
    rows = [jnp.broadcast_to(factor * other_factor, (8, 128))] if msg.shape[1] > 32 else []
    fill(msg, pairs, rows)


def seams(aux, pred_ref, got, factors, drift_ref, low_ref, pair_ref, pair_f_ref, put):
    sub, lane = iotas(16)
    by, bx = sub % 4, sub // 4
    sx, sy = lane // 64, (lane // 32) % 2
    before = [jnp.zeros((16, 128), F32)] * 2
    for k in range(got.shape[0]):
        f, t, go = factors(k), halves(got, k), aux.z > k
        before = [jnp.where(go, f * before[h] + t[h], before[h]) for h in range(2)]
    before = [pair_f_ref[0:1, :] * before[h] + pair_ref[h] for h in range(2)]
    drift_y = [jnp.where(aux.row == 0.0, 0.0, before[h] - low_ref[h]) for h in range(2)]
    drift_x = [drift_ref[h] for h in range(2)]
    gain_x = [gain_at(8 * bx + 2 * q + sx, aux.log_x) for q in range(4)]
    gain_y = [gain_at(8 * by + 2 * q + sy, aux.log_y) for q in range(4)]
    spread_x = [[None] * 4 for _ in range(4)]
    spread_y = [[None] * 4 for _ in range(4)]
    for q in range(4):
        d = drift_x[q % 2]
        d = jnp.where(sx == q // 2, d, turn_lanes(d, 64))
        e = drift_y[q % 2]
        e = jnp.where(sy == q // 2, e, swap_sy(e, lane))
        for qz in range(4):
            m = d
            for k in range(4):
                m = jnp.where(bx == k, turn_rows(d, 4 * (k - qz)), m)
            spread_x[q][qz] = m
            m = e
            for k in range(4):
                m = jnp.where(by == k, turn_rows(e, k - qz), m)
            spread_y[q][qz] = m
    for qx in range(4):
        for qy in range(4):
            for qz in range(4):
                q = 16 * qx + 4 * qy + qz
                value = pred_ref[pl.ds(16 * q, 16), :].astype(F32)
                value = value + gain_x[qx] * spread_x[qy][qz] + gain_y[qy] * spread_y[qx][qz]
                put(q, value)


def first_kernel(latent, occupancy, carry_x, carry_y, w_in, w_down, w_mid, w_up, w_out, *rest):
    pred_ref, msg, west, south, north, aux_ref, wide_in, wide_out = rest[:8]
    latent_v, occupancy_v, carry_x_v, carry_y_v, w_in_v, w_down_v, w_mid_v, w_up_v, w_out_v = rest[8:17]
    state, first_ref, second_ref, sems = rest[17:]
    pairs = [
        (latent, latent_v),
        (w_in, w_in_v),
        (w_down, w_down_v),
        (w_mid, w_mid_v),
        (w_up, w_up_v),
        (w_out, w_out_v),
        (occupancy, occupancy_v),
        (carry_x, carry_x_v),
        (carry_y, carry_y_v),
    ]
    copies = [pltpu.make_async_copy(src, dst, sems.at[k]) for k, (src, dst) in enumerate(pairs)]
    for copy in copies:
        copy.start()
    x, y, z, core = (lax.axis_index(name) for name in ("x", "y", "z", "core"))
    columns = lax.axis_size("y")
    copies[0].wait()
    copies[1].wait()
    wide_in[...] = (0.5 * widen(w_in_v[...])).astype(BF16)
    turned = jnp.swapaxes(latent_v[...].astype(F32), 0, 1)
    state[...] = turned.reshape(1024, 128).astype(BF16)
    for copy in copies[2:]:
        copy.wait()

    def ready():
        wide_out[...] = widen(w_out_v[...]).T.astype(BF16)
        rates = jnp.concatenate([carry_x_v[...], carry_y_v[...]], axis=0)
        rates = jnp.concatenate([rates] * 8, axis=1)
        aux_ref[0:2, :] = jnp.log(rates)
        for k, place in enumerate((x * columns + y, x, y, 2 * z + core, z, core)):
            aux_ref[2 + k : 3 + k, :] = jnp.full((1, 128), place, jnp.int32).astype(F32)
        r, c = (lax.broadcasted_iota(jnp.int32, (16, 16), k) for k in (0, 1))
        occupied = jnp.where(r == c, occupancy_v[...].astype(F32), 0.0)
        aux_ref[8:24, :] = jnp.broadcast_to(jnp.sum(occupied, axis=1, keepdims=True), (16, 128))
        return Aux(aux_ref)

    weights = (wide_in, w_down_v, w_mid_v, w_up_v, wide_out)
    net(state, ready, weights, first_ref, second_ref, pred_ref, (msg, west, south, north))


def next_kernel(aux_ref, pred, got, drift, low, pair, pair_f, wide_in, w_down, w_mid, w_up, wide_out, *rest):
    outs, (factor_ref, state, first_ref, second_ref) = rest[:5], rest[5:]
    aux = Aux(aux_ref)
    for k in range(got.shape[0]):
        factor_ref[k : k + 1, :] = got[k, 32:33, :]

    def put(q, value):
        state[pl.ds(16 * q, 16), :] = value.astype(BF16)

    seams(aux, pred, got, lambda k: got[k, 32:33, :], drift, low, pair, pair_f, put)
    net(state, lambda: aux, (wide_in, w_down, w_mid, w_up, wide_out), first_ref, second_ref, outs[0], outs[1:])


def last_kernel(aux_ref, pred, got, drift, low, pair, pair_f, factor_ref, out, state, turned, sems):
    copies = []

    def put(q, value):
        state[q] = value
        if q % 16 == 15:
            rows = pl.ds(q - 15, 16)
            turned[:, rows, :] = jnp.swapaxes(state[rows], 0, 1).astype(BF16)
            copies.append(pltpu.make_async_copy(turned.at[:, rows, :], out.at[:, rows, :], sems.at[q // 16]))
            copies[-1].start()

    seams(Aux(aux_ref), pred, got, lambda k: factor_ref[k : k + 1, :], drift, low, pair, pair_f, put)
    for copy in copies:
        copy.wait()


def call(kernel, out_shape, scratch, args, name, space=pltpu.VMEM, limit=24, out_space=pltpu.VMEM):
    vmem = pl.BlockSpec(memory_space=out_space)
    return pl.pallas_call(
        kernel,
        out_shape=out_shape,
        in_specs=[pl.BlockSpec(memory_space=space)] * len(args),
        out_specs=jax.tree.map(lambda _: vmem, out_shape),
        scratch_shapes=scratch,
        compiler_params=pltpu.CompilerParams(vmem_limit_bytes=limit * 1024 * 1024),
        name=name,
    )(*args)


def per_device(sizes, latent, occupancy, carry_x, carry_y, w_in, w_down, w_mid, w_up, w_out):
    xs, ys, zs, _ = sizes
    shape = jax.ShapeDtypeStruct
    plane, row = shape((2, 16, 128), F32), shape((8, 128), F32)
    net_scratch = [
        pltpu.VMEM((1024, 128), BF16),
        pltpu.VMEM((1024, 512), BF16),
        pltpu.VMEM((1536, 128), BF16),
    ]
    for step in range(STEPS):
        tall = 40 if step == 0 else 32
        net_out = (shape((1024, 128), BF16), shape((ys, tall, 128), F32), plane, plane, plane)
        if step == 0:
            args = (latent[0, 0], occupancy[0], carry_x[0], carry_y[0], w_in, w_down, w_mid, w_up, w_out.T)
            held = [pltpu.VMEM(a.shape, a.dtype) for a in args]
            args = [pltpu.with_memory_space_constraint(a, pltpu.HBM) for a in args]
            pred, msg, west, south, north, aux, wide_in, wide_out = call(
                first_kernel,
                (*net_out, shape((24, 128), F32), shape((128, 512), BF16), shape((512, 128), BF16)),
                held + net_scratch + [pltpu.SemaphoreType.DMA((len(args),))],
                args,
                "net_first",
                pl.ANY,
            )
        else:
            pred, msg, west, south, north, factors_z = call(
                next_kernel,
                (*net_out, shape((zs, 128), F32)),
                net_scratch,
                (aux, *seam_ins, wide_in, w_down, w_mid, w_up, wide_out),
                "seams_net",
            )
        got = lax.all_to_all(msg, "y", 0, 0)
        group_out = (shape((2 * xs, 40, 128), F32), plane, row)
        if step == 0:
            msg, start, start_f, factors_y = call(
                group_kernel,
                (*group_out, shape((ys, 128), F32)),
                [],
                (aux, got, west, south, north),
                "group",
            )
        else:
            msg, start, start_f = call(
                group_kernel, group_out, [], (aux, got, factors_y, west, south, north), "group"
            )
        got = lax.all_to_all(msg, ("x", "core"), 0, 0)
        msg, *seam_ins = call(
            turn_kernel,
            (shape((zs, tall, 128), F32), plane, plane, plane, row),
            [],
            (aux, got, start, start_f, south, north),
            "turn",
        )
        got = lax.all_to_all(msg, "z", 0, 0)
        seam_ins = (pred, got, *seam_ins)
    out = call(
        last_kernel,
        shape((16, 64, 128), BF16),
        [pltpu.VMEM((64, 16, 128), F32), pltpu.VMEM((16, 64, 128), BF16), pltpu.SemaphoreType.DMA((4,))],
        (aux, *seam_ins, factors_z),
        "seams_last",
        out_space=pl.ANY,
    )
    return out[None, None]


def solution(mesh):
    columns, rows = mesh.shape["gx"], mesh.shape["gy"]
    inner = 8 if columns % 8 == 0 else 2
    sizes = (columns // inner, inner, rows // 2, 2)
    parts = jax.sharding.Mesh(mesh.devices.reshape(sizes), ("x", "y", "z", "core"))
    gx, gy = ("x", "y"), ("z", "core")
    in_specs = (
        P(gx, gy, None, None, None),
        P(gx, gy, None),
        P(gx, gy, None),
        P(gx, gy, None),
        P(),
        P(),
        P(),
        P(),
        P(),
    )
    return jax.shard_map(
        functools.partial(per_device, sizes),
        mesh=parts,
        in_specs=in_specs,
        out_specs=P(gx, gy, None, None, None),
        check_vma=False,
    )
```

```python
import functools

import jax
import jax.numpy as jnp
from jax import lax
from jax.experimental import pallas as pl
from jax.experimental.pallas import tpu as pltpu
from jax.sharding import PartitionSpec as P

STEPS = 2
F32 = jnp.float32
BF16 = jnp.bfloat16


def silu_of_half(half):
    return half + half * jnp.tanh(half)


def silu(v):
    return silu_of_half(0.5 * v)


def iotas(rows):
    sub = lax.broadcasted_iota(jnp.int32, (rows, 128), 0)
    lane = lax.broadcasted_iota(jnp.int32, (rows, 128), 1)
    return sub, lane


def turn_lanes(x, by):
    return pltpu.roll(x, by % 128, x.ndim - 1)


def turn_rows(x, by):
    by = by % x.shape[0]
    return x if by == 0 else pltpu.roll(x, by, 0)


def swap_sy(x, lane):
    return jnp.where((lane // 32) % 2 == 0, turn_lanes(x, -32), turn_lanes(x, 32))


def edge_gain(logs):
    return sum(jnp.exp((p + 0.5) / 32.0 * logs) for p in range(24, 32)) * 0.125


def gain_at(place, logs):
    return jnp.exp(place.astype(F32) / 32.0 * logs + (0.5 / 32.0) * logs)


def widen(narrow):
    row = jnp.concatenate([narrow.astype(F32)] * 8, axis=1)
    both = jnp.concatenate([row] * 8, axis=0)
    r = lax.broadcasted_iota(jnp.int32, both.shape, 0) // 16
    c = lax.broadcasted_iota(jnp.int32, both.shape, 1) // 64
    return jnp.where(r == c, both, 0.0)


def net(state, ready, weights, first_ref, second_ref, pred_ref, outs):
    wide_in, w_down, w_mid, w_up, wide_out = weights
    msg, west_ref, south_ref, north_ref = outs
    sub, lane = iotas(16)
    by, bx = sub % 4, sub // 4
    total_x = [[None] * 4 for _ in range(4)]
    south, north = [0.0] * 4, [0.0] * 4
    aux = ready()
    log_x, occupied, col = aux.log_x, aux.occupied, aux.col
    second_ref[pl.ds(0, 256), :] = jnp.zeros((256, 128), BF16)
    second_ref[pl.ds(1280, 256), :] = jnp.zeros((256, 128), BF16)
    mids = jnp.concatenate([0.5 * w_mid[k] for k in range(7)], axis=0)
    firsts, middles, uppers = {}, {}, {}

    def lower(k, n):
        rows = pl.ds(n * k, n)
        first = silu_of_half(jnp.dot(state[rows, :], wide_in[...], preferred_element_type=F32)).astype(BF16)
        first_ref[rows, :] = 0.5 * first
        firsts[k] = first

    def down(k, n):
        pre = jnp.dot(firsts.pop(k), w_down[...], preferred_element_type=F32)
        half = pre * (0.5 * lax.rsqrt(jnp.mean(pre * pre, axis=-1, keepdims=True) + 1e-06))
        second_ref[pl.ds(256 + n * k, n), :] = silu_of_half(half).astype(BF16)

    def stencil(k, n):
        base = n * k
        second = second_ref[pl.ds(base + 256, n), :]
        parts = [second, second_ref[pl.ds(base, n), :], second_ref[pl.ds(base + 512, n), :]]
        gap = jnp.zeros((64, 128), BF16)
        gap16 = jnp.zeros((16, 128), BF16)
        left, right, below, above = [], [], [], []
        for plane in range(n // 256):
            own = second[256 * plane : 256 * plane + 256]
            left += [gap, own[:192]]
            right += [own[64:], gap]
            for qy in range(4):
                o = own[64 * qy : 64 * qy + 64]
                below += [gap16, o[:48]]
                above += [o[16:], gap16]
        parts += [jnp.concatenate(p, axis=0) for p in (left, right, below, above)]
        stacked = jnp.concatenate(parts, axis=1)
        mixed = jnp.dot(stacked, mids, preferred_element_type=F32)
        middles[k] = (second.astype(F32) + silu_of_half(mixed)).astype(BF16)

    def up(k, n):
        rows = pl.ds(n * k, n)
        upper = jnp.dot(middles.pop(k), 0.5 * w_up[...], preferred_element_type=F32) + first_ref[rows, :].astype(F32)
        uppers[k] = silu_of_half(upper).astype(BF16)

    def out(k, n):
        rows = pl.ds(n * k, n)
        update = jnp.dot(uppers.pop(k), wide_out[...], preferred_element_type=F32)
        update = update.reshape(n // 16, 16, 128) * occupied[None]
        preds = (state[rows, :].astype(F32).reshape(n // 16, 16, 128) + update).astype(BF16)
        pred_ref[rows, :] = preds.reshape(n, 128)
        for plane in range(n // 256):
            qx = n // 256 * k + plane
            pred = preds[16 * plane : 16 * plane + 16].astype(F32)
            for qy in range(4):
                for qz in range(4):
                    value = pred[4 * qy + qz]
                    total_x[qy][qz] = value if qx == 0 else total_x[qy][qz] + value
            for qz in range(4):
                s = pred[qz] + pred[4 + qz] + pred[8 + qz] + pred[12 + qz]
                s = (s + swap_sy(s, lane)) * 0.125
                south[qx] = south[qx] + jnp.where(by == qz, turn_rows(s, qz), 0.0)
                north[qx] = north[qx] + jnp.where(by == qz, turn_rows(s, qz - 3), 0.0)

    lower(0, 256)
    lower(1, 256)
    for k in range(2, 4):
        lower(k, 256)
        down(k - 2, 256)
    down(2, 256)
    down(3, 256)
    for k in range(2):
        stencil(k, 512)
    for k in range(2):
        up(k, 512)
        out(k, 512)

    west, east = [0.0] * 4, [0.0] * 4
    for qy in range(4):
        for qz in range(4):
            s = total_x[qy][qz]
            s = (s + turn_lanes(s, 64)) * 0.125
            west[qy] = west[qy] + jnp.where(bx == qz, turn_rows(s, 4 * qz), 0.0)
            east[qy] = east[qy] + jnp.where(bx == qz, turn_rows(s, 4 * qz + 4), 0.0)
    low_sx, low_sy = lane < 64, (lane // 32) % 2 == 0
    factor = jnp.where(col == 0.0, 0.0, edge_gain(log_x))
    terms = []
    for h in range(2):
        w = jnp.where(low_sx, west[h], west[2 + h])
        terms.append(jnp.where(low_sx, east[h], east[2 + h]) - factor * w)
        west_ref[h] = w
        south_ref[h] = jnp.where(low_sy, south[h], south[2 + h])
        north_ref[h] = jnp.where(low_sy, north[h], north[2 + h])
    fill(msg, terms, factor)


class Aux:
    def __init__(self, ref):
        self.log_x, self.log_y = ref[0:1, :], ref[1:2, :]
        self.col, self.x, self.y, self.row, self.z, self.core = (ref[k : k + 1, :] for k in range(2, 8))
        self.occupied = ref[8:24, :]


def has_factor(ref):
    return len(ref.shape) == 4


def halves(ref, k):
    if has_factor(ref):
        return [ref[k, pl.ds(4 * h, 4)].reshape(16, 128) for h in range(2)]
    return [ref[k, pl.ds(16 * h, 16), :] for h in range(2)]


def fill(msg, planes, factor):
    n = msg.shape[0]
    for h, value in enumerate(planes):
        if has_factor(msg):
            msg[:, pl.ds(4 * h, 4)] = jnp.broadcast_to(value.reshape(1, 4, 4, 128), (n, 4, 4, 128))
        else:
            msg[:, pl.ds(16 * h, 16), :] = jnp.broadcast_to(value[None], (n, 16, 128))
    if has_factor(msg):
        msg[:, 8] = jnp.broadcast_to(factor[None], (n, 4, 128))


def line_of(planes):
    sub, lane = iotas(16)
    value = planes[0] + planes[1]
    value = ((value + turn_lanes(value, 32)) + (turn_lanes(value, 64) + turn_lanes(value, 96))) * 0.125
    low, line = lane < 64, value
    for qz in range(4):
        line = jnp.where(low & (sub == qz), turn_rows(value, -3 * qz), line)
        line = jnp.where(~low & (sub == qz), turn_rows(value, -3 * qz - 3), line)
    return line[0:4]


def both_strips(line):
    low = iotas(4)[1] < 64
    other = turn_lanes(line, 64)
    return jnp.where(low, line, other), jnp.where(low, other, line)


def four(line):
    return jnp.concatenate([line] * 4, axis=0)


def place_y(sub, lane):
    return [8 * (sub // 4) + 2 * (2 * ((lane // 32) % 2) + h) + lane // 64 for h in range(2)]


def edge_y(aux):
    return jnp.where(aux.row == 0.0, 0.0, edge_gain(aux.log_y))


def group_kernel(aux_ref, got, *rest):
    if has_factor(got):
        west, south, north, msg, start_ref, start_f_ref, factor_ref = rest
        for k in range(got.shape[0]):
            factor_ref[k : k + 1, :] = got[k, 8, 0:1, :]
    else:
        factor_ref, west, south, north, msg, start_ref, start_f_ref = rest
    aux = Aux(aux_ref)
    zero, one = [jnp.zeros((16, 128), F32)] * 2, jnp.ones((1, 128), F32)
    before, before_f, total, total_f = zero, one, zero, one
    for k in range(got.shape[0]):
        f, t, go = factor_ref[k : k + 1, :], halves(got, k), aux.y > k
        before = [jnp.where(go, f * before[h] + t[h], before[h]) for h in range(2)]
        before_f = jnp.where(go, f * before_f, before_f)
        total = [f * total[h] + t[h] for h in range(2)]
        total_f = f * total_f
    start = [before[h] - west[h] for h in range(2)]
    factor_y = edge_y(aux)
    term_y = [north[h] - factor_y * south[h] for h in range(2)]
    line_start, line_total = line_of(start), line_of(total)
    for h in range(2):
        start_ref[h] = start[h]
    start_f_ref[...] = jnp.broadcast_to(before_f, (8, 128))
    for x in range(msg.shape[0] // 2):
        mine = aux.x == x
        tail = [
            jnp.where(mine, line_start, line_total),
            jnp.where(mine, before_f, total_f),
            factor_y,
            aux.log_x,
            factor_y,
        ]
        tail = jnp.concatenate(tail, axis=0)
        for core in range(2):
            for h in range(2):
                msg[2 * x + core, pl.ds(16 * h, 16), :] = jnp.where(aux.core == core, total[h], term_y[h])
            msg[2 * x + core, 32:40, :] = tail


def turn_kernel(aux_ref, got, start_ref, start_f_ref, south, north, msg, drift_ref, low_ref, pair_ref, pair_f_ref):
    aux = Aux(aux_ref)
    first = aux.core == 0.0
    begin = [jnp.zeros((16, 128), F32)] * 2
    lines = [jnp.zeros((4, 128), F32)] * 2
    term, mine_tails = [0.0, 0.0], [0.0, 0.0]
    for x in range(got.shape[0] // 2):
        one, two = halves(got, 2 * x), halves(got, 2 * x + 1)
        tails = got[2 * x, 32:40, :], got[2 * x + 1, 32:40, :]
        tails = [jnp.where(first, *tails), jnp.where(first, *tails[::-1])]
        go, mine = aux.x > x, aux.x == x
        own = [jnp.where(first, one[h], two[h]) for h in range(2)]
        begin = [jnp.where(go, tails[0][4:5] * begin[h] + own[h], begin[h]) for h in range(2)]
        lines = [jnp.where(go, t[4:5] * line + t[0:4], line) for t, line in zip(tails, lines)]
        term = [jnp.where(mine, jnp.where(first, two[h], one[h]), term[h]) for h in range(2)]
        mine_tails = [jnp.where(mine, t, kept) for t, kept in zip(tails, mine_tails)]
    away = aux.col == 0.0
    lines = [jnp.where(away, 0.0, t[4:5] * line + t[0:4]) for t, line in zip(mine_tails, lines)]
    factor, other_factor = (t[5:6] for t in mine_tails)
    strips = [both_strips(line) for line in lines]
    south_line = four(strips[0][0])
    term_line = four(strips[0][1] - factor * strips[0][0])
    other_line = four(strips[1][1] - other_factor * strips[1][0])
    places = place_y(*iotas(16))
    pairs = []
    for h in range(2):
        gain = gain_at(places[h], aux.log_x)
        drift_ref[h] = jnp.where(away, 0.0, start_f_ref[0:1, :] * begin[h] + start_ref[h])
        low_ref[h] = south[h] + gain * south_line
        own = north[h] - factor * south[h] + gain * term_line
        other = term[h] + gain_at(places[h], mine_tails[1][6:7]) * other_line
        pair_ref[h] = jnp.where(first, 0.0, other)
        pairs.append(jnp.where(first, other_factor * own + other, factor * other + own))
    pair_f_ref[...] = jnp.broadcast_to(jnp.where(first, 1.0, other_factor), (8, 128))
    fill(msg, pairs, factor * other_factor)


def seams(aux, pred_ref, got, factors, drift_ref, low_ref, pair_ref, pair_f_ref, put):
    sub, lane = iotas(16)
    by, bx = sub % 4, sub // 4
    sx, sy = lane // 64, (lane // 32) % 2
    before = [jnp.zeros((16, 128), F32)] * 2
    for k in range(got.shape[0]):
        f, t, go = factors(k), halves(got, k), aux.z > k
        before = [jnp.where(go, f * before[h] + t[h], before[h]) for h in range(2)]
    before = [pair_f_ref[0:1, :] * before[h] + pair_ref[h] for h in range(2)]
    drift_y = [jnp.where(aux.row == 0.0, 0.0, before[h] - low_ref[h]) for h in range(2)]
    drift_x = [drift_ref[h] for h in range(2)]
    gain_x = [gain_at(8 * bx + 2 * q + sx, aux.log_x) for q in range(4)]
    gain_y = [gain_at(8 * by + 2 * q + sy, aux.log_y) for q in range(4)]
    spread_x = [[None] * 4 for _ in range(4)]
    spread_y = [[None] * 4 for _ in range(4)]
    for q in range(4):
        d = drift_x[q % 2]
        d = jnp.where(sx == q // 2, d, turn_lanes(d, 64))
        e = drift_y[q % 2]
        e = jnp.where(sy == q // 2, e, swap_sy(e, lane))
        for qz in range(4):
            m = d
            for k in range(4):
                m = jnp.where(bx == k, turn_rows(d, 4 * (k - qz)), m)
            spread_x[q][qz] = m
            m = e
            for k in range(4):
                m = jnp.where(by == k, turn_rows(e, k - qz), m)
            spread_y[q][qz] = m
    for qx in range(4):
        for qy in range(4):
            for qz in range(4):
                q = 16 * qx + 4 * qy + qz
                value = pred_ref[pl.ds(16 * q, 16), :].astype(F32)
                value = value + gain_x[qx] * spread_x[qy][qz] + gain_y[qy] * spread_y[qx][qz]
                put(q, value)


def first_kernel(latent, occupancy, carry_x, carry_y, w_in, w_down, w_mid, w_up, w_out, *rest):
    pred_ref, msg, west, south, north, aux_ref, wide_in, wide_out = rest[:8]
    latent_v, occupancy_v, carry_x_v, carry_y_v, w_in_v, w_down_v, w_mid_v, w_up_v, w_out_v = rest[8:17]
    state, first_ref, second_ref, sems = rest[17:]
    pairs = [
        (latent, latent_v),
        (w_in, w_in_v),
        (w_down, w_down_v),
        (w_mid, w_mid_v),
        (w_up, w_up_v),
        (w_out, w_out_v),
        (occupancy, occupancy_v),
        (carry_x, carry_x_v),
        (carry_y, carry_y_v),
    ]
    copies = [pltpu.make_async_copy(src, dst, sems.at[k]) for k, (src, dst) in enumerate(pairs)]
    for copy in copies:
        copy.start()
    x, y, z, core = (lax.axis_index(name) for name in ("x", "y", "z", "core"))
    columns = lax.axis_size("y")
    copies[0].wait()
    copies[1].wait()
    wide_in[...] = (0.5 * widen(w_in_v[...])).astype(BF16)
    turned = jnp.swapaxes(latent_v[...].astype(F32), 0, 1)
    state[...] = turned.reshape(1024, 128).astype(BF16)
    for copy in copies[2:]:
        copy.wait()

    def ready():
        wide_out[...] = widen(w_out_v[...]).T.astype(BF16)
        rates = jnp.concatenate([carry_x_v[...], carry_y_v[...]], axis=0)
        rates = jnp.concatenate([rates] * 8, axis=1)
        aux_ref[0:2, :] = jnp.log(rates)
        for k, place in enumerate((x * columns + y, x, y, 2 * z + core, z, core)):
            aux_ref[2 + k : 3 + k, :] = jnp.full((1, 128), place, jnp.int32).astype(F32)
        r, c = (lax.broadcasted_iota(jnp.int32, (16, 16), k) for k in (0, 1))
        occupied = jnp.where(r == c, occupancy_v[...].astype(F32), 0.0)
        aux_ref[8:24, :] = jnp.broadcast_to(jnp.sum(occupied, axis=1, keepdims=True), (16, 128))
        return Aux(aux_ref)

    weights = (wide_in, w_down_v, w_mid_v, w_up_v, wide_out)
    net(state, ready, weights, first_ref, second_ref, pred_ref, (msg, west, south, north))


def next_kernel(aux_ref, pred, got, drift, low, pair, pair_f, wide_in, w_down, w_mid, w_up, wide_out, *rest):
    outs, (factor_ref, state, first_ref, second_ref) = rest[:5], rest[5:]
    aux = Aux(aux_ref)
    for k in range(got.shape[0]):
        factor_ref[k : k + 1, :] = got[k, 8, 0:1, :]

    def put(q, value):
        state[pl.ds(16 * q, 16), :] = value.astype(BF16)

    seams(aux, pred, got, lambda k: got[k, 8, 0:1, :], drift, low, pair, pair_f, put)
    net(state, lambda: aux, (wide_in, w_down, w_mid, w_up, wide_out), first_ref, second_ref, outs[0], outs[1:])


def last_kernel(aux_ref, pred, got, drift, low, pair, pair_f, factor_ref, out, state, turned, sems):
    copies = []

    def put(q, value):
        state[q] = value
        if q % 16 == 15:
            rows = pl.ds(q - 15, 16)
            turned[:, rows, :] = jnp.swapaxes(state[rows], 0, 1).astype(BF16)
            copies.append(pltpu.make_async_copy(turned.at[:, rows, :], out.at[:, rows, :], sems.at[q // 16]))
            copies[-1].start()

    seams(Aux(aux_ref), pred, got, lambda k: factor_ref[k : k + 1, :], drift, low, pair, pair_f, put)
    for copy in copies:
        copy.wait()


def call(kernel, out_shape, scratch, args, name, space=pltpu.VMEM, limit=24, out_space=pltpu.VMEM):
    vmem = pl.BlockSpec(memory_space=out_space)
    return pl.pallas_call(
        kernel,
        out_shape=out_shape,
        in_specs=[pl.BlockSpec(memory_space=space)] * len(args),
        out_specs=jax.tree.map(lambda _: vmem, out_shape),
        scratch_shapes=scratch,
        compiler_params=pltpu.CompilerParams(vmem_limit_bytes=limit * 1024 * 1024),
        name=name,
    )(*args)


def per_device(sizes, latent, occupancy, carry_x, carry_y, w_in, w_down, w_mid, w_up, w_out):
    xs, ys, zs, _ = sizes
    shape = jax.ShapeDtypeStruct
    plane, row = shape((2, 16, 128), F32), shape((8, 128), F32)
    net_scratch = [
        pltpu.VMEM((1024, 128), BF16),
        pltpu.VMEM((1024, 512), BF16),
        pltpu.VMEM((1536, 128), BF16),
    ]
    for step in range(STEPS):
        message = (9, 4, 128) if step == 0 else (32, 128)
        net_out = (shape((1024, 128), BF16), shape((ys, *message), F32), plane, plane, plane)
        if step == 0:
            args = (latent[0, 0], occupancy[0], carry_x[0], carry_y[0], w_in, w_down, w_mid, w_up, w_out.T)
            held = [pltpu.VMEM(a.shape, a.dtype) for a in args]
            args = [pltpu.with_memory_space_constraint(a, pltpu.HBM) for a in args]
            pred, msg, west, south, north, aux, wide_in, wide_out = call(
                first_kernel,
                (*net_out, shape((24, 128), F32), shape((128, 512), BF16), shape((512, 128), BF16)),
                held + net_scratch + [pltpu.SemaphoreType.DMA((len(args),))],
                args,
                "net_first",
                pl.ANY,
            )
        else:
            pred, msg, west, south, north, factors_z = call(
                next_kernel,
                (*net_out, shape((zs, 128), F32)),
                net_scratch,
                (aux, *seam_ins, wide_in, w_down, w_mid, w_up, wide_out),
                "seams_net",
            )
        got = lax.all_to_all(msg, "y", 0, 0)
        group_out = (shape((2 * xs, 40, 128), F32), plane, row)
        if step == 0:
            msg, start, start_f, factors_y = call(
                group_kernel,
                (*group_out, shape((ys, 128), F32)),
                [],
                (aux, got, west, south, north),
                "group",
            )
        else:
            msg, start, start_f = call(
                group_kernel, group_out, [], (aux, got, factors_y, west, south, north), "group"
            )
        got = lax.all_to_all(msg, ("x", "core"), 0, 0)
        msg, *seam_ins = call(
            turn_kernel,
            (shape((zs, *message), F32), plane, plane, plane, row),
            [],
            (aux, got, start, start_f, south, north),
            "turn",
        )
        got = lax.all_to_all(msg, "z", 0, 0)
        seam_ins = (pred, got, *seam_ins)
    out = call(
        last_kernel,
        shape((16, 64, 128), BF16),
        [pltpu.VMEM((64, 16, 128), F32), pltpu.VMEM((16, 64, 128), BF16), pltpu.SemaphoreType.DMA((4,))],
        (aux, *seam_ins, factors_z),
        "seams_last",
        out_space=pl.ANY,
    )
    return out[None, None]


def solution(mesh):
    columns, rows = mesh.shape["gx"], mesh.shape["gy"]
    inner = 8 if columns % 8 == 0 else 2
    sizes = (columns // inner, inner, rows // 2, 2)
    parts = jax.sharding.Mesh(mesh.devices.reshape(sizes), ("x", "y", "z", "core"))
    gx, gy = ("x", "y"), ("z", "core")
    in_specs = (
        P(gx, gy, None, None, None),
        P(gx, gy, None),
        P(gx, gy, None),
        P(gx, gy, None),
        P(),
        P(),
        P(),
        P(),
        P(),
    )
    return jax.shard_map(
        functools.partial(per_device, sizes),
        mesh=parts,
        in_specs=in_specs,
        out_specs=P(gx, gy, None, None, None),
        check_vma=False,
    )
```

```python
import functools

import jax
import jax.numpy as jnp
from jax import lax
from jax.experimental import pallas as pl
from jax.experimental.pallas import tpu as pltpu
from jax.sharding import PartitionSpec as P

STEPS = 2
F32 = jnp.float32
BF16 = jnp.bfloat16


def silu_of_half(half):
    return half + half * jnp.tanh(half)


def silu(v):
    return silu_of_half(0.5 * v)


def iotas(rows):
    sub = lax.broadcasted_iota(jnp.int32, (rows, 128), 0)
    lane = lax.broadcasted_iota(jnp.int32, (rows, 128), 1)
    return sub, lane


def turn_lanes(x, by):
    return pltpu.roll(x, by % 128, x.ndim - 1)


def turn_rows(x, by):
    by = by % x.shape[0]
    return x if by == 0 else pltpu.roll(x, by, 0)


def swap_sy(x, lane):
    return jnp.where((lane // 32) % 2 == 0, turn_lanes(x, -32), turn_lanes(x, 32))


def edge_gain(logs):
    return sum(jnp.exp((p + 0.5) / 32.0 * logs) for p in range(24, 32)) * 0.125


def gain_at(place, logs):
    return jnp.exp(place.astype(F32) / 32.0 * logs + (0.5 / 32.0) * logs)


def widen(narrow):
    row = jnp.concatenate([narrow.astype(F32)] * 8, axis=1)
    both = jnp.concatenate([row] * 8, axis=0)
    r = lax.broadcasted_iota(jnp.int32, both.shape, 0) // 16
    c = lax.broadcasted_iota(jnp.int32, both.shape, 1) // 64
    return jnp.where(r == c, both, 0.0)


def net(state, ready, weights, first_ref, second_ref, pred_ref, outs):
    wide_in, w_down, w_mid, w_up, wide_out = weights
    msg, west_ref, south_ref, north_ref = outs
    sub, lane = iotas(16)
    by, bx = sub % 4, sub // 4
    total_x = [[None] * 4 for _ in range(4)]
    south, north = [0.0] * 4, [0.0] * 4
    aux = ready()
    log_x, occupied, col = aux.log_x, aux.occupied, aux.col
    second_ref[pl.ds(0, 256), :] = jnp.zeros((256, 128), BF16)
    second_ref[pl.ds(1280, 256), :] = jnp.zeros((256, 128), BF16)
    mids = jnp.concatenate([0.5 * w_mid[k] for k in range(7)], axis=0)
    firsts, middles, uppers = {}, {}, {}

    def lower(k, n):
        rows = pl.ds(n * k, n)
        first = silu_of_half(jnp.dot(state[rows, :], wide_in[...], preferred_element_type=F32)).astype(BF16)
        first_ref[rows, :] = 0.5 * first
        firsts[k] = first

    def down(k, n):
        pre = jnp.dot(firsts.pop(k), w_down[...], preferred_element_type=F32)
        half = pre * (0.5 * lax.rsqrt(jnp.mean(pre * pre, axis=-1, keepdims=True) + 1e-06))
        second_ref[pl.ds(256 + n * k, n), :] = silu_of_half(half).astype(BF16)

    def stencil(k, n):
        base = n * k
        second = second_ref[pl.ds(base + 256, n), :]
        parts = [second, second_ref[pl.ds(base, n), :], second_ref[pl.ds(base + 512, n), :]]
        gap = jnp.zeros((64, 128), BF16)
        gap16 = jnp.zeros((16, 128), BF16)
        left, right, below, above = [], [], [], []
        for plane in range(n // 256):
            own = second[256 * plane : 256 * plane + 256]
            left += [gap, own[:192]]
            right += [own[64:], gap]
            for qy in range(4):
                o = own[64 * qy : 64 * qy + 64]
                below += [gap16, o[:48]]
                above += [o[16:], gap16]
        parts += [jnp.concatenate(p, axis=0) for p in (left, right, below, above)]
        stacked = jnp.concatenate(parts, axis=1)
        mixed = jnp.dot(stacked, mids, preferred_element_type=F32)
        middles[k] = (second.astype(F32) + silu_of_half(mixed)).astype(BF16)

    def up(k, n):
        rows = pl.ds(n * k, n)
        upper = jnp.dot(middles.pop(k), 0.5 * w_up[...], preferred_element_type=F32) + first_ref[rows, :].astype(F32)
        uppers[k] = silu_of_half(upper).astype(BF16)

    def out(k, n):
        rows = pl.ds(n * k, n)
        update = jnp.dot(uppers.pop(k), wide_out[...], preferred_element_type=F32)
        update = update.reshape(n // 16, 16, 128) * occupied[None]
        preds = (state[rows, :].astype(F32).reshape(n // 16, 16, 128) + update).astype(BF16)
        pred_ref[rows, :] = preds.reshape(n, 128)
        for plane in range(n // 256):
            qx = n // 256 * k + plane
            pred = preds[16 * plane : 16 * plane + 16].astype(F32)
            for qy in range(4):
                for qz in range(4):
                    value = pred[4 * qy + qz]
                    total_x[qy][qz] = value if qx == 0 else total_x[qy][qz] + value
            for qz in range(4):
                s = pred[qz] + pred[4 + qz] + pred[8 + qz] + pred[12 + qz]
                s = (s + swap_sy(s, lane)) * 0.125
                south[qx] = south[qx] + jnp.where(by == qz, turn_rows(s, qz), 0.0)
                north[qx] = north[qx] + jnp.where(by == qz, turn_rows(s, qz - 3), 0.0)

    lower(0, 256)
    lower(1, 256)
    for k in range(2, 4):
        lower(k, 256)
        down(k - 2, 256)
    down(2, 256)
    down(3, 256)
    for k in range(2):
        stencil(k, 512)
    for k in range(2):
        up(k, 512)
        out(k, 512)

    west, east = [0.0] * 4, [0.0] * 4
    for qy in range(4):
        for qz in range(4):
            s = total_x[qy][qz]
            s = (s + turn_lanes(s, 64)) * 0.125
            west[qy] = west[qy] + jnp.where(bx == qz, turn_rows(s, 4 * qz), 0.0)
            east[qy] = east[qy] + jnp.where(bx == qz, turn_rows(s, 4 * qz + 4), 0.0)
    low_sx, low_sy = lane < 64, (lane // 32) % 2 == 0
    factor = jnp.where(col == 0.0, 0.0, edge_gain(log_x))
    terms = []
    for h in range(2):
        w = jnp.where(low_sx, west[h], west[2 + h])
        terms.append(jnp.where(low_sx, east[h], east[2 + h]) - factor * w)
        west_ref[h] = w
        south_ref[h] = jnp.where(low_sy, south[h], south[2 + h])
        north_ref[h] = jnp.where(low_sy, north[h], north[2 + h])
    fill(msg, terms, factor)


class Aux:
    def __init__(self, ref):
        self.log_x, self.log_y = ref[0:1, :], ref[1:2, :]
        self.col, self.x, self.y, self.row, self.z, self.core = (ref[k : k + 1, :] for k in range(2, 8))
        self.occupied = ref[8:24, :]


def has_factor(ref):
    return len(ref.shape) == 4


def halves(ref, k):
    if has_factor(ref):
        return [ref[k, pl.ds(4 * h, 4)].reshape(16, 128) for h in range(2)]
    return [ref[k, pl.ds(16 * h, 16), :] for h in range(2)]


def fill(msg, planes, factor):
    n = msg.shape[0]
    for h, value in enumerate(planes):
        if has_factor(msg):
            msg[:, pl.ds(4 * h, 4)] = jnp.broadcast_to(value.reshape(1, 4, 4, 128), (n, 4, 4, 128))
        else:
            msg[:, pl.ds(16 * h, 16), :] = jnp.broadcast_to(value[None], (n, 16, 128))
    if has_factor(msg):
        msg[:, 8] = jnp.broadcast_to(factor[None], (n, 4, 128))


def line_of(planes):
    sub, lane = iotas(16)
    value = planes[0] + planes[1]
    value = ((value + turn_lanes(value, 32)) + (turn_lanes(value, 64) + turn_lanes(value, 96))) * 0.125
    low, line = lane < 64, value
    for qz in range(4):
        line = jnp.where(low & (sub == qz), turn_rows(value, -3 * qz), line)
        line = jnp.where(~low & (sub == qz), turn_rows(value, -3 * qz - 3), line)
    return line[0:4]


def both_strips(line):
    low = iotas(4)[1] < 64
    other = turn_lanes(line, 64)
    return jnp.where(low, line, other), jnp.where(low, other, line)


def four(line):
    return jnp.concatenate([line] * 4, axis=0)


def place_y(sub, lane):
    return [8 * (sub // 4) + 2 * (2 * ((lane // 32) % 2) + h) + lane // 64 for h in range(2)]


def edge_y(aux):
    return jnp.where(aux.row == 0.0, 0.0, edge_gain(aux.log_y))


def group_kernel(aux_ref, got, *rest):
    if has_factor(got):
        west, south, north, msg, start_ref, start_f_ref, factor_ref = rest
        for k in range(got.shape[0]):
            factor_ref[k : k + 1, :] = got[k, 8, 0:1, :]
    else:
        factor_ref, west, south, north, msg, start_ref, start_f_ref = rest
    aux = Aux(aux_ref)
    zero, one = [jnp.zeros((16, 128), F32)] * 2, jnp.ones((1, 128), F32)
    before, before_f, total, total_f = zero, one, zero, one
    for k in range(got.shape[0]):
        f, t, go = factor_ref[k : k + 1, :], halves(got, k), aux.y > k
        before = [jnp.where(go, f * before[h] + t[h], before[h]) for h in range(2)]
        before_f = jnp.where(go, f * before_f, before_f)
        total = [f * total[h] + t[h] for h in range(2)]
        total_f = f * total_f
    start = [before[h] - west[h] for h in range(2)]
    factor_y = edge_y(aux)
    term_y = [north[h] - factor_y * south[h] for h in range(2)]
    line_start, line_total = line_of(start), line_of(total)
    for h in range(2):
        start_ref[h] = start[h]
    start_f_ref[...] = jnp.broadcast_to(before_f, (8, 128))
    for x in range(msg.shape[0] // 2):
        mine = aux.x == x
        tail = [
            jnp.where(mine, line_start, line_total),
            jnp.where(mine, before_f, total_f),
            factor_y,
            aux.log_x,
            factor_y,
        ]
        tail = jnp.concatenate(tail, axis=0)
        for core in range(2):
            for h in range(2):
                value = jnp.where(aux.core == core, total[h], term_y[h])
                if len(msg.shape) == 4:
                    msg[2 * x + core, pl.ds(4 * h, 4)] = value.reshape(4, 4, 128)
                else:
                    msg[2 * x + core, pl.ds(16 * h, 16), :] = value
            if len(msg.shape) == 4:
                msg[2 * x + core, 8] = tail[0:4]
            else:
                msg[2 * x + core, 32:40, :] = tail


def turn_kernel(aux_ref, got, start_ref, start_f_ref, south, north, *rest):
    if len(got.shape) == 4:
        kept, msg, drift_ref, low_ref, pair_ref, pair_f_ref = rest
        tail_of = lambda peer: jnp.concatenate([got[peer, 8], kept[peer]], axis=0)
    else:
        msg, drift_ref, low_ref, pair_ref, pair_f_ref, kept = rest
        kept[...] = got[:, 36:40, :]
        tail_of = lambda peer: got[peer, 32:40, :]
    aux = Aux(aux_ref)
    first = aux.core == 0.0
    begin = [jnp.zeros((16, 128), F32)] * 2
    lines = [jnp.zeros((4, 128), F32)] * 2
    term, mine_tails = [0.0, 0.0], [0.0, 0.0]
    for x in range(got.shape[0] // 2):
        one, two = halves(got, 2 * x), halves(got, 2 * x + 1)
        tails = tail_of(2 * x), tail_of(2 * x + 1)
        tails = [jnp.where(first, *tails), jnp.where(first, *tails[::-1])]
        go, mine = aux.x > x, aux.x == x
        own = [jnp.where(first, one[h], two[h]) for h in range(2)]
        begin = [jnp.where(go, tails[0][4:5] * begin[h] + own[h], begin[h]) for h in range(2)]
        lines = [jnp.where(go, t[4:5] * line + t[0:4], line) for t, line in zip(tails, lines)]
        term = [jnp.where(mine, jnp.where(first, two[h], one[h]), term[h]) for h in range(2)]
        mine_tails = [jnp.where(mine, t, kept) for t, kept in zip(tails, mine_tails)]
    away = aux.col == 0.0
    lines = [jnp.where(away, 0.0, t[4:5] * line + t[0:4]) for t, line in zip(mine_tails, lines)]
    factor, other_factor = (t[5:6] for t in mine_tails)
    strips = [both_strips(line) for line in lines]
    south_line = four(strips[0][0])
    term_line = four(strips[0][1] - factor * strips[0][0])
    other_line = four(strips[1][1] - other_factor * strips[1][0])
    places = place_y(*iotas(16))
    pairs = []
    for h in range(2):
        gain = gain_at(places[h], aux.log_x)
        drift_ref[h] = jnp.where(away, 0.0, start_f_ref[0:1, :] * begin[h] + start_ref[h])
        low_ref[h] = south[h] + gain * south_line
        own = north[h] - factor * south[h] + gain * term_line
        other = term[h] + gain_at(places[h], mine_tails[1][6:7]) * other_line
        pair_ref[h] = jnp.where(first, 0.0, other)
        pairs.append(jnp.where(first, other_factor * own + other, factor * other + own))
    pair_f_ref[...] = jnp.broadcast_to(jnp.where(first, 1.0, other_factor), (8, 128))
    fill(msg, pairs, factor * other_factor)


def seams(aux, pred_ref, got, factors, drift_ref, low_ref, pair_ref, pair_f_ref, put):
    sub, lane = iotas(16)
    by, bx = sub % 4, sub // 4
    sx, sy = lane // 64, (lane // 32) % 2
    before = [jnp.zeros((16, 128), F32)] * 2
    for k in range(got.shape[0]):
        f, t, go = factors(k), halves(got, k), aux.z > k
        before = [jnp.where(go, f * before[h] + t[h], before[h]) for h in range(2)]
    before = [pair_f_ref[0:1, :] * before[h] + pair_ref[h] for h in range(2)]
    drift_y = [jnp.where(aux.row == 0.0, 0.0, before[h] - low_ref[h]) for h in range(2)]
    drift_x = [drift_ref[h] for h in range(2)]
    gain_x = [gain_at(8 * bx + 2 * q + sx, aux.log_x) for q in range(4)]
    gain_y = [gain_at(8 * by + 2 * q + sy, aux.log_y) for q in range(4)]
    spread_x = [[None] * 4 for _ in range(4)]
    spread_y = [[None] * 4 for _ in range(4)]
    for q in range(4):
        d = drift_x[q % 2]
        d = jnp.where(sx == q // 2, d, turn_lanes(d, 64))
        e = drift_y[q % 2]
        e = jnp.where(sy == q // 2, e, swap_sy(e, lane))
        for qz in range(4):
            m = d
            for k in range(4):
                m = jnp.where(bx == k, turn_rows(d, 4 * (k - qz)), m)
            spread_x[q][qz] = m
            m = e
            for k in range(4):
                m = jnp.where(by == k, turn_rows(e, k - qz), m)
            spread_y[q][qz] = m
    for qx in range(4):
        for qy in range(4):
            for qz in range(4):
                q = 16 * qx + 4 * qy + qz
                value = pred_ref[pl.ds(16 * q, 16), :].astype(F32)
                value = value + gain_x[qx] * spread_x[qy][qz] + gain_y[qy] * spread_y[qx][qz]
                put(q, value)


def first_kernel(latent, occupancy, carry_x, carry_y, w_in, w_down, w_mid, w_up, w_out, *rest):
    pred_ref, msg, west, south, north, aux_ref, wide_in, wide_out = rest[:8]
    latent_v, occupancy_v, carry_x_v, carry_y_v, w_in_v, w_down_v, w_mid_v, w_up_v, w_out_v = rest[8:17]
    state, first_ref, second_ref, sems = rest[17:]
    pairs = [
        (latent, latent_v),
        (w_in, w_in_v),
        (w_down, w_down_v),
        (w_mid, w_mid_v),
        (w_up, w_up_v),
        (w_out, w_out_v),
        (occupancy, occupancy_v),
        (carry_x, carry_x_v),
        (carry_y, carry_y_v),
    ]
    copies = [pltpu.make_async_copy(src, dst, sems.at[k]) for k, (src, dst) in enumerate(pairs)]
    for copy in copies:
        copy.start()
    x, y, z, core = (lax.axis_index(name) for name in ("x", "y", "z", "core"))
    columns = lax.axis_size("y")
    copies[0].wait()
    copies[1].wait()
    wide_in[...] = (0.5 * widen(w_in_v[...])).astype(BF16)
    turned = jnp.swapaxes(latent_v[...].astype(F32), 0, 1)
    state[...] = turned.reshape(1024, 128).astype(BF16)
    for copy in copies[2:]:
        copy.wait()

    def ready():
        wide_out[...] = widen(w_out_v[...]).T.astype(BF16)
        rates = jnp.concatenate([carry_x_v[...], carry_y_v[...]], axis=0)
        rates = jnp.concatenate([rates] * 8, axis=1)
        aux_ref[0:2, :] = jnp.log(rates)
        for k, place in enumerate((x * columns + y, x, y, 2 * z + core, z, core)):
            aux_ref[2 + k : 3 + k, :] = jnp.full((1, 128), place, jnp.int32).astype(F32)
        r, c = (lax.broadcasted_iota(jnp.int32, (16, 16), k) for k in (0, 1))
        occupied = jnp.where(r == c, occupancy_v[...].astype(F32), 0.0)
        aux_ref[8:24, :] = jnp.broadcast_to(jnp.sum(occupied, axis=1, keepdims=True), (16, 128))
        return Aux(aux_ref)

    weights = (wide_in, w_down_v, w_mid_v, w_up_v, wide_out)
    net(state, ready, weights, first_ref, second_ref, pred_ref, (msg, west, south, north))


def next_kernel(aux_ref, pred, got, drift, low, pair, pair_f, wide_in, w_down, w_mid, w_up, wide_out, *rest):
    outs, (factor_ref, state, first_ref, second_ref) = rest[:5], rest[5:]
    aux = Aux(aux_ref)
    for k in range(got.shape[0]):
        factor_ref[k : k + 1, :] = got[k, 8, 0:1, :]

    def put(q, value):
        state[pl.ds(16 * q, 16), :] = value.astype(BF16)

    seams(aux, pred, got, lambda k: got[k, 8, 0:1, :], drift, low, pair, pair_f, put)
    net(state, lambda: aux, (wide_in, w_down, w_mid, w_up, wide_out), first_ref, second_ref, outs[0], outs[1:])


def last_kernel(aux_ref, pred, got, drift, low, pair, pair_f, factor_ref, out, state, turned, sems):
    copies = []

    def put(q, value):
        state[q] = value
        if q % 16 == 15:
            rows = pl.ds(q - 15, 16)
            turned[:, rows, :] = jnp.swapaxes(state[rows], 0, 1).astype(BF16)
            copies.append(pltpu.make_async_copy(turned.at[:, rows, :], out.at[:, rows, :], sems.at[q // 16]))
            copies[-1].start()

    seams(Aux(aux_ref), pred, got, lambda k: factor_ref[k : k + 1, :], drift, low, pair, pair_f, put)
    for copy in copies:
        copy.wait()


def call(kernel, out_shape, scratch, args, name, space=pltpu.VMEM, limit=24, out_space=pltpu.VMEM):
    vmem = pl.BlockSpec(memory_space=out_space)
    return pl.pallas_call(
        kernel,
        out_shape=out_shape,
        in_specs=[pl.BlockSpec(memory_space=space)] * len(args),
        out_specs=jax.tree.map(lambda _: vmem, out_shape),
        scratch_shapes=scratch,
        compiler_params=pltpu.CompilerParams(vmem_limit_bytes=limit * 1024 * 1024),
        name=name,
    )(*args)


def per_device(sizes, latent, occupancy, carry_x, carry_y, w_in, w_down, w_mid, w_up, w_out):
    xs, ys, zs, _ = sizes
    shape = jax.ShapeDtypeStruct
    plane, row = shape((2, 16, 128), F32), shape((8, 128), F32)
    net_scratch = [
        pltpu.VMEM((1024, 128), BF16),
        pltpu.VMEM((1024, 512), BF16),
        pltpu.VMEM((1536, 128), BF16),
    ]
    for step in range(STEPS):
        message = (9, 4, 128) if step == 0 else (32, 128)
        net_out = (shape((1024, 128), BF16), shape((ys, *message), F32), plane, plane, plane)
        if step == 0:
            args = (latent[0, 0], occupancy[0], carry_x[0], carry_y[0], w_in, w_down, w_mid, w_up, w_out.T)
            held = [pltpu.VMEM(a.shape, a.dtype) for a in args]
            args = [pltpu.with_memory_space_constraint(a, pltpu.HBM) for a in args]
            pred, msg, west, south, north, aux, wide_in, wide_out = call(
                first_kernel,
                (*net_out, shape((24, 128), F32), shape((128, 512), BF16), shape((512, 128), BF16)),
                held + net_scratch + [pltpu.SemaphoreType.DMA((len(args),))],
                args,
                "net_first",
                pl.ANY,
            )
        else:
            pred, msg, west, south, north, factors_z = call(
                next_kernel,
                (*net_out, shape((zs, 128), F32)),
                net_scratch,
                (aux, *seam_ins, wide_in, w_down, w_mid, w_up, wide_out),
                "seams_net",
            )
        got = lax.all_to_all(msg, "y", 0, 0)
        group_out = (shape((2 * xs, *((40, 128) if step == 0 else (9, 4, 128))), F32), plane, row)
        if step == 0:
            msg, start, start_f, factors_y = call(
                group_kernel,
                (*group_out, shape((ys, 128), F32)),
                [],
                (aux, got, west, south, north),
                "group",
            )
        else:
            msg, start, start_f = call(
                group_kernel, group_out, [], (aux, got, factors_y, west, south, north), "group"
            )
        got = lax.all_to_all(msg, ("x", "core"), 0, 0)
        turn_out = (shape((zs, *message), F32), plane, plane, plane, row)
        turn_args = (aux, got, start, start_f, south, north)
        if step == 0:
            msg, *seam_ins, kept = call(turn_kernel, (*turn_out, shape((2 * xs, 4, 128), F32)), [], turn_args, "turn")
        else:
            msg, *seam_ins = call(turn_kernel, turn_out, [], (*turn_args, kept), "turn")
        got = lax.all_to_all(msg, "z", 0, 0)
        seam_ins = (pred, got, *seam_ins)
    out = call(
        last_kernel,
        shape((16, 64, 128), BF16),
        [pltpu.VMEM((64, 16, 128), F32), pltpu.VMEM((16, 64, 128), BF16), pltpu.SemaphoreType.DMA((4,))],
        (aux, *seam_ins, factors_z),
        "seams_last",
        out_space=pl.ANY,
    )
    return out[None, None]


def solution(mesh):
    columns, rows = mesh.shape["gx"], mesh.shape["gy"]
    inner = 8 if columns % 8 == 0 else 2
    sizes = (columns // inner, inner, rows // 2, 2)
    parts = jax.sharding.Mesh(mesh.devices.reshape(sizes), ("x", "y", "z", "core"))
    gx, gy = ("x", "y"), ("z", "core")
    in_specs = (
        P(gx, gy, None, None, None),
        P(gx, gy, None),
        P(gx, gy, None),
        P(gx, gy, None),
        P(),
        P(),
        P(),
        P(),
        P(),
    )
    return jax.shard_map(
        functools.partial(per_device, sizes),
        mesh=parts,
        in_specs=in_specs,
        out_specs=P(gx, gy, None, None, None),
        check_vma=False,
    )
```

```python
import functools

import jax
import jax.numpy as jnp
from jax import lax
from jax.experimental import pallas as pl
from jax.experimental.pallas import tpu as pltpu
from jax.sharding import PartitionSpec as P

STEPS = 2
F32 = jnp.float32
BF16 = jnp.bfloat16


def silu_of_half(half):
    return half + half * jnp.tanh(half)


def silu(v):
    return silu_of_half(0.5 * v)


def iotas(rows):
    sub = lax.broadcasted_iota(jnp.int32, (rows, 128), 0)
    lane = lax.broadcasted_iota(jnp.int32, (rows, 128), 1)
    return sub, lane


def turn_lanes(x, by):
    return pltpu.roll(x, by % 128, x.ndim - 1)


def turn_rows(x, by):
    by = by % x.shape[0]
    return x if by == 0 else pltpu.roll(x, by, 0)


def swap_sy(x, lane):
    return jnp.where((lane // 32) % 2 == 0, turn_lanes(x, -32), turn_lanes(x, 32))


def edge_gain(logs):
    return sum(jnp.exp((p + 0.5) / 32.0 * logs) for p in range(24, 32)) * 0.125


def gain_at(place, logs):
    return jnp.exp(place.astype(F32) / 32.0 * logs + (0.5 / 32.0) * logs)


def widen(narrow):
    row = jnp.concatenate([narrow.astype(F32)] * 8, axis=1)
    both = jnp.concatenate([row] * 8, axis=0)
    r = lax.broadcasted_iota(jnp.int32, both.shape, 0) // 16
    c = lax.broadcasted_iota(jnp.int32, both.shape, 1) // 64
    return jnp.where(r == c, both, 0.0)


def net(state, ready, weights, first_ref, second_ref, pred_ref, outs):
    wide_in, w_down, w_mid, w_up, wide_out = weights
    msg, west_ref, south_ref, north_ref = outs
    sub, lane = iotas(16)
    by, bx = sub % 4, sub // 4
    total_x = [[None] * 4 for _ in range(4)]
    south, north = [0.0] * 4, [0.0] * 4
    aux = ready()
    log_x, occupied, col = aux.log_x, aux.occupied, aux.col
    second_ref[pl.ds(0, 256), :] = jnp.zeros((256, 128), BF16)
    second_ref[pl.ds(1280, 256), :] = jnp.zeros((256, 128), BF16)
    mids = jnp.concatenate([0.5 * w_mid[k] for k in range(7)], axis=0)
    firsts, middles, uppers = {}, {}, {}

    def lower(k, n):
        rows = pl.ds(n * k, n)
        first = silu_of_half(jnp.dot(state[rows, :], wide_in[...], preferred_element_type=F32)).astype(BF16)
        first_ref[rows, :] = 0.5 * first
        firsts[k] = first

    def down(k, n):
        pre = jnp.dot(firsts.pop(k), w_down[...], preferred_element_type=F32)
        half = pre * (0.5 * lax.rsqrt(jnp.mean(pre * pre, axis=-1, keepdims=True) + 1e-06))
        second_ref[pl.ds(256 + n * k, n), :] = silu_of_half(half).astype(BF16)

    def stencil(k, n):
        base = n * k
        second = second_ref[pl.ds(base + 256, n), :]
        parts = [second, second_ref[pl.ds(base, n), :], second_ref[pl.ds(base + 512, n), :]]
        gap = jnp.zeros((64, 128), BF16)
        gap16 = jnp.zeros((16, 128), BF16)
        left, right, below, above = [], [], [], []
        for plane in range(n // 256):
            own = second[256 * plane : 256 * plane + 256]
            left += [gap, own[:192]]
            right += [own[64:], gap]
            for qy in range(4):
                o = own[64 * qy : 64 * qy + 64]
                below += [gap16, o[:48]]
                above += [o[16:], gap16]
        parts += [jnp.concatenate(p, axis=0) for p in (left, right, below, above)]
        stacked = jnp.concatenate(parts, axis=1)
        mixed = jnp.dot(stacked, mids, preferred_element_type=F32)
        middles[k] = (second.astype(F32) + silu_of_half(mixed)).astype(BF16)

    def up(k, n):
        rows = pl.ds(n * k, n)
        upper = jnp.dot(middles.pop(k), 0.5 * w_up[...], preferred_element_type=F32) + first_ref[rows, :].astype(F32)
        uppers[k] = silu_of_half(upper).astype(BF16)

    def out(k, n):
        rows = pl.ds(n * k, n)
        update = jnp.dot(uppers.pop(k), wide_out[...], preferred_element_type=F32)
        update = update.reshape(n // 16, 16, 128) * occupied[None]
        preds = (state[rows, :].astype(F32).reshape(n // 16, 16, 128) + update).astype(BF16)
        pred_ref[rows, :] = preds.reshape(n, 128)
        for plane in range(n // 256):
            qx = n // 256 * k + plane
            pred = preds[16 * plane : 16 * plane + 16].astype(F32)
            for qy in range(4):
                for qz in range(4):
                    value = pred[4 * qy + qz]
                    total_x[qy][qz] = value if qx == 0 else total_x[qy][qz] + value
            for qz in range(4):
                s = pred[qz] + pred[4 + qz] + pred[8 + qz] + pred[12 + qz]
                s = (s + swap_sy(s, lane)) * 0.125
                south[qx] = south[qx] + jnp.where(by == qz, turn_rows(s, qz), 0.0)
                north[qx] = north[qx] + jnp.where(by == qz, turn_rows(s, qz - 3), 0.0)

    lower(0, 256)
    lower(1, 256)
    for k in range(2, 4):
        lower(k, 256)
        down(k - 2, 256)
    down(2, 256)
    down(3, 256)
    for k in range(2):
        stencil(k, 512)
    for k in range(2):
        up(k, 512)
        out(k, 512)

    west, east = [0.0] * 4, [0.0] * 4
    for qy in range(4):
        for qz in range(4):
            s = total_x[qy][qz]
            s = (s + turn_lanes(s, 64)) * 0.125
            west[qy] = west[qy] + jnp.where(bx == qz, turn_rows(s, 4 * qz), 0.0)
            east[qy] = east[qy] + jnp.where(bx == qz, turn_rows(s, 4 * qz + 4), 0.0)
    low_sx, low_sy = lane < 64, (lane // 32) % 2 == 0
    factor = jnp.where(col == 0.0, 0.0, edge_gain(log_x))
    terms = []
    for h in range(2):
        w = jnp.where(low_sx, west[h], west[2 + h])
        terms.append(jnp.where(low_sx, east[h], east[2 + h]) - factor * w)
        west_ref[h] = w
        south_ref[h] = jnp.where(low_sy, south[h], south[2 + h])
        north_ref[h] = jnp.where(low_sy, north[h], north[2 + h])
    fill(msg, terms, factor)


class Aux:
    def __init__(self, ref):
        self.log_x, self.log_y = ref[0:1, :], ref[1:2, :]
        self.col, self.x, self.y, self.row, self.z, self.core = (ref[k : k + 1, :] for k in range(2, 8))
        self.occupied = ref[8:24, :]


def has_factor(ref):
    return len(ref.shape) == 4


def halves(ref, k):
    if has_factor(ref):
        return [ref[k, pl.ds(16 * h, 16)].reshape(16, 128) for h in range(2)]
    return [ref[k, pl.ds(16 * h, 16), :] for h in range(2)]


def fill(msg, planes, factor):
    n = msg.shape[0]
    for h, value in enumerate(planes):
        if has_factor(msg):
            msg[:, pl.ds(16 * h, 16)] = jnp.broadcast_to(value.reshape(1, 16, 1, 128), (n, 16, 1, 128))
        else:
            msg[:, pl.ds(16 * h, 16), :] = jnp.broadcast_to(value[None], (n, 16, 128))
    if has_factor(msg):
        msg[:, 32] = jnp.broadcast_to(factor[None], (n, 1, 128))


def line_of(planes):
    sub, lane = iotas(16)
    value = planes[0] + planes[1]
    value = ((value + turn_lanes(value, 32)) + (turn_lanes(value, 64) + turn_lanes(value, 96))) * 0.125
    low, line = lane < 64, value
    for qz in range(4):
        line = jnp.where(low & (sub == qz), turn_rows(value, -3 * qz), line)
        line = jnp.where(~low & (sub == qz), turn_rows(value, -3 * qz - 3), line)
    return line[0:4]


def both_strips(line):
    low = iotas(4)[1] < 64
    other = turn_lanes(line, 64)
    return jnp.where(low, line, other), jnp.where(low, other, line)


def four(line):
    return jnp.concatenate([line] * 4, axis=0)


def place_y(sub, lane):
    return [8 * (sub // 4) + 2 * (2 * ((lane // 32) % 2) + h) + lane // 64 for h in range(2)]


def edge_y(aux):
    return jnp.where(aux.row == 0.0, 0.0, edge_gain(aux.log_y))


def group_kernel(aux_ref, got, *rest):
    if has_factor(got):
        west, south, north, msg, start_ref, start_f_ref, factor_ref = rest
        for k in range(got.shape[0]):
            factor_ref[k : k + 1, :] = got[k, 32, 0:1, :]
    else:
        factor_ref, west, south, north, msg, start_ref, start_f_ref = rest
    aux = Aux(aux_ref)
    zero, one = [jnp.zeros((16, 128), F32)] * 2, jnp.ones((1, 128), F32)
    before, before_f, total, total_f = zero, one, zero, one
    for k in range(got.shape[0]):
        f, t, go = factor_ref[k : k + 1, :], halves(got, k), aux.y > k
        before = [jnp.where(go, f * before[h] + t[h], before[h]) for h in range(2)]
        before_f = jnp.where(go, f * before_f, before_f)
        total = [f * total[h] + t[h] for h in range(2)]
        total_f = f * total_f
    start = [before[h] - west[h] for h in range(2)]
    factor_y = edge_y(aux)
    term_y = [north[h] - factor_y * south[h] for h in range(2)]
    line_start, line_total = line_of(start), line_of(total)
    for h in range(2):
        start_ref[h] = start[h]
    start_f_ref[...] = jnp.broadcast_to(before_f, (8, 128))
    for x in range(msg.shape[0] // 2):
        mine = aux.x == x
        tail = [
            jnp.where(mine, line_start, line_total),
            jnp.where(mine, before_f, total_f),
            factor_y,
            aux.log_x,
            factor_y,
        ]
        tail = jnp.concatenate(tail, axis=0)
        for core in range(2):
            for h in range(2):
                msg[2 * x + core, pl.ds(16 * h, 16), :] = jnp.where(aux.core == core, total[h], term_y[h])
            msg[2 * x + core, 32:40, :] = tail


def turn_kernel(aux_ref, got, start_ref, start_f_ref, south, north, msg, drift_ref, low_ref, pair_ref, pair_f_ref):
    aux = Aux(aux_ref)
    first = aux.core == 0.0
    begin = [jnp.zeros((16, 128), F32)] * 2
    lines = [jnp.zeros((4, 128), F32)] * 2
    term, mine_tails = [0.0, 0.0], [0.0, 0.0]
    for x in range(got.shape[0] // 2):
        one, two = halves(got, 2 * x), halves(got, 2 * x + 1)
        tails = got[2 * x, 32:40, :], got[2 * x + 1, 32:40, :]
        tails = [jnp.where(first, *tails), jnp.where(first, *tails[::-1])]
        go, mine = aux.x > x, aux.x == x
        own = [jnp.where(first, one[h], two[h]) for h in range(2)]
        begin = [jnp.where(go, tails[0][4:5] * begin[h] + own[h], begin[h]) for h in range(2)]
        lines = [jnp.where(go, t[4:5] * line + t[0:4], line) for t, line in zip(tails, lines)]
        term = [jnp.where(mine, jnp.where(first, two[h], one[h]), term[h]) for h in range(2)]
        mine_tails = [jnp.where(mine, t, kept) for t, kept in zip(tails, mine_tails)]
    away = aux.col == 0.0
    lines = [jnp.where(away, 0.0, t[4:5] * line + t[0:4]) for t, line in zip(mine_tails, lines)]
    factor, other_factor = (t[5:6] for t in mine_tails)
    strips = [both_strips(line) for line in lines]
    south_line = four(strips[0][0])
    term_line = four(strips[0][1] - factor * strips[0][0])
    other_line = four(strips[1][1] - other_factor * strips[1][0])
    places = place_y(*iotas(16))
    pairs = []
    for h in range(2):
        gain = gain_at(places[h], aux.log_x)
        drift_ref[h] = jnp.where(away, 0.0, start_f_ref[0:1, :] * begin[h] + start_ref[h])
        low_ref[h] = south[h] + gain * south_line
        own = north[h] - factor * south[h] + gain * term_line
        other = term[h] + gain_at(places[h], mine_tails[1][6:7]) * other_line
        pair_ref[h] = jnp.where(first, 0.0, other)
        pairs.append(jnp.where(first, other_factor * own + other, factor * other + own))
    pair_f_ref[...] = jnp.broadcast_to(jnp.where(first, 1.0, other_factor), (8, 128))
    fill(msg, pairs, factor * other_factor)


def seams(aux, pred_ref, got, factors, drift_ref, low_ref, pair_ref, pair_f_ref, put):
    sub, lane = iotas(16)
    by, bx = sub % 4, sub // 4
    sx, sy = lane // 64, (lane // 32) % 2
    before = [jnp.zeros((16, 128), F32)] * 2
    for k in range(got.shape[0]):
        f, t, go = factors(k), halves(got, k), aux.z > k
        before = [jnp.where(go, f * before[h] + t[h], before[h]) for h in range(2)]
    before = [pair_f_ref[0:1, :] * before[h] + pair_ref[h] for h in range(2)]
    drift_y = [jnp.where(aux.row == 0.0, 0.0, before[h] - low_ref[h]) for h in range(2)]
    drift_x = [drift_ref[h] for h in range(2)]
    gain_x = [gain_at(8 * bx + 2 * q + sx, aux.log_x) for q in range(4)]
    gain_y = [gain_at(8 * by + 2 * q + sy, aux.log_y) for q in range(4)]
    spread_x = [[None] * 4 for _ in range(4)]
    spread_y = [[None] * 4 for _ in range(4)]
    for q in range(4):
        d = drift_x[q % 2]
        d = jnp.where(sx == q // 2, d, turn_lanes(d, 64))
        e = drift_y[q % 2]
        e = jnp.where(sy == q // 2, e, swap_sy(e, lane))
        for qz in range(4):
            m = d
            for k in range(4):
                m = jnp.where(bx == k, turn_rows(d, 4 * (k - qz)), m)
            spread_x[q][qz] = m
            m = e
            for k in range(4):
                m = jnp.where(by == k, turn_rows(e, k - qz), m)
            spread_y[q][qz] = m
    for qx in range(4):
        for qy in range(4):
            for qz in range(4):
                q = 16 * qx + 4 * qy + qz
                value = pred_ref[pl.ds(16 * q, 16), :].astype(F32)
                value = value + gain_x[qx] * spread_x[qy][qz] + gain_y[qy] * spread_y[qx][qz]
                put(q, value)


def first_kernel(latent, occupancy, carry_x, carry_y, w_in, w_down, w_mid, w_up, w_out, *rest):
    pred_ref, msg, west, south, north, aux_ref, wide_in, wide_out = rest[:8]
    latent_v, occupancy_v, carry_x_v, carry_y_v, w_in_v, w_down_v, w_mid_v, w_up_v, w_out_v = rest[8:17]
    state, first_ref, second_ref, sems = rest[17:]
    pairs = [
        (latent, latent_v),
        (w_in, w_in_v),
        (w_down, w_down_v),
        (w_mid, w_mid_v),
        (w_up, w_up_v),
        (w_out, w_out_v),
        (occupancy, occupancy_v),
        (carry_x, carry_x_v),
        (carry_y, carry_y_v),
    ]
    copies = [pltpu.make_async_copy(src, dst, sems.at[k]) for k, (src, dst) in enumerate(pairs)]
    for copy in copies:
        copy.start()
    x, y, z, core = (lax.axis_index(name) for name in ("x", "y", "z", "core"))
    columns = lax.axis_size("y")
    copies[0].wait()
    copies[1].wait()
    wide_in[...] = (0.5 * widen(w_in_v[...])).astype(BF16)
    turned = jnp.swapaxes(latent_v[...].astype(F32), 0, 1)
    state[...] = turned.reshape(1024, 128).astype(BF16)
    for copy in copies[2:]:
        copy.wait()

    def ready():
        wide_out[...] = widen(w_out_v[...]).T.astype(BF16)
        rates = jnp.concatenate([carry_x_v[...], carry_y_v[...]], axis=0)
        rates = jnp.concatenate([rates] * 8, axis=1)
        aux_ref[0:2, :] = jnp.log(rates)
        for k, place in enumerate((x * columns + y, x, y, 2 * z + core, z, core)):
            aux_ref[2 + k : 3 + k, :] = jnp.full((1, 128), place, jnp.int32).astype(F32)
        r, c = (lax.broadcasted_iota(jnp.int32, (16, 16), k) for k in (0, 1))
        occupied = jnp.where(r == c, occupancy_v[...].astype(F32), 0.0)
        aux_ref[8:24, :] = jnp.broadcast_to(jnp.sum(occupied, axis=1, keepdims=True), (16, 128))
        return Aux(aux_ref)

    weights = (wide_in, w_down_v, w_mid_v, w_up_v, wide_out)
    net(state, ready, weights, first_ref, second_ref, pred_ref, (msg, west, south, north))


def next_kernel(aux_ref, pred, got, drift, low, pair, pair_f, wide_in, w_down, w_mid, w_up, wide_out, *rest):
    outs, (factor_ref, state, first_ref, second_ref) = rest[:5], rest[5:]
    aux = Aux(aux_ref)
    for k in range(got.shape[0]):
        factor_ref[k : k + 1, :] = got[k, 32, 0:1, :]

    def put(q, value):
        state[pl.ds(16 * q, 16), :] = value.astype(BF16)

    seams(aux, pred, got, lambda k: got[k, 32, 0:1, :], drift, low, pair, pair_f, put)
    net(state, lambda: aux, (wide_in, w_down, w_mid, w_up, wide_out), first_ref, second_ref, outs[0], outs[1:])


def last_kernel(aux_ref, pred, got, drift, low, pair, pair_f, factor_ref, out, state, turned, sems):
    copies = []

    def put(q, value):
        state[q] = value
        if q % 16 == 15:
            rows = pl.ds(q - 15, 16)
            turned[:, rows, :] = jnp.swapaxes(state[rows], 0, 1).astype(BF16)
            copies.append(pltpu.make_async_copy(turned.at[:, rows, :], out.at[:, rows, :], sems.at[q // 16]))
            copies[-1].start()

    seams(Aux(aux_ref), pred, got, lambda k: factor_ref[k : k + 1, :], drift, low, pair, pair_f, put)
    for copy in copies:
        copy.wait()


def call(kernel, out_shape, scratch, args, name, space=pltpu.VMEM, limit=24, out_space=pltpu.VMEM):
    vmem = pl.BlockSpec(memory_space=out_space)
    return pl.pallas_call(
        kernel,
        out_shape=out_shape,
        in_specs=[pl.BlockSpec(memory_space=space)] * len(args),
        out_specs=jax.tree.map(lambda _: vmem, out_shape),
        scratch_shapes=scratch,
        compiler_params=pltpu.CompilerParams(vmem_limit_bytes=limit * 1024 * 1024),
        name=name,
    )(*args)


def per_device(sizes, latent, occupancy, carry_x, carry_y, w_in, w_down, w_mid, w_up, w_out):
    xs, ys, zs, _ = sizes
    shape = jax.ShapeDtypeStruct
    plane, row = shape((2, 16, 128), F32), shape((8, 128), F32)
    net_scratch = [
        pltpu.VMEM((1024, 128), BF16),
        pltpu.VMEM((1024, 512), BF16),
        pltpu.VMEM((1536, 128), BF16),
    ]
    for step in range(STEPS):
        message = (33, 1, 128) if step == 0 else (32, 128)
        net_out = (shape((1024, 128), BF16), shape((ys, *message), F32), plane, plane, plane)
        if step == 0:
            args = (latent[0, 0], occupancy[0], carry_x[0], carry_y[0], w_in, w_down, w_mid, w_up, w_out.T)
            held = [pltpu.VMEM(a.shape, a.dtype) for a in args]
            args = [pltpu.with_memory_space_constraint(a, pltpu.HBM) for a in args]
            pred, msg, west, south, north, aux, wide_in, wide_out = call(
                first_kernel,
                (*net_out, shape((24, 128), F32), shape((128, 512), BF16), shape((512, 128), BF16)),
                held + net_scratch + [pltpu.SemaphoreType.DMA((len(args),))],
                args,
                "net_first",
                pl.ANY,
            )
        else:
            pred, msg, west, south, north, factors_z = call(
                next_kernel,
                (*net_out, shape((zs, 128), F32)),
                net_scratch,
                (aux, *seam_ins, wide_in, w_down, w_mid, w_up, wide_out),
                "seams_net",
            )
        got = lax.all_to_all(msg, "y", 0, 0)
        group_out = (shape((2 * xs, 40, 128), F32), plane, row)
        if step == 0:
            msg, start, start_f, factors_y = call(
                group_kernel,
                (*group_out, shape((ys, 128), F32)),
                [],
                (aux, got, west, south, north),
                "group",
            )
        else:
            msg, start, start_f = call(
                group_kernel, group_out, [], (aux, got, factors_y, west, south, north), "group"
            )
        got = lax.all_to_all(msg, ("x", "core"), 0, 0)
        msg, *seam_ins = call(
            turn_kernel,
            (shape((zs, *message), F32), plane, plane, plane, row),
            [],
            (aux, got, start, start_f, south, north),
            "turn",
        )
        got = lax.all_to_all(msg, "z", 0, 0)
        seam_ins = (pred, got, *seam_ins)
    out = call(
        last_kernel,
        shape((16, 64, 128), BF16),
        [pltpu.VMEM((64, 16, 128), F32), pltpu.VMEM((16, 64, 128), BF16), pltpu.SemaphoreType.DMA((4,))],
        (aux, *seam_ins, factors_z),
        "seams_last",
        out_space=pl.ANY,
    )
    return out[None, None]


def solution(mesh):
    columns, rows = mesh.shape["gx"], mesh.shape["gy"]
    inner = 8 if columns % 8 == 0 else 2
    sizes = (columns // inner, inner, rows // 2, 2)
    parts = jax.sharding.Mesh(mesh.devices.reshape(sizes), ("x", "y", "z", "core"))
    gx, gy = ("x", "y"), ("z", "core")
    in_specs = (
        P(gx, gy, None, None, None),
        P(gx, gy, None),
        P(gx, gy, None),
        P(gx, gy, None),
        P(),
        P(),
        P(),
        P(),
        P(),
    )
    return jax.shard_map(
        functools.partial(per_device, sizes),
        mesh=parts,
        in_specs=in_specs,
        out_specs=P(gx, gy, None, None, None),
        check_vma=False,
    )
```
